32 devices in a mesh: grp: 2 (over y), pre: 4 (over z), row: 4 (over x, core).
Axes of the slice: x: 2, y: 2, z: 4, core: 2. Of those that a mesh axis runs over, the one named last changes fastest.
Arguments:
- queries: bfloat16 [32, 2, 8192], P(('grp', 'row')), parts along dimension 0, may hold values from -200 to 200
- prefix_keys: bfloat16 [1024, 1024], P(('grp', 'pre')), parts along dimension 0, may hold values from -7 to 7
- prefix_values: bfloat16 [1024, 1024], P(('grp', 'pre')), parts along dimension 0, may hold values from -6 to 6
- suffix_keys: bfloat16 [32, 64, 1024], P(('grp', 'row'), 'pre'), parts along dimension 0, may hold values from -6 to 6
- suffix_values: bfloat16 [32, 64, 1024], P(('grp', 'row'), 'pre'), parts along dimension 0, may hold values from -6 to 6
- new_keys: bfloat16 [32, 2, 1024], P(('grp', 'row')), parts along dimension 0, may hold values from -6 to 6
- new_values: bfloat16 [32, 2, 1024], P(('grp', 'row')), parts along dimension 0, may hold values from -6 to 6
- hidden: bfloat16 [32, 2, 8192], P(('grp', 'pre'), None, 'row'), parts along dimension 0, may hold values from -6 to 6
- adapter_ids: int32 [32], P(('grp', 'row')), parts along dimension 0, may hold values from 0 to 127
- suffix_lengths: int32 [32], P(('grp', 'row')), parts along dimension 0, may hold values from 1 to 64
- kv_scales: bfloat16 [128, 2, 1024], replicated, may hold values from 0.25 to 1.75
- ffn_scales: bfloat16 [128, 14336], P(None, 'pre'), may hold values from 0.25 to 1.75
- out_weight: bfloat16 [8192, 8192], P('pre', 'row'), may hold values from -0.0625 to 0.0625
- norm_gain: bfloat16 [8192], P('row'), may hold values from 0.25 to 1.75
- gate_up: bfloat16 [8192, 2, 14336], P('row', None, 'pre'), may hold values from -0.0625 to 0.0625
Outputs:
- residual: bfloat16 [32, 2, 8192], P(('grp', 'pre'), None, 'row'), parts along dimension 0
- activation: bfloat16 [32, 2, 14336], P(('grp', 'row'), None, 'pre'), parts along dimension 0
The draws below stay inside these ranges and needn't reach their ends.
There are 2 independent parts, one for each index of `grp`. The reference program is written for one: setup_inputs(seed, part) draws one part's arguments, and reference() takes and returns one part's arrays. A program takes and returns all parts, laid end to end along the dimension named above; an argument that names none is the same for every part. Nothing has to cross between parts.
All inputs are finite; a program needn't handle non-finite values.
Results may differ from the reference program's by a relative error of at most 0.015.
Values may be sent and summed in bfloat16 or wider, within the bound.
No kernel may reach another device: no remote copies, remote signals or barrier semaphores. Data moves between devices by JAX's collectives and lax.ppermute only.
A program may use at most 128 MiB of HBM per device.

```python
import jax
import jax.numpy as jnp
from jax import lax

D = 8192
HEADS = 64
KV_HEADS = 8
HD = 128
FFW = 14336
ADAPTERS = 128
STEPS = 2
ROWS = 16
PREFIX = 512
SUFFIX = 64


def shared_keys(key):
    prompt = jax.random.truncated_normal(jax.random.fold_in(key, 101), -6.0, 6.0, (PREFIX, KV_HEADS * HD), jnp.float32)
    fresh = jax.random.truncated_normal(jax.random.fold_in(key, 103), -6.0, 6.0, (ROWS, STEPS, KV_HEADS * HD), jnp.float32)
    return (prompt, fresh)


def draw_prefix_keys(key, part):
    return shared_keys(key)[0].astype(jnp.bfloat16)


def draw_new_keys(key, part):
    return shared_keys(key)[1].astype(jnp.bfloat16)


def draw_queries(key, part):
    prompt, fresh = shared_keys(key)
    group_size = HEADS // KV_HEADS
    noise = jax.random.truncated_normal(jax.random.fold_in(key, 104), -6.0, 6.0, (ROWS, STEPS, D), jnp.float32)
    running = jnp.cumsum(fresh, axis=1).reshape(ROWS, STEPS, KV_HEADS, 1, HD)
    spread = jnp.broadcast_to(running, (ROWS, STEPS, KV_HEADS, group_size, HD)).reshape(ROWS, STEPS, D)
    result = noise + 0.6 * spread
    return result.astype(jnp.bfloat16)


def with_ends(values, key, low, largest):
    extent = values.shape
    index_at = [jax.random.randint(jax.random.fold_in(key, axis), (), 0, extent[axis]) for axis in range(len(extent))]
    values = values.at[tuple(index_at)].set(low)
    longest = extent.index(max(extent))
    index_at[longest] = (index_at[longest] + 1) % extent[longest]
    return values.at[tuple(index_at)].set(largest)


def block_scale(own_key, dims, split, low, largest):
    def one(axis_at, shards_of):
        steps = jax.random.uniform(jax.random.fold_in(jax.random.fold_in(own_key, 6), axis_at), (shards_of,), jnp.float32, low / len(split), largest / len(split))
        return jnp.repeat(jnp.exp(steps), dims[axis_at] // shards_of).reshape((-1,) + (1,) * (len(dims) - axis_at - 1))

    factor_of = one(*split[0])
    for cut in split[1:]:
        factor_of = factor_of * one(*cut)
    return factor_of


def normal_values(key, dims, scale, most, shards=(), kind=jnp.bfloat16):
    drawn = jax.random.normal(key, dims, jnp.float32) * scale
    if len(shards) > 0:
        drawn = block_scale(key, dims, shards, -0.22, 0.18) * drawn
    return jnp.clip(drawn, min=-most, max=most).astype(kind)


def setup_inputs(seed: int = 0, part: int = 0) -> dict:
    key_of = jax.random.split(jax.random.key(seed), 16)
    own_keys = jax.random.split(jax.random.fold_in(key_of[15], part), 16)
    return {
        "queries": draw_queries(jax.random.fold_in(jax.random.fold_in(key_of[15], part), 71), part),
        "prefix_keys": draw_prefix_keys(jax.random.fold_in(jax.random.fold_in(key_of[15], part), 71), part),
        "prefix_values": normal_values(own_keys[2], (PREFIX, KV_HEADS * HD), 1.0, 6.0, ((0, 4),)),
        "suffix_keys": normal_values(own_keys[3], (ROWS, SUFFIX, KV_HEADS * HD), 1.0, 6.0, ((0, 4), (1, 4))),
        "suffix_values": normal_values(own_keys[4], (ROWS, SUFFIX, KV_HEADS * HD), 1.0, 6.0, ((0, 4), (1, 4))),
        "new_keys": draw_new_keys(jax.random.fold_in(jax.random.fold_in(key_of[15], part), 71), part),
        "new_values": normal_values(own_keys[6], (ROWS, STEPS, KV_HEADS * HD), 1.0, 6.0, ((0, 4),)),
        "hidden": normal_values(own_keys[7], (ROWS, STEPS, D), 1.0, 6.0, ((0, 4), (2, 4))),
        "adapter_ids": with_ends(jax.random.randint(own_keys[8], (ROWS,), 0, ADAPTERS), jax.random.fold_in(own_keys[8], 1), 0, ADAPTERS - 1).astype(jnp.int32),
        "suffix_lengths": with_ends(jax.random.randint(own_keys[9], (ROWS,), 1, SUFFIX + 1), jax.random.fold_in(own_keys[9], 1), 1, SUFFIX).astype(jnp.int32),
        "kv_scales": jnp.clip(1.0 + 0.15 * jax.random.normal(key_of[10], (ADAPTERS, 2, KV_HEADS * HD), jnp.float32), 0.25, 1.75).astype(jnp.bfloat16),
        "ffn_scales": jnp.clip(1.0 + 0.15 * jax.random.normal(key_of[11], (ADAPTERS, FFW), jnp.float32), 0.25, 1.75).astype(jnp.bfloat16),
        "out_weight": normal_values(key_of[12], (D, D), D ** -0.5, 0.0625, ((0, 4), (1, 4))),
        "norm_gain": jnp.clip(1.0 + 0.15 * jax.random.normal(key_of[13], (D,), jnp.float32), 0.25, 1.75).astype(jnp.bfloat16),
        "gate_up": normal_values(key_of[14], (D, 2, FFW), D ** -0.5, 0.0625, ((0, 4), (2, 4))),
    }


masked_score = -1e+30

def settle(values):
    return lax.optimization_barrier(values.astype(jnp.bfloat16)).astype(jnp.float32)

def reference(queries, prefix_keys, prefix_values, suffix_keys, suffix_values, new_keys, new_values, hidden, adapter_ids, suffix_lengths, kv_scales, ffn_scales, out_weight, norm_gain, gate_up):
    group_size = HEADS // KV_HEADS
    score_scale = HD ** (-0.5)
    chosen = jnp.take(kv_scales, adapter_ids, axis=0).astype(jnp.float32)
    key_scale = chosen[:, 0].reshape(ROWS, KV_HEADS, HD)
    value_scale = chosen[:, 1].reshape(ROWS, KV_HEADS, HD)
    query_heads = queries.astype(jnp.float32).reshape(ROWS, STEPS, KV_HEADS, group_size, HD)
    scaled_query = settle(query_heads * key_scale[:, None, :, None, :])
    fresh_key = settle(new_keys.astype(jnp.float32).reshape(ROWS, STEPS, KV_HEADS, HD) * key_scale[:, None])
    fresh_value = settle(new_values.astype(jnp.float32).reshape(ROWS, STEPS, KV_HEADS, HD) * value_scale[:, None])
    cached_key = prefix_keys.astype(jnp.float32).reshape(PREFIX, KV_HEADS, HD)
    cached_value = prefix_values.astype(jnp.float32).reshape(PREFIX, KV_HEADS, HD)
    recent_key = suffix_keys.astype(jnp.float32).reshape(ROWS, SUFFIX, KV_HEADS, HD)
    recent_value = suffix_values.astype(jnp.float32).reshape(ROWS, SUFFIX, KV_HEADS, HD)
    prefix_scores = jnp.einsum('rskgd,tkd->rskgt', scaled_query, cached_key) * score_scale
    in_suffix = (jnp.arange(SUFFIX, dtype=jnp.int32)[None, :] < suffix_lengths[:, None])[:, None, None, None, :]
    suffix_scores = jnp.einsum('rskgd,rtkd->rskgt', query_heads, recent_key) * score_scale
    suffix_scores = jnp.where(in_suffix, suffix_scores, masked_score)
    in_order = (jnp.arange(STEPS)[None, :] <= jnp.arange(STEPS)[:, None])[None, :, None, None, :]
    new_scores = jnp.einsum('rskgd,rnkd->rskgn', query_heads, fresh_key) * score_scale
    new_scores = jnp.where(in_order, new_scores, masked_score)
    peak_score = jnp.maximum(jnp.maximum(lax.optimization_barrier(jnp.max(prefix_scores, axis=-1)), lax.optimization_barrier(jnp.max(suffix_scores, axis=-1))), lax.optimization_barrier(jnp.max(new_scores, axis=-1)))
    prefix_weight = settle(jnp.exp(prefix_scores - peak_score[..., None]))
    suffix_weight = settle(jnp.where(in_suffix, jnp.exp(suffix_scores - peak_score[..., None]), 0.0))
    new_weight = settle(jnp.where(in_order, jnp.exp(new_scores - peak_score[..., None]), 0.0))
    weight_sum = lax.optimization_barrier(jnp.sum(prefix_weight, axis=-1)) + lax.optimization_barrier(jnp.sum(suffix_weight, axis=-1)) + lax.optimization_barrier(jnp.sum(new_weight, axis=-1))
    numerator = jnp.einsum('rskgt,tkd->rskgd', prefix_weight, cached_value) * value_scale[:, None, :, None, :]
    numerator = numerator + jnp.einsum('rskgt,rtkd->rskgd', suffix_weight, recent_value)
    numerator = numerator + jnp.einsum('rskgn,rnkd->rskgd', new_weight, fresh_value)
    mixed_heads = (numerator / weight_sum[..., None]).astype(jnp.bfloat16).reshape(ROWS * STEPS, D)
    projected = jnp.dot(mixed_heads, out_weight, preferred_element_type=jnp.float32)
    residual = (hidden.astype(jnp.float32).reshape(ROWS * STEPS, D) + projected).astype(jnp.bfloat16)
    widened = residual.astype(jnp.float32)
    inverse = lax.rsqrt(lax.optimization_barrier(jnp.sum(widened * widened, axis=1, keepdims=True)) / D + 1e-05)
    normed = (widened * norm_gain.astype(jnp.float32)).astype(jnp.bfloat16)
    gate_part = jnp.dot(normed, gate_up[:, 0, :], preferred_element_type=jnp.float32) * inverse
    up_part = jnp.dot(normed, gate_up[:, 1, :], preferred_element_type=jnp.float32) * inverse
    adapter_rows = jnp.take(ffn_scales, adapter_ids, axis=0).astype(jnp.float32)
    activation = (jax.nn.silu(gate_part) * up_part).reshape(ROWS, STEPS, FFW) * adapter_rows[:, None, :]
    return (residual.reshape(ROWS, STEPS, D), activation.astype(jnp.bfloat16))
```

```python
import functools

import jax
import jax.numpy as jnp
from jax import lax
from jax.experimental import pallas as pl
from jax.experimental.pallas import tpu as pltpu
from jax.sharding import PartitionSpec as P

D = 8192
HEADS = 64
KV_HEADS = 8
HD = 128
STEPS = 2
LANES = 128

masked_score = -1e30
f32 = jnp.float32
bf16 = jnp.bfloat16
VMEM = pl.BlockSpec(memory_space=pltpu.VMEM)
SMEM = pl.BlockSpec(memory_space=pltpu.SMEM)
ANY = pl.BlockSpec(memory_space=pl.ANY)


def wrapped(index, count):
    return lax.rem(index + count, count)


def dot(left, right):
    return jnp.dot(left, right, preferred_element_type=f32)


def dot_t(left, right):
    return lax.dot_general(left, right, (((1,), (1,)), ((), ())), preferred_element_type=f32)


def pick(index, scalars):
    value = jnp.full(index.shape, scalars[0], jnp.int32)
    for at in range(1, len(scalars)):
        value = jnp.where(index == at, scalars[at], value)
    return value


def three_parts(value):
    high = value.astype(bf16).astype(f32)
    rest = value - high
    middle = rest.astype(bf16).astype(f32)
    return high, middle, rest - middle


def attend_kernel(
    pre_count,
    ids,
    lengths,
    where,
    queries,
    prefix_keys,
    prefix_values,
    suffix_keys,
    suffix_values,
    new_keys,
    new_values,
    kv_scales,
    *rest,
):
    outs, (scales, stage, sem) = rest[:pre_count], rest[pre_count:]
    rows = queries.shape[0]
    tokens = rows * STEPS
    suffix_local = suffix_keys.shape[1]
    width = suffix_keys.shape[2]
    suffix_all = rows * suffix_local
    group = HEADS // KV_HEADS
    block = HEADS * HD // pre_count
    block_heads = block // HD
    me = where[0]
    copies = [
        pltpu.make_async_copy(kv_scales.at[ids[r]], scales.at[r], sem.at[r]) for r in range(rows)
    ]
    for copy in copies:
        copy.start()

    count = group * tokens
    row_at = lax.broadcasted_iota(jnp.int32, (count, LANES), 0)
    column = lax.broadcasted_iota(jnp.int32, (count, LANES), 1)
    token = lax.rem(row_at, tokens)
    row_of = token // STEPS
    step = lax.rem(token, STEPS)
    limit = pick(row_of, [lengths[r] for r in range(rows)])
    in_suffix = (
        (column < suffix_all)
        & (column // suffix_local == row_of)
        & (me * suffix_local + lax.rem(column, suffix_local) < limit)
    )
    fresh = column - suffix_all
    in_new = (
        (fresh >= 0)
        & (fresh < tokens)
        & (fresh // STEPS == row_of)
        & (lax.rem(fresh + LANES * STEPS, STEPS) <= step)
        & (me == 0)
    )
    allowed = in_suffix | in_new

    query = queries[...].reshape(tokens, HEADS * HD).astype(f32)
    fill = jnp.zeros((LANES - suffix_all - tokens, width), f32)
    for copy in copies:
        copy.wait()
    scale = scales[...].reshape(tokens, width).astype(f32)
    odd = lax.rem(lax.broadcasted_iota(jnp.int32, scale.shape, 0), 2) == 1
    key_scale = jnp.where(odd, pltpu.roll(scale, 1, 0), scale)
    value_scale = jnp.where(odd, scale, pltpu.roll(scale, tokens - 1, 0))
    fresh_key = new_keys[...].reshape(tokens, width).astype(f32) * key_scale
    fresh_value = new_values[...].reshape(tokens, width).astype(f32) * value_scale
    own_keys = jnp.concatenate(
        [
            suffix_keys[...].reshape(suffix_all, width),
            jnp.concatenate([fresh_key, fill], axis=0).astype(bf16),
        ],
        axis=0,
    )
    own_values = jnp.concatenate(
        [
            suffix_values[...].reshape(suffix_all, width),
            jnp.concatenate([fresh_value, fill], axis=0).astype(bf16),
        ],
        axis=0,
    )
    lane = lax.broadcasted_iota(jnp.int32, (tokens, LANES), 1)
    peaks = [jnp.zeros((tokens, LANES), f32) for _ in range(pre_count)]
    sums = [jnp.zeros((tokens, LANES), f32) for _ in range(pre_count)]
    for k in range(KV_HEADS):
        span = slice(k * HD, (k + 1) * HD)
        heads = [query[:, h * HD : (h + 1) * HD] for h in range(k * group, (k + 1) * group)]
        plain = jnp.concatenate(heads, axis=0).astype(bf16)
        scaled = jnp.concatenate([head * key_scale[:, span] for head in heads], axis=0).astype(bf16)
        prefix_scores = dot_t(scaled, prefix_keys[:, span]) * (HD**-0.5)
        own_scores = jnp.where(allowed, dot_t(plain, own_keys[:, span]) * (HD**-0.5), masked_score)
        peak = jnp.max(jnp.maximum(prefix_scores, own_scores), axis=1, keepdims=True)
        prefix_weight = jnp.exp(prefix_scores - peak).astype(bf16)
        own_weight = jnp.where(allowed, jnp.exp(own_scores - peak), 0.0).astype(bf16)
        total = jnp.sum(prefix_weight.astype(f32) + own_weight.astype(f32), axis=1, keepdims=True)
        from_prefix = dot(prefix_weight, prefix_values[:, span])
        from_own = dot(own_weight, own_values[:, span])
        for g in range(group):
            h = k * group + g
            at, j = h // block_heads, h % block_heads
            part = slice(g * tokens, (g + 1) * tokens)
            value = from_prefix[part] * value_scale[:, span] + from_own[part]
            stage[at, :, j * HD : (j + 1) * HD] = value.astype(bf16)
            peaks[at] = jnp.where(lane == j, peak[part], peaks[at])
            sums[at] = jnp.where(lane == j, total[part], sums[at])
    for at in range(pre_count):
        packed = jnp.zeros((tokens, LANES), f32)
        for place, piece in enumerate(three_parts(peaks[at]) + three_parts(sums[at])):
            packed = packed + (pltpu.roll(piece, place * block_heads, 1) if place else piece)
        stage[at, :, block:] = packed.astype(bf16)
    for s in range(pre_count):
        outs[s][...] = stage[wrapped(me + s, pre_count)]


def merge_kernel(parts, *rest):
    blocks, out = rest[:parts], rest[parts]
    block = out.shape[1]
    block_heads = block // HD
    peaks, sums = [], []
    for ref in blocks:
        packed = ref[:, block:].astype(f32)
        pieces = [
            pltpu.roll(packed, LANES - place * block_heads, 1) if place else packed
            for place in range(6)
        ]
        peaks.append(pieces[0] + pieces[1] + pieces[2])
        sums.append(pieces[3] + pieces[4] + pieces[5])
    lane = lax.broadcasted_iota(jnp.int32, peaks[0].shape, 1)
    real = lane < block_heads
    highest = functools.reduce(jnp.maximum, peaks)
    factors = [jnp.where(real, jnp.exp(jnp.where(real, peak - highest, 0.0)), 0.0) for peak in peaks]
    total = sum(factor * amount for factor, amount in zip(factors, sums))
    total = jnp.where(real, total, 1.0)
    factors = [factor / total for factor in factors]
    for j in range(block_heads):
        span = slice(j * HD, (j + 1) * HD)
        value = sum(
            ref[:, span].astype(f32) * factor[:, j : j + 1] for ref, factor in zip(blocks, factors)
        )
        out[:, span] = value.astype(bf16)


def project_kernel(row_count, pre_count, where, *rest):
    blocks, weight = rest[:row_count], rest[row_count]
    outs = rest[row_count + 1 : row_count + 1 + pre_count]
    stacked, product = rest[row_count + 1 + pre_count :]
    tokens = blocks[0].shape[0]
    amount = outs[0].shape[0]
    pre_at, row_at = where[0], where[1]
    for s, ref in enumerate(blocks):
        start = pl.multiple_of(wrapped(row_at - s, row_count) * tokens, tokens)
        stacked[pl.ds(start, tokens), :] = ref[...].astype(f32)
    product[...] = dot(stacked[...].astype(bf16), weight[...])
    for s, out in enumerate(outs):
        start = pl.multiple_of(wrapped(pre_at + s, pre_count) * amount, amount)
        out[...] = product[pl.ds(start, amount), :].astype(out.dtype)


def residual_kernel(parts, hidden, *rest):
    blocks, (out, sent) = rest[:parts], rest[parts:]
    amount, width = sent.shape
    value = sum(ref[...].astype(f32) for ref in blocks)
    value = hidden[...].reshape(amount, width).astype(f32) + value
    sent[...] = value.astype(bf16)
    out[...] = value.astype(bf16).reshape(out.shape)


def feed_kernel(pre_count, row_count, where, gain, *rest):
    blocks, weight = rest[:pre_count], rest[pre_count]
    outs = rest[pre_count + 1 : pre_count + 1 + row_count]
    stacked, spread, product = rest[pre_count + 1 + row_count :]
    amount, depth = blocks[0].shape
    rows = pre_count * amount
    tokens = rows // row_count
    wide = weight.shape[2]
    pre_at, row_at = where[0], where[1]
    for s, ref in enumerate(blocks):
        start = pl.multiple_of(wrapped(pre_at - s, pre_count) * amount, amount)
        stacked[pl.ds(start, amount), :] = ref[...].astype(f32)
    value = stacked[...]
    squares = jnp.sum(value * value, axis=1, keepdims=True)
    normed = (value * gain[...].astype(f32)).astype(bf16)
    source = lax.broadcasted_iota(jnp.int32, (HD, 2 * HD), 0)
    target = lax.broadcasted_iota(jnp.int32, (HD, 2 * HD), 1)
    for b in range(depth // HD):
        piece = normed[:, b * HD : (b + 1) * HD]
        for half in range(2):
            selector = (target == 2 * source + half).astype(bf16)
            spread[half * rows : (half + 1) * rows, 2 * b * HD : 2 * (b + 1) * HD] = dot(
                piece, selector
            ).astype(bf16)
    left = spread[...]
    flat = weight.reshape(2 * depth, wide)
    tile = next(size for size in (512, 448, 256, 128) if wide % size == 0)
    for j in range(wide // tile):
        product[:, j * tile : (j + 1) * tile] = dot(left, flat[:, j * tile : (j + 1) * tile])
    lane = lax.broadcasted_iota(jnp.int32, (rows, LANES), 1)
    pieces = three_parts(squares)
    packed = sum(jnp.where(lane == place, piece, 0.0) for place, piece in enumerate(pieces))
    product[0:rows, wide:] = packed
    for s, out in enumerate(outs):
        start = pl.multiple_of(wrapped(row_at + s, row_count) * tokens, tokens)
        out[:, :wide] = product[pl.ds(start, tokens), :wide].astype(out.dtype)
        out[:, wide : 2 * wide] = product[pl.ds(rows + start, tokens), :wide].astype(out.dtype)
        out[:, 2 * wide :] = product[pl.ds(start, tokens), wide:].astype(out.dtype)


def scale_kernel(ids, table, out):
    tokens = out.shape[0]
    adapters = table.shape[0]
    row_of = lax.broadcasted_iota(jnp.int32, (tokens, adapters), 0) // STEPS
    column = lax.broadcasted_iota(jnp.int32, (tokens, adapters), 1)
    chosen = pick(row_of, [ids[r] for r in range(tokens // STEPS)])
    out[...] = dot((chosen == column).astype(bf16), table[...])


def activate_kernel(parts, scales, *rest):
    blocks, out = rest[:parts], rest[parts]
    tokens, wide = scales.shape
    squares = sum(ref[:, 2 * wide :].astype(f32) for ref in blocks)
    squares = jnp.sum(squares, axis=1, keepdims=True)
    inverse = lax.rsqrt(squares / D + 1e-05)
    gate = sum(ref[:, :wide].astype(f32) for ref in blocks) * inverse
    up = sum(ref[:, wide : 2 * wide].astype(f32) for ref in blocks) * inverse
    value = gate / (1.0 + jnp.exp(-gate)) * up * scales[...]
    out[...] = value.astype(bf16).reshape(out.shape)


def shifted(parts, axis):
    count = lax.axis_size(axis)
    return [parts[0]] + [
        lax.ppermute(parts[s], axis, [(i, (i + s) % count) for i in range(count)])
        for s in range(1, count)
    ]


def shape_of(dims, dtype=bf16):
    return jax.ShapeDtypeStruct(dims, dtype)


def params(mib):
    return pltpu.CompilerParams(vmem_limit_bytes=mib << 20)


def per_device(
    queries,
    prefix_keys,
    prefix_values,
    suffix_keys,
    suffix_values,
    new_keys,
    new_values,
    hidden,
    adapter_ids,
    suffix_lengths,
    kv_scales,
    ffn_scales,
    out_weight,
    norm_gain,
    gate_up,
):
    rows = queries.shape[0]
    tokens = rows * STEPS
    kv_width = prefix_keys.shape[1]
    pre_count = lax.axis_size("pre")
    row_count = lax.axis_size("row")
    where = jnp.stack([lax.axis_index("pre"), lax.axis_index("row")]).astype(jnp.int32)
    block = HEADS * HD // pre_count
    amount = hidden.shape[0] * STEPS
    out_cols = out_weight.shape[1]
    depth, _, wide = gate_up.shape

    ffn_rows = pl.pallas_call(
        scale_kernel,
        in_specs=[SMEM, VMEM],
        out_specs=VMEM,
        out_shape=shape_of((tokens, wide), f32),
        compiler_params=params(4),
    )(adapter_ids, ffn_scales)

    partials = pl.pallas_call(
        functools.partial(attend_kernel, pre_count),
        in_specs=[SMEM] * 3 + [VMEM] * 7 + [ANY],
        out_specs=[VMEM] * pre_count,
        out_shape=[shape_of((tokens, block + LANES))] * pre_count,
        scratch_shapes=[
            pltpu.VMEM((rows, 2, kv_width), bf16),
            pltpu.VMEM((pre_count, tokens, block + LANES), bf16),
            pltpu.SemaphoreType.DMA((rows,)),
        ],
        compiler_params=params(8),
    )(
        adapter_ids,
        suffix_lengths,
        where,
        queries,
        prefix_keys,
        prefix_values,
        suffix_keys,
        suffix_values,
        new_keys,
        new_values,
        kv_scales,
    )
    mixed = pl.pallas_call(
        functools.partial(merge_kernel, pre_count),
        in_specs=[VMEM] * pre_count,
        out_specs=VMEM,
        out_shape=shape_of((tokens, block)),
        compiler_params=params(4),
    )(*shifted(partials, "pre"))
    gathered = shifted([mixed] * row_count, "row")
    products = pl.pallas_call(
        functools.partial(project_kernel, row_count, pre_count),
        in_specs=[SMEM] + [VMEM] * (row_count + 1),
        out_specs=[VMEM] * pre_count,
        out_shape=[
            shape_of((amount, out_cols), bf16 if s else f32) for s in range(pre_count)
        ],
        scratch_shapes=[
            pltpu.VMEM((row_count * tokens, block), f32),
            pltpu.VMEM((row_count * tokens, out_cols), f32),
        ],
        compiler_params=params(12),
    )(where, *gathered, out_weight)
    residual, sent = pl.pallas_call(
        functools.partial(residual_kernel, pre_count),
        in_specs=[VMEM] * (pre_count + 1),
        out_specs=[VMEM] * 2,
        out_shape=[shape_of(hidden.shape), shape_of((amount, out_cols))],
        compiler_params=params(4),
    )(hidden, *shifted(products, "pre"))
    stacked = shifted([sent] * pre_count, "pre")
    total_rows = pre_count * amount
    fed = pl.pallas_call(
        functools.partial(feed_kernel, pre_count, row_count),
        in_specs=[SMEM] + [VMEM] * (pre_count + 2),
        out_specs=[VMEM] * row_count,
        out_shape=[
            shape_of((tokens, 2 * wide + LANES), bf16 if s else f32) for s in range(row_count)
        ],
        scratch_shapes=[
            pltpu.VMEM((total_rows, depth), f32),
            pltpu.VMEM((2 * total_rows, 2 * depth), bf16),
            pltpu.VMEM((2 * total_rows, wide + LANES), f32),
        ],
        compiler_params=params(40),
    )(where, norm_gain.reshape(1, depth), *stacked, gate_up)
    activation = pl.pallas_call(
        functools.partial(activate_kernel, row_count),
        in_specs=[VMEM] * (row_count + 1),
        out_specs=VMEM,
        out_shape=shape_of((rows, STEPS, wide)),
        compiler_params=params(4),
    )(ffn_rows, *shifted(fed, "row"))
    return (residual, activation)


def solution(mesh):
    placed = (
        P(("grp", "row"), None, None),
        P(("grp", "pre"), None),
        P(("grp", "pre"), None),
        P(("grp", "row"), "pre", None),
        P(("grp", "row"), "pre", None),
        P(("grp", "row"), None, None),
        P(("grp", "row"), None, None),
        P(("grp", "pre"), None, "row"),
        P(("grp", "row")),
        P(("grp", "row")),
        P(),
        P(None, "pre"),
        P("pre", "row"),
        P("row"),
        P("row", None, "pre"),
    )
    return jax.shard_map(
        per_device,
        mesh=mesh,
        in_specs=placed,
        out_specs=(P(("grp", "pre"), None, "row"), P(("grp", "row"), None, "pre")),
        check_vma=False,
    )
```

```python
import functools

import jax
import jax.numpy as jnp
from jax import lax
from jax.experimental import pallas as pl
from jax.experimental.pallas import tpu as pltpu
from jax.sharding import PartitionSpec as P

D = 8192
HEADS = 64
KV_HEADS = 8
HD = 128
STEPS = 2
LANES = 128

masked_score = -1e30
f32 = jnp.float32
bf16 = jnp.bfloat16
VMEM = pl.BlockSpec(memory_space=pltpu.VMEM)
SMEM = pl.BlockSpec(memory_space=pltpu.SMEM)
HBM = pl.BlockSpec(memory_space=pltpu.HBM)


def wrapped(index, count):
    return lax.rem(index + count, count)


def dot(left, right):
    return jnp.dot(left, right, preferred_element_type=f32)


def dot_t(left, right):
    return lax.dot_general(left, right, (((1,), (1,)), ((), ())), preferred_element_type=f32)


def pick(index, scalars):
    value = jnp.full(index.shape, scalars[0], jnp.int32)
    for at in range(1, len(scalars)):
        value = jnp.where(index == at, scalars[at], value)
    return value


def three_parts(value):
    high = value.astype(bf16).astype(f32)
    rest = value - high
    middle = rest.astype(bf16).astype(f32)
    return high, middle, rest - middle


def attend_kernel(
    pre_count,
    ids,
    lengths,
    where,
    queries,
    prefix_keys,
    prefix_values,
    suffix_keys,
    suffix_values,
    new_keys,
    new_values,
    kv_scales,
    *rest,
):
    outs, (scales, stage, sem) = rest[:pre_count], rest[pre_count : pre_count + 3]
    held, held_sem = rest[pre_count + 3 : -1], rest[-1]
    sources = (
        queries,
        prefix_keys,
        suffix_keys,
        new_keys,
        new_values,
        suffix_values,
        prefix_values,
    )
    loads = [
        pltpu.make_async_copy(source, target, held_sem.at[at])
        for at, (source, target) in enumerate(zip(sources, held))
    ]
    for copy in loads:
        copy.start()
    queries, prefix_keys, suffix_keys, new_keys, new_values, suffix_values, prefix_values = held
    rows = queries.shape[0]
    tokens = rows * STEPS
    suffix_local = suffix_keys.shape[1]
    width = suffix_keys.shape[2]
    suffix_all = rows * suffix_local
    group = HEADS // KV_HEADS
    block = HEADS * HD // pre_count
    block_heads = block // HD
    me = where[0]
    copies = [
        pltpu.make_async_copy(kv_scales.at[ids[r]], scales.at[r], sem.at[r]) for r in range(rows)
    ]
    for copy in copies:
        copy.start()

    count = group * tokens
    row_at = lax.broadcasted_iota(jnp.int32, (count, LANES), 0)
    column = lax.broadcasted_iota(jnp.int32, (count, LANES), 1)
    token = lax.rem(row_at, tokens)
    row_of = token // STEPS
    step = lax.rem(token, STEPS)
    limit = pick(row_of, [lengths[r] for r in range(rows)])
    in_suffix = (
        (column < suffix_all)
        & (column // suffix_local == row_of)
        & (me * suffix_local + lax.rem(column, suffix_local) < limit)
    )
    fresh = column - suffix_all
    in_new = (
        (fresh >= 0)
        & (fresh < tokens)
        & (fresh // STEPS == row_of)
        & (lax.rem(fresh + LANES * STEPS, STEPS) <= step)
        & (me == 0)
    )
    allowed = in_suffix | in_new

    for copy in loads:
        copy.wait()
    query = queries[...].reshape(tokens, HEADS * HD).astype(f32)
    fill = jnp.zeros((LANES - suffix_all - tokens, width), f32)
    for copy in copies:
        copy.wait()
    scale = scales[...].reshape(tokens, width).astype(f32)
    odd = lax.rem(lax.broadcasted_iota(jnp.int32, scale.shape, 0), 2) == 1
    key_scale = jnp.where(odd, pltpu.roll(scale, 1, 0), scale)
    value_scale = jnp.where(odd, scale, pltpu.roll(scale, tokens - 1, 0))
    fresh_key = new_keys[...].reshape(tokens, width).astype(f32) * key_scale
    fresh_value = new_values[...].reshape(tokens, width).astype(f32) * value_scale
    own_keys = jnp.concatenate(
        [
            suffix_keys[...].reshape(suffix_all, width),
            jnp.concatenate([fresh_key, fill], axis=0).astype(bf16),
        ],
        axis=0,
    )
    own_values = jnp.concatenate(
        [
            suffix_values[...].reshape(suffix_all, width),
            jnp.concatenate([fresh_value, fill], axis=0).astype(bf16),
        ],
        axis=0,
    )
    lane = lax.broadcasted_iota(jnp.int32, (tokens, LANES), 1)
    peaks = [jnp.zeros((tokens, LANES), f32) for _ in range(pre_count)]
    sums = [jnp.zeros((tokens, LANES), f32) for _ in range(pre_count)]
    for k in range(KV_HEADS):
        span = slice(k * HD, (k + 1) * HD)
        heads = [query[:, h * HD : (h + 1) * HD] for h in range(k * group, (k + 1) * group)]
        plain = jnp.concatenate(heads, axis=0).astype(bf16)
        scaled = jnp.concatenate([head * key_scale[:, span] for head in heads], axis=0).astype(bf16)
        prefix_scores = dot_t(scaled, prefix_keys[:, span]) * (HD**-0.5)
        own_scores = jnp.where(allowed, dot_t(plain, own_keys[:, span]) * (HD**-0.5), masked_score)
        peak = jnp.max(jnp.maximum(prefix_scores, own_scores), axis=1, keepdims=True)
        prefix_weight = jnp.exp(prefix_scores - peak).astype(bf16)
        own_weight = jnp.where(allowed, jnp.exp(own_scores - peak), 0.0).astype(bf16)
        total = jnp.sum(prefix_weight.astype(f32) + own_weight.astype(f32), axis=1, keepdims=True)
        from_prefix = dot(prefix_weight, prefix_values[:, span])
        from_own = dot(own_weight, own_values[:, span])
        for g in range(group):
            h = k * group + g
            at, j = h // block_heads, h % block_heads
            part = slice(g * tokens, (g + 1) * tokens)
            value = from_prefix[part] * value_scale[:, span] + from_own[part]
            stage[at, :, j * HD : (j + 1) * HD] = value.astype(bf16)
            peaks[at] = jnp.where(lane == j, peak[part], peaks[at])
            sums[at] = jnp.where(lane == j, total[part], sums[at])
    for at in range(pre_count):
        packed = jnp.zeros((tokens, LANES), f32)
        for place, piece in enumerate(three_parts(peaks[at]) + three_parts(sums[at])):
            packed = packed + (pltpu.roll(piece, place * block_heads, 1) if place else piece)
        stage[at, :, block:] = packed.astype(bf16)
    for s in range(pre_count):
        outs[s][...] = stage[wrapped(me + s, pre_count)]


def merge_kernel(parts, *rest):
    blocks, out = rest[:parts], rest[parts]
    block = out.shape[1]
    block_heads = block // HD
    peaks, sums = [], []
    for ref in blocks:
        packed = ref[:, block:].astype(f32)
        pieces = [
            pltpu.roll(packed, LANES - place * block_heads, 1) if place else packed
            for place in range(6)
        ]
        peaks.append(pieces[0] + pieces[1] + pieces[2])
        sums.append(pieces[3] + pieces[4] + pieces[5])
    lane = lax.broadcasted_iota(jnp.int32, peaks[0].shape, 1)
    real = lane < block_heads
    highest = functools.reduce(jnp.maximum, peaks)
    factors = [jnp.where(real, jnp.exp(jnp.where(real, peak - highest, 0.0)), 0.0) for peak in peaks]
    total = sum(factor * amount for factor, amount in zip(factors, sums))
    total = jnp.where(real, total, 1.0)
    factors = [factor / total for factor in factors]
    for j in range(block_heads):
        span = slice(j * HD, (j + 1) * HD)
        value = sum(
            ref[:, span].astype(f32) * factor[:, j : j + 1] for ref, factor in zip(blocks, factors)
        )
        out[:, span] = value.astype(bf16)


def project_kernel(row_count, pre_count, where, *rest):
    blocks, weight = rest[:row_count], rest[row_count]
    outs = rest[row_count + 1 : row_count + 1 + pre_count]
    stacked, product = rest[row_count + 1 + pre_count :]
    tokens = blocks[0].shape[0]
    amount = outs[0].shape[0]
    pre_at, row_at = where[0], where[1]
    for s, ref in enumerate(blocks):
        start = pl.multiple_of(wrapped(row_at - s, row_count) * tokens, tokens)
        stacked[pl.ds(start, tokens), :] = ref[...].astype(f32)
    product[...] = dot(stacked[...].astype(bf16), weight[...])
    for s, out in enumerate(outs):
        start = pl.multiple_of(wrapped(pre_at + s, pre_count) * amount, amount)
        out[...] = product[pl.ds(start, amount), :].astype(out.dtype)


def residual_kernel(parts, hidden, *rest):
    blocks, (out, sent) = rest[:parts], rest[parts:]
    amount, width = sent.shape
    value = sum(ref[...].astype(f32) for ref in blocks)
    value = hidden[...].reshape(amount, width).astype(f32) + value
    sent[...] = value.astype(bf16)
    out[...] = value.astype(bf16).reshape(out.shape)


def feed_kernel(pre_count, row_count, where, gain, *rest):
    blocks, weight = rest[:pre_count], rest[pre_count]
    outs = rest[pre_count + 1 : pre_count + 1 + row_count]
    stacked, spread, product = rest[pre_count + 1 + row_count :]
    amount, depth = blocks[0].shape
    rows = pre_count * amount
    tokens = rows // row_count
    wide = weight.shape[2]
    pre_at, row_at = where[0], where[1]
    for s, ref in enumerate(blocks):
        start = pl.multiple_of(wrapped(pre_at - s, pre_count) * amount, amount)
        stacked[pl.ds(start, amount), :] = ref[...].astype(f32)
    value = stacked[...]
    squares = jnp.sum(value * value, axis=1, keepdims=True)
    normed = (value * gain[...].astype(f32).reshape(1, depth)).astype(bf16)
    source = lax.broadcasted_iota(jnp.int32, (HD, 2 * HD), 0)
    target = lax.broadcasted_iota(jnp.int32, (HD, 2 * HD), 1)
    for b in range(depth // HD):
        piece = normed[:, b * HD : (b + 1) * HD]
        for half in range(2):
            selector = (target == 2 * source + half).astype(bf16)
            spread[half * rows : (half + 1) * rows, 2 * b * HD : 2 * (b + 1) * HD] = dot(
                piece, selector
            ).astype(bf16)
    left = spread[...]
    flat = weight.reshape(2 * depth, wide)
    tile = next(size for size in (512, 448, 256, 128) if wide % size == 0)
    for j in range(wide // tile):
        product[:, j * tile : (j + 1) * tile] = dot(left, flat[:, j * tile : (j + 1) * tile])
    lane = lax.broadcasted_iota(jnp.int32, (rows, LANES), 1)
    pieces = three_parts(squares)
    packed = sum(jnp.where(lane == place, piece, 0.0) for place, piece in enumerate(pieces))
    product[0:rows, wide:] = packed
    for s, out in enumerate(outs):
        start = pl.multiple_of(wrapped(row_at + s, row_count) * tokens, tokens)
        out[:, :wide] = product[pl.ds(start, tokens), :wide].astype(out.dtype)
        out[:, wide : 2 * wide] = product[pl.ds(rows + start, tokens), :wide].astype(out.dtype)
        out[:, 2 * wide :] = product[pl.ds(start, tokens), wide:].astype(out.dtype)


def scale_kernel(ids, table, out):
    tokens = out.shape[0]
    adapters = table.shape[0]
    row_of = lax.broadcasted_iota(jnp.int32, (tokens, adapters), 0) // STEPS
    column = lax.broadcasted_iota(jnp.int32, (tokens, adapters), 1)
    chosen = pick(row_of, [ids[r] for r in range(tokens // STEPS)])
    out[...] = dot((chosen == column).astype(bf16), table[...])


def activate_kernel(parts, scales, *rest):
    blocks, out = rest[:parts], rest[parts]
    tokens, wide = scales.shape
    squares = sum(ref[:, 2 * wide :].astype(f32) for ref in blocks)
    squares = jnp.sum(squares, axis=1, keepdims=True)
    inverse = lax.rsqrt(squares / D + 1e-05)
    gate = sum(ref[:, :wide].astype(f32) for ref in blocks) * inverse
    up = sum(ref[:, wide : 2 * wide].astype(f32) for ref in blocks) * inverse
    value = gate / (1.0 + jnp.exp(-gate)) * up * scales[...]
    out[...] = value.astype(bf16).reshape(out.shape)


def shifted(parts, axis):
    count = lax.axis_size(axis)
    return [parts[0]] + [
        lax.ppermute(parts[s], axis, [(i, (i + s) % count) for i in range(count)])
        for s in range(1, count)
    ]


def shape_of(dims, dtype=bf16):
    return jax.ShapeDtypeStruct(dims, dtype)


def params(mib):
    return pltpu.CompilerParams(vmem_limit_bytes=mib << 20)


def cost(micros):
    return pl.CostEstimate(flops=micros * 10**9, bytes_accessed=0, transcendentals=0)


def per_device(
    queries,
    prefix_keys,
    prefix_values,
    suffix_keys,
    suffix_values,
    new_keys,
    new_values,
    hidden,
    adapter_ids,
    suffix_lengths,
    kv_scales,
    ffn_scales,
    out_weight,
    norm_gain,
    gate_up,
):
    rows = queries.shape[0]
    tokens = rows * STEPS
    kv_width = prefix_keys.shape[1]
    pre_count = lax.axis_size("pre")
    row_count = lax.axis_size("row")
    where = jnp.stack([lax.axis_index("pre"), lax.axis_index("row")]).astype(jnp.int32)
    block = HEADS * HD // pre_count
    amount = hidden.shape[0] * STEPS
    out_cols = out_weight.shape[1]
    depth, _, wide = gate_up.shape

    ffn_rows = pl.pallas_call(
        scale_kernel,
        in_specs=[SMEM, VMEM],
        out_specs=VMEM,
        out_shape=shape_of((tokens, wide), f32),
        compiler_params=params(4),
    )(adapter_ids, ffn_scales)

    partials = pl.pallas_call(
        functools.partial(attend_kernel, pre_count),
        in_specs=[SMEM] * 3 + [HBM] * 8,
        out_specs=[VMEM] * pre_count,
        out_shape=[shape_of((tokens, block + LANES))] * pre_count,
        scratch_shapes=[
            pltpu.VMEM((rows, 2, kv_width), bf16),
            pltpu.VMEM((pre_count, tokens, block + LANES), bf16),
            pltpu.SemaphoreType.DMA((rows,)),
        ]
        + [
            pltpu.VMEM(source.shape, source.dtype)
            for source in (
                queries,
                prefix_keys,
                suffix_keys,
                new_keys,
                new_values,
                suffix_values,
                prefix_values,
            )
        ]
        + [pltpu.SemaphoreType.DMA((7,))],
        compiler_params=params(60),
        cost_estimate=cost(20),
    )(
        adapter_ids,
        suffix_lengths,
        where,
        queries,
        prefix_keys,
        prefix_values,
        suffix_keys,
        suffix_values,
        new_keys,
        new_values,
        kv_scales,
    )
    mixed = pl.pallas_call(
        functools.partial(merge_kernel, pre_count),
        in_specs=[VMEM] * pre_count,
        out_specs=VMEM,
        out_shape=shape_of((tokens, block)),
        compiler_params=params(4),
        cost_estimate=cost(40),
    )(*shifted(partials, "pre"))
    gathered = shifted([mixed] * row_count, "row")
    products = pl.pallas_call(
        functools.partial(project_kernel, row_count, pre_count),
        in_specs=[SMEM] + [VMEM] * (row_count + 1),
        out_specs=[VMEM] * pre_count,
        out_shape=[
            shape_of((amount, out_cols), bf16 if s else f32) for s in range(pre_count)
        ],
        scratch_shapes=[
            pltpu.VMEM((row_count * tokens, block), f32),
            pltpu.VMEM((row_count * tokens, out_cols), f32),
        ],
        compiler_params=params(8),
        cost_estimate=cost(40),
    )(where, *gathered, out_weight)
    residual, sent = pl.pallas_call(
        functools.partial(residual_kernel, pre_count),
        in_specs=[VMEM] * (pre_count + 1),
        out_specs=[VMEM] * 2,
        out_shape=[shape_of(hidden.shape), shape_of((amount, out_cols))],
        compiler_params=params(4),
        cost_estimate=cost(40),
    )(hidden, *shifted(products, "pre"))
    stacked = shifted([sent] * pre_count, "pre")
    total_rows = pre_count * amount
    fed = pl.pallas_call(
        functools.partial(feed_kernel, pre_count, row_count),
        in_specs=[SMEM] + [VMEM] * (pre_count + 2),
        out_specs=[VMEM] * row_count,
        out_shape=[
            shape_of((tokens, 2 * wide + LANES), bf16 if s else f32) for s in range(row_count)
        ],
        scratch_shapes=[
            pltpu.VMEM((total_rows, depth), f32),
            pltpu.VMEM((2 * total_rows, 2 * depth), bf16),
            pltpu.VMEM((2 * total_rows, wide + LANES), f32),
        ],
        compiler_params=params(8),
        cost_estimate=cost(16),
    )(where, norm_gain, *stacked, gate_up)
    activation = pl.pallas_call(
        functools.partial(activate_kernel, row_count),
        in_specs=[VMEM] * (row_count + 1),
        out_specs=VMEM,
        out_shape=shape_of((rows, STEPS, wide)),
        compiler_params=params(4),
    )(ffn_rows, *shifted(fed, "row"))
    return (residual, activation)


def solution(mesh):
    placed = (
        P(("grp", "row"), None, None),
        P(("grp", "pre"), None),
        P(("grp", "pre"), None),
        P(("grp", "row"), "pre", None),
        P(("grp", "row"), "pre", None),
        P(("grp", "row"), None, None),
        P(("grp", "row"), None, None),
        P(("grp", "pre"), None, "row"),
        P(("grp", "row")),
        P(("grp", "row")),
        P(),
        P(None, "pre"),
        P("pre", "row"),
        P("row"),
        P("row", None, "pre"),
    )
    return jax.shard_map(
        per_device,
        mesh=mesh,
        in_specs=placed,
        out_specs=(P(("grp", "pre"), None, "row"), P(("grp", "row"), None, "pre")),
        check_vma=False,
    )
```

```python
import functools

import jax
import jax.numpy as jnp
from jax import lax
from jax.experimental import pallas as pl
from jax.experimental.pallas import tpu as pltpu
from jax.sharding import PartitionSpec as P

D = 8192
HEADS = 64
KV_HEADS = 8
HD = 128
STEPS = 2
LANES = 128

masked_score = -1e30
f32 = jnp.float32
bf16 = jnp.bfloat16
VMEM = pl.BlockSpec(memory_space=pltpu.VMEM)
SMEM = pl.BlockSpec(memory_space=pltpu.SMEM)
HBM = pl.BlockSpec(memory_space=pltpu.HBM)


def target_of(index, step, count):
    if count & (count - 1) == 0:
        return index ^ step
    return (index + step) % count


def source_of(index, step, count):
    if count & (count - 1) == 0:
        return index ^ step
    return lax.rem(index + count - step, count)


def dot(left, right):
    return jnp.dot(left, right, preferred_element_type=f32)


def dot_t(left, right):
    return lax.dot_general(left, right, (((1,), (1,)), ((), ())), preferred_element_type=f32)


def pick(index, scalars):
    value = jnp.full(index.shape, scalars[0], jnp.int32)
    for at in range(1, len(scalars)):
        value = jnp.where(index == at, scalars[at], value)
    return value


def three_parts(value):
    high = value.astype(bf16).astype(f32)
    rest = value - high
    middle = rest.astype(bf16).astype(f32)
    return high, middle, rest - middle


def attend_kernel(
    pre_count,
    ids,
    lengths,
    queries,
    prefix_keys,
    prefix_values,
    suffix_keys,
    suffix_values,
    new_keys,
    new_values,
    kv_scales,
    *rest,
):
    outs, (scales, stage, sem) = rest[:pre_count], rest[pre_count : pre_count + 3]
    held, (id_mem, length_mem, small_sem, held_sem) = rest[pre_count + 3 : -4], rest[-4:]
    id_copy = pltpu.make_async_copy(ids, id_mem, small_sem.at[0])
    length_copy = pltpu.make_async_copy(lengths, length_mem, small_sem.at[1])
    id_copy.start()
    length_copy.start()
    sources = (
        queries,
        prefix_keys,
        suffix_keys,
        new_keys,
        new_values,
        suffix_values,
        prefix_values,
    )
    loads = [
        pltpu.make_async_copy(source, target, held_sem.at[at])
        for at, (source, target) in enumerate(zip(sources, held))
    ]
    for copy in loads:
        copy.start()
    queries, prefix_keys, suffix_keys, new_keys, new_values, suffix_values, prefix_values = held
    rows = queries.shape[0]
    tokens = rows * STEPS
    suffix_local = suffix_keys.shape[1]
    width = suffix_keys.shape[2]
    suffix_all = rows * suffix_local
    group = HEADS // KV_HEADS
    block = HEADS * HD // pre_count
    block_heads = block // HD
    me = lax.axis_index("pre")
    id_copy.wait()
    copies = [
        pltpu.make_async_copy(kv_scales.at[id_mem[r]], scales.at[r], sem.at[r])
        for r in range(rows)
    ]
    for copy in copies:
        copy.start()

    length_copy.wait()
    count = group * tokens
    row_at = lax.broadcasted_iota(jnp.int32, (count, LANES), 0)
    column = lax.broadcasted_iota(jnp.int32, (count, LANES), 1)
    token = lax.rem(row_at, tokens)
    row_of = token // STEPS
    step = lax.rem(token, STEPS)
    limit = pick(row_of, [length_mem[r] for r in range(rows)])
    in_suffix = (
        (column < suffix_all)
        & (column // suffix_local == row_of)
        & (me * suffix_local + lax.rem(column, suffix_local) < limit)
    )
    fresh = column - suffix_all
    in_new = (
        (fresh >= 0)
        & (fresh < tokens)
        & (fresh // STEPS == row_of)
        & (lax.rem(fresh + LANES * STEPS, STEPS) <= step)
        & (me == 0)
    )
    allowed = in_suffix | in_new

    for copy in loads:
        copy.wait()
    query = queries[...].reshape(tokens, HEADS * HD).astype(f32)
    fill = jnp.zeros((LANES - suffix_all - tokens, width), f32)
    for copy in copies:
        copy.wait()
    scale = scales[...].reshape(tokens, width).astype(f32)
    odd = lax.rem(lax.broadcasted_iota(jnp.int32, scale.shape, 0), 2) == 1
    key_scale = jnp.where(odd, pltpu.roll(scale, 1, 0), scale)
    value_scale = jnp.where(odd, scale, pltpu.roll(scale, tokens - 1, 0))
    fresh_key = new_keys[...].reshape(tokens, width).astype(f32) * key_scale
    fresh_value = new_values[...].reshape(tokens, width).astype(f32) * value_scale
    own_keys = jnp.concatenate(
        [
            suffix_keys[...].reshape(suffix_all, width),
            jnp.concatenate([fresh_key, fill], axis=0).astype(bf16),
        ],
        axis=0,
    )
    own_values = jnp.concatenate(
        [
            suffix_values[...].reshape(suffix_all, width),
            jnp.concatenate([fresh_value, fill], axis=0).astype(bf16),
        ],
        axis=0,
    )
    lane = lax.broadcasted_iota(jnp.int32, (tokens, LANES), 1)
    peaks = [jnp.zeros((tokens, LANES), f32) for _ in range(pre_count)]
    sums = [jnp.zeros((tokens, LANES), f32) for _ in range(pre_count)]
    for k in range(KV_HEADS):
        span = slice(k * HD, (k + 1) * HD)
        heads = [query[:, h * HD : (h + 1) * HD] for h in range(k * group, (k + 1) * group)]
        plain = jnp.concatenate(heads, axis=0).astype(bf16)
        scaled = jnp.concatenate([head * key_scale[:, span] for head in heads], axis=0).astype(bf16)
        prefix_scores = dot_t(scaled, prefix_keys[:, span]) * (HD**-0.5)
        own_scores = jnp.where(allowed, dot_t(plain, own_keys[:, span]) * (HD**-0.5), masked_score)
        peak = jnp.max(jnp.maximum(prefix_scores, own_scores), axis=1, keepdims=True)
        prefix_weight = jnp.exp(prefix_scores - peak).astype(bf16)
        own_weight = jnp.where(allowed, jnp.exp(own_scores - peak), 0.0).astype(bf16)
        total = jnp.sum(prefix_weight.astype(f32) + own_weight.astype(f32), axis=1, keepdims=True)
        from_prefix = dot(prefix_weight, prefix_values[:, span])
        from_own = dot(own_weight, own_values[:, span])
        for g in range(group):
            h = k * group + g
            at, j = h // block_heads, h % block_heads
            part = slice(g * tokens, (g + 1) * tokens)
            value = from_prefix[part] * value_scale[:, span] + from_own[part]
            stage[at, :, j * HD : (j + 1) * HD] = value.astype(bf16)
            peaks[at] = jnp.where(lane == j, peak[part], peaks[at])
            sums[at] = jnp.where(lane == j, total[part], sums[at])
    for at in range(pre_count):
        packed = jnp.zeros((tokens, LANES), f32)
        for place, piece in enumerate(three_parts(peaks[at]) + three_parts(sums[at])):
            packed = packed + (pltpu.roll(piece, place * block_heads, 1) if place else piece)
        stage[at, :, block:] = packed.astype(bf16)
    for s in range(pre_count):
        outs[s][...] = stage[target_of(me, s, pre_count)]


def merge_kernel(parts, *rest):
    blocks, out = rest[:parts], rest[parts]
    block = out.shape[1]
    block_heads = block // HD
    peaks, sums = [], []
    for ref in blocks:
        packed = ref[:, block:].astype(f32)
        pieces = [
            pltpu.roll(packed, LANES - place * block_heads, 1) if place else packed
            for place in range(6)
        ]
        peaks.append(pieces[0] + pieces[1] + pieces[2])
        sums.append(pieces[3] + pieces[4] + pieces[5])
    lane = lax.broadcasted_iota(jnp.int32, peaks[0].shape, 1)
    real = lane < block_heads
    highest = functools.reduce(jnp.maximum, peaks)
    factors = [jnp.where(real, jnp.exp(jnp.where(real, peak - highest, 0.0)), 0.0) for peak in peaks]
    total = sum(factor * amount for factor, amount in zip(factors, sums))
    total = jnp.where(real, total, 1.0)
    factors = [factor / total for factor in factors]
    for j in range(block_heads):
        span = slice(j * HD, (j + 1) * HD)
        value = sum(
            ref[:, span].astype(f32) * factor[:, j : j + 1] for ref, factor in zip(blocks, factors)
        )
        out[:, span] = value.astype(bf16)


def project_kernel(row_count, pre_count, *rest):
    blocks, weight = rest[:row_count], rest[row_count]
    outs = rest[row_count + 1 : row_count + 1 + pre_count]
    stacked, product = rest[row_count + 1 + pre_count :]
    tokens = blocks[0].shape[0]
    amount = outs[0].shape[0]
    pre_at, row_at = lax.axis_index("pre"), lax.axis_index("row")
    for s, ref in enumerate(blocks):
        start = pl.multiple_of(source_of(row_at, s, row_count) * tokens, tokens)
        stacked[pl.ds(start, tokens), :] = ref[...].astype(f32)
    product[...] = dot(stacked[...].astype(bf16), weight[...])
    for s, out in enumerate(outs):
        start = pl.multiple_of(target_of(pre_at, s, pre_count) * amount, amount)
        out[...] = product[pl.ds(start, amount), :].astype(out.dtype)


def residual_kernel(parts, hidden, *rest):
    blocks, (out, sent) = rest[:parts], rest[parts:]
    amount, width = sent.shape
    value = sum(ref[...].astype(f32) for ref in blocks)
    value = hidden[...].reshape(amount, width).astype(f32) + value
    sent[...] = value.astype(bf16)
    out[...] = value.astype(bf16).reshape(out.shape)


def feed_kernel(pre_count, row_count, gain, *rest):
    blocks, weight = rest[:pre_count], rest[pre_count]
    outs = rest[pre_count + 1 : pre_count + 1 + row_count]
    stacked, spread, product = rest[pre_count + 1 + row_count :]
    amount, depth = blocks[0].shape
    rows = pre_count * amount
    tokens = rows // row_count
    wide = weight.shape[2]
    pre_at, row_at = lax.axis_index("pre"), lax.axis_index("row")
    for s, ref in enumerate(blocks):
        start = pl.multiple_of(source_of(pre_at, s, pre_count) * amount, amount)
        stacked[pl.ds(start, amount), :] = ref[...].astype(f32)
    value = stacked[...]
    squares = jnp.sum(value * value, axis=1, keepdims=True)
    normed = (value * gain[...].astype(f32).reshape(1, depth)).astype(bf16)
    source = lax.broadcasted_iota(jnp.int32, (HD, 2 * HD), 0)
    target = lax.broadcasted_iota(jnp.int32, (HD, 2 * HD), 1)
    for b in range(depth // HD):
        piece = normed[:, b * HD : (b + 1) * HD]
        for half in range(2):
            selector = (target == 2 * source + half).astype(bf16)
            spread[half * rows : (half + 1) * rows, 2 * b * HD : 2 * (b + 1) * HD] = dot(
                piece, selector
            ).astype(bf16)
    left = spread[...]
    flat = weight.reshape(2 * depth, wide)
    tile = next(size for size in (512, 448, 256, 128) if wide % size == 0)
    for j in range(wide // tile):
        product[:, j * tile : (j + 1) * tile] = dot(left, flat[:, j * tile : (j + 1) * tile])
    lane = lax.broadcasted_iota(jnp.int32, (rows, LANES), 1)
    pieces = three_parts(squares)
    packed = sum(jnp.where(lane == place, piece, 0.0) for place, piece in enumerate(pieces))
    product[0:rows, wide:] = packed
    for s, out in enumerate(outs):
        start = pl.multiple_of(target_of(row_at, s, row_count) * tokens, tokens)
        out[:, :wide] = product[pl.ds(start, tokens), :wide].astype(out.dtype)
        out[:, wide : 2 * wide] = product[pl.ds(rows + start, tokens), :wide].astype(out.dtype)
        out[:, 2 * wide :] = product[pl.ds(start, tokens), wide:].astype(out.dtype)


def scale_kernel(ids, table, out):
    tokens = out.shape[0]
    adapters = table.shape[0]
    row_of = lax.broadcasted_iota(jnp.int32, (tokens, adapters), 0) // STEPS
    column = lax.broadcasted_iota(jnp.int32, (tokens, adapters), 1)
    chosen = pick(row_of, [ids[r] for r in range(tokens // STEPS)])
    out[...] = dot((chosen == column).astype(bf16), table[...])


def activate_kernel(parts, scales, *rest):
    blocks, out = rest[:parts], rest[parts]
    tokens, wide = scales.shape
    squares = sum(ref[:, 2 * wide :].astype(f32) for ref in blocks)
    squares = jnp.sum(squares, axis=1, keepdims=True)
    inverse = lax.rsqrt(squares / D + 1e-05)
    gate = sum(ref[:, :wide].astype(f32) for ref in blocks) * inverse
    up = sum(ref[:, wide : 2 * wide].astype(f32) for ref in blocks) * inverse
    value = gate / (1.0 + jnp.exp(-gate)) * up * scales[...]
    out[...] = value.astype(bf16).reshape(out.shape)


def shifted(parts, axis):
    count = lax.axis_size(axis)
    return [parts[0]] + [
        lax.ppermute(parts[s], axis, [(i, target_of(i, s, count)) for i in range(count)])
        for s in range(1, count)
    ]


def shape_of(dims, dtype=bf16):
    return jax.ShapeDtypeStruct(dims, dtype)


def params(mib):
    return pltpu.CompilerParams(vmem_limit_bytes=mib << 20)


def cost(micros):
    return pl.CostEstimate(flops=micros * 10**9, bytes_accessed=0, transcendentals=0)


def per_device(
    queries,
    prefix_keys,
    prefix_values,
    suffix_keys,
    suffix_values,
    new_keys,
    new_values,
    hidden,
    adapter_ids,
    suffix_lengths,
    kv_scales,
    ffn_scales,
    out_weight,
    norm_gain,
    gate_up,
):
    rows = queries.shape[0]
    tokens = rows * STEPS
    kv_width = prefix_keys.shape[1]
    pre_count = lax.axis_size("pre")
    row_count = lax.axis_size("row")
    block = HEADS * HD // pre_count
    amount = hidden.shape[0] * STEPS
    out_cols = out_weight.shape[1]
    depth, _, wide = gate_up.shape

    ffn_rows = pl.pallas_call(
        scale_kernel,
        in_specs=[SMEM, VMEM],
        out_specs=VMEM,
        out_shape=shape_of((tokens, wide), f32),
        compiler_params=params(4),
    )(adapter_ids, ffn_scales)

    partials = pl.pallas_call(
        functools.partial(attend_kernel, pre_count),
        in_specs=[HBM] * 10,
        out_specs=[VMEM] * pre_count,
        out_shape=[shape_of((tokens, block + LANES))] * pre_count,
        scratch_shapes=[
            pltpu.VMEM((rows, 2, kv_width), bf16),
            pltpu.VMEM((pre_count, tokens, block + LANES), bf16),
            pltpu.SemaphoreType.DMA((rows,)),
        ]
        + [
            pltpu.VMEM(source.shape, source.dtype)
            for source in (
                queries,
                prefix_keys,
                suffix_keys,
                new_keys,
                new_values,
                suffix_values,
                prefix_values,
            )
        ]
        + [
            pltpu.SMEM((rows,), jnp.int32),
            pltpu.SMEM((rows,), jnp.int32),
            pltpu.SemaphoreType.DMA((2,)),
            pltpu.SemaphoreType.DMA((7,)),
        ],
        compiler_params=params(60),
        cost_estimate=cost(20),
    )(
        adapter_ids,
        suffix_lengths,
        queries,
        prefix_keys,
        prefix_values,
        suffix_keys,
        suffix_values,
        new_keys,
        new_values,
        kv_scales,
    )
    mixed = pl.pallas_call(
        functools.partial(merge_kernel, pre_count),
        in_specs=[VMEM] * pre_count,
        out_specs=VMEM,
        out_shape=shape_of((tokens, block)),
        compiler_params=params(4),
        cost_estimate=cost(40),
    )(*shifted(partials, "pre"))
    gathered = shifted([mixed] * row_count, "row")
    products = pl.pallas_call(
        functools.partial(project_kernel, row_count, pre_count),
        in_specs=[VMEM] * (row_count + 1),
        out_specs=[VMEM] * pre_count,
        out_shape=[
            shape_of((amount, out_cols), bf16 if s else f32) for s in range(pre_count)
        ],
        scratch_shapes=[
            pltpu.VMEM((row_count * tokens, block), f32),
            pltpu.VMEM((row_count * tokens, out_cols), f32),
        ],
        compiler_params=params(8),
        cost_estimate=cost(40),
    )(*gathered, out_weight)
    residual, sent = pl.pallas_call(
        functools.partial(residual_kernel, pre_count),
        in_specs=[VMEM] * (pre_count + 1),
        out_specs=[VMEM] * 2,
        out_shape=[shape_of(hidden.shape), shape_of((amount, out_cols))],
        compiler_params=params(4),
        cost_estimate=cost(40),
    )(hidden, *shifted(products, "pre"))
    stacked = shifted([sent] * pre_count, "pre")
    total_rows = pre_count * amount
    fed = pl.pallas_call(
        functools.partial(feed_kernel, pre_count, row_count),
        in_specs=[VMEM] * (pre_count + 2),
        out_specs=[VMEM] * row_count,
        out_shape=[
            shape_of((tokens, 2 * wide + LANES), bf16 if s else f32) for s in range(row_count)
        ],
        scratch_shapes=[
            pltpu.VMEM((total_rows, depth), f32),
            pltpu.VMEM((2 * total_rows, 2 * depth), bf16),
            pltpu.VMEM((2 * total_rows, wide + LANES), f32),
        ],
        compiler_params=params(8),
        cost_estimate=cost(16),
    )(norm_gain, *stacked, gate_up)
    activation = pl.pallas_call(
        functools.partial(activate_kernel, row_count),
        in_specs=[VMEM] * (row_count + 1),
        out_specs=VMEM,
        out_shape=shape_of((rows, STEPS, wide)),
        compiler_params=params(4),
    )(ffn_rows, *shifted(fed, "row"))
    return (residual, activation)


def solution(mesh):
    placed = (
        P(("grp", "row"), None, None),
        P(("grp", "pre"), None),
        P(("grp", "pre"), None),
        P(("grp", "row"), "pre", None),
        P(("grp", "row"), "pre", None),
        P(("grp", "row"), None, None),
        P(("grp", "row"), None, None),
        P(("grp", "pre"), None, "row"),
        P(("grp", "row")),
        P(("grp", "row")),
        P(),
        P(None, "pre"),
        P("pre", "row"),
        P("row"),
        P("row", None, "pre"),
    )
    return jax.shard_map(
        per_device,
        mesh=mesh,
        in_specs=placed,
        out_specs=(P(("grp", "pre"), None, "row"), P(("grp", "row"), None, "pre")),
        check_vma=False,
    )
```

```python
import functools

import jax
import jax.numpy as jnp
from jax import lax
from jax.experimental import pallas as pl
from jax.experimental.pallas import tpu as pltpu
from jax.sharding import PartitionSpec as P

D = 8192
HEADS = 64
KV_HEADS = 8
HD = 128
STEPS = 2
LANES = 128

masked_score = -1e30
f32 = jnp.float32
bf16 = jnp.bfloat16
VMEM = pl.BlockSpec(memory_space=pltpu.VMEM)
SMEM = pl.BlockSpec(memory_space=pltpu.SMEM)
HBM = pl.BlockSpec(memory_space=pltpu.HBM)


def target_of(index, step, count):
    if count & (count - 1) == 0:
        return index ^ step
    return (index + step) % count


def source_of(index, step, count):
    if count & (count - 1) == 0:
        return index ^ step
    return lax.rem(index + count - step, count)


def dot(left, right):
    return jnp.dot(left, right, preferred_element_type=f32)


def dot_t(left, right):
    return lax.dot_general(left, right, (((1,), (1,)), ((), ())), preferred_element_type=f32)


def pick(index, scalars):
    value = jnp.full(index.shape, scalars[0], jnp.int32)
    for at in range(1, len(scalars)):
        value = jnp.where(index == at, scalars[at], value)
    return value


def three_parts(value):
    high = value.astype(bf16).astype(f32)
    rest = value - high
    middle = rest.astype(bf16).astype(f32)
    return high, middle, rest - middle


def attend_kernel(
    pre_count,
    ids,
    lengths,
    queries,
    prefix_keys,
    prefix_values,
    suffix_keys,
    suffix_values,
    new_keys,
    new_values,
    kv_scales,
    *rest,
):
    outs, (scales, stage, sem) = rest[:pre_count], rest[pre_count : pre_count + 3]
    held, (id_mem, length_mem, small_sem, held_sem) = rest[pre_count + 3 : -4], rest[-4:]
    id_copy = pltpu.make_async_copy(ids, id_mem, small_sem.at[0])
    length_copy = pltpu.make_async_copy(lengths, length_mem, small_sem.at[1])
    id_copy.start()
    length_copy.start()
    sources = (
        queries,
        prefix_keys,
        suffix_keys,
        new_keys,
        new_values,
        suffix_values,
        prefix_values,
    )
    loads = [
        pltpu.make_async_copy(source, target, held_sem.at[at])
        for at, (source, target) in enumerate(zip(sources, held))
    ]
    for copy in loads:
        copy.start()
    queries, prefix_keys, suffix_keys, new_keys, new_values, suffix_values, prefix_values = held
    rows = queries.shape[0]
    tokens = rows * STEPS
    suffix_local = suffix_keys.shape[1]
    width = suffix_keys.shape[2]
    suffix_all = rows * suffix_local
    group = HEADS // KV_HEADS
    block = HEADS * HD // pre_count
    block_heads = block // HD
    me = lax.axis_index("pre")
    id_copy.wait()
    copies = [
        pltpu.make_async_copy(kv_scales.at[id_mem[r]], scales.at[r], sem.at[r])
        for r in range(rows)
    ]
    for copy in copies:
        copy.start()

    length_copy.wait()
    count = group * tokens
    row_at = lax.broadcasted_iota(jnp.int32, (count, LANES), 0)
    column = lax.broadcasted_iota(jnp.int32, (count, LANES), 1)
    token = lax.rem(row_at, tokens)
    row_of = token // STEPS
    step = lax.rem(token, STEPS)
    limit = pick(row_of, [length_mem[r] for r in range(rows)])
    in_suffix = (
        (column < suffix_all)
        & (column // suffix_local == row_of)
        & (me * suffix_local + lax.rem(column, suffix_local) < limit)
    )
    fresh = column - suffix_all
    in_new = (
        (fresh >= 0)
        & (fresh < tokens)
        & (fresh // STEPS == row_of)
        & (lax.rem(fresh + LANES * STEPS, STEPS) <= step)
        & (me == 0)
    )
    allowed = in_suffix | in_new

    for copy in loads:
        copy.wait()
    query = queries[...].reshape(tokens, HEADS * HD).astype(f32)
    fill = jnp.zeros((LANES - suffix_all - tokens, width), f32)
    for copy in copies:
        copy.wait()
    scale = scales[...].reshape(tokens, width).astype(f32)
    odd = lax.rem(lax.broadcasted_iota(jnp.int32, scale.shape, 0), 2) == 1
    key_scale = jnp.where(odd, pltpu.roll(scale, 1, 0), scale)
    value_scale = jnp.where(odd, scale, pltpu.roll(scale, tokens - 1, 0))
    fresh_key = new_keys[...].reshape(tokens, width).astype(f32) * key_scale
    fresh_value = new_values[...].reshape(tokens, width).astype(f32) * value_scale
    own_keys = jnp.concatenate(
        [
            suffix_keys[...].reshape(suffix_all, width),
            jnp.concatenate([fresh_key, fill], axis=0).astype(bf16),
        ],
        axis=0,
    )
    own_values = jnp.concatenate(
        [
            suffix_values[...].reshape(suffix_all, width),
            jnp.concatenate([fresh_value, fill], axis=0).astype(bf16),
        ],
        axis=0,
    )
    lane = lax.broadcasted_iota(jnp.int32, (tokens, LANES), 1)
    peaks = [jnp.zeros((tokens, LANES), f32) for _ in range(pre_count)]
    sums = [jnp.zeros((tokens, LANES), f32) for _ in range(pre_count)]
    for k in range(KV_HEADS):
        span = slice(k * HD, (k + 1) * HD)
        heads = [query[:, h * HD : (h + 1) * HD] for h in range(k * group, (k + 1) * group)]
        plain = jnp.concatenate(heads, axis=0).astype(bf16)
        scaled = jnp.concatenate([head * key_scale[:, span] for head in heads], axis=0).astype(bf16)
        prefix_scores = dot_t(scaled, prefix_keys[:, span]) * (HD**-0.5)
        own_scores = jnp.where(allowed, dot_t(plain, own_keys[:, span]) * (HD**-0.5), masked_score)
        peak = jnp.max(jnp.maximum(prefix_scores, own_scores), axis=1, keepdims=True)
        prefix_weight = jnp.exp(prefix_scores - peak).astype(bf16)
        own_weight = jnp.where(allowed, jnp.exp(own_scores - peak), 0.0).astype(bf16)
        total = jnp.sum(prefix_weight.astype(f32) + own_weight.astype(f32), axis=1, keepdims=True)
        from_prefix = dot(prefix_weight, prefix_values[:, span])
        from_own = dot(own_weight, own_values[:, span])
        for g in range(group):
            h = k * group + g
            at, j = h // block_heads, h % block_heads
            part = slice(g * tokens, (g + 1) * tokens)
            value = from_prefix[part] * value_scale[:, span] + from_own[part]
            stage[at, :, j * HD : (j + 1) * HD] = value.astype(bf16)
            peaks[at] = jnp.where(lane == j, peak[part], peaks[at])
            sums[at] = jnp.where(lane == j, total[part], sums[at])
    for at in range(pre_count):
        packed = jnp.zeros((tokens, LANES), f32)
        for place, piece in enumerate(three_parts(peaks[at]) + three_parts(sums[at])):
            packed = packed + (pltpu.roll(piece, place * block_heads, 1) if place else piece)
        stage[at, :, block:] = packed.astype(bf16)
    for s in range(pre_count):
        outs[s][...] = stage[target_of(me, s, pre_count)]


def merge_kernel(parts, *rest):
    blocks, out = rest[:parts], rest[parts]
    block = out.shape[1]
    block_heads = block // HD
    peaks, sums = [], []
    for ref in blocks:
        packed = ref[:, block:].astype(f32)
        pieces = [
            pltpu.roll(packed, LANES - place * block_heads, 1) if place else packed
            for place in range(6)
        ]
        peaks.append(pieces[0] + pieces[1] + pieces[2])
        sums.append(pieces[3] + pieces[4] + pieces[5])
    lane = lax.broadcasted_iota(jnp.int32, peaks[0].shape, 1)
    real = lane < block_heads
    highest = functools.reduce(jnp.maximum, peaks)
    factors = [jnp.where(real, jnp.exp(jnp.where(real, peak - highest, 0.0)), 0.0) for peak in peaks]
    total = sum(factor * amount for factor, amount in zip(factors, sums))
    total = jnp.where(real, total, 1.0)
    factors = [factor / total for factor in factors]
    for j in range(block_heads):
        span = slice(j * HD, (j + 1) * HD)
        value = sum(
            ref[:, span].astype(f32) * factor[:, j : j + 1] for ref, factor in zip(blocks, factors)
        )
        out[:, span] = value.astype(bf16)


def project_kernel(row_count, pre_count, *rest):
    blocks, weight = rest[:row_count], rest[row_count]
    outs = rest[row_count + 1 : row_count + 1 + pre_count]
    stacked, product = rest[row_count + 1 + pre_count :]
    tokens = blocks[0].shape[0]
    amount = outs[0].shape[0]
    pre_at, row_at = lax.axis_index("pre"), lax.axis_index("row")
    for s, ref in enumerate(blocks):
        start = pl.multiple_of(source_of(row_at, s, row_count) * tokens, tokens)
        stacked[pl.ds(start, tokens), :] = ref[...].astype(f32)
    product[...] = dot(stacked[...].astype(bf16), weight[...])
    for s, out in enumerate(outs):
        start = pl.multiple_of(target_of(pre_at, s, pre_count) * amount, amount)
        out[...] = product[pl.ds(start, amount), :].astype(out.dtype)


def residual_kernel(parts, hidden, *rest):
    blocks, (out, sent) = rest[:parts], rest[parts:]
    amount, width = sent.shape
    value = sum(ref[...].astype(f32) for ref in blocks)
    value = hidden[...].reshape(amount, width).astype(f32) + value
    sent[...] = value.astype(bf16)
    out[...] = value.astype(bf16).reshape(out.shape)


def column_tile(columns):
    return next(size for size in (512, 256, 128) if columns % size == 0)


def split_columns(wide):
    unit = 512 if wide >= 1024 else LANES
    first = -(-(wide // 2) // unit) * unit
    return first, wide - first


def hand_out(row_count, product, columns, extra, keep, sent):
    rows = product.shape[0] // 2
    tokens = keep.shape[1]
    row_at = lax.axis_index("row")
    for j in range(row_count // 2):
        for at, out in ((row_at ^ (2 * j), keep), (row_at ^ (2 * j + 1), sent)):
            start = pl.multiple_of(at * tokens, tokens)
            own = pl.ds(start, tokens)
            out[j, :, :columns] = product[own, :columns].astype(out.dtype)
            out[j, :, columns : 2 * columns] = product[
                pl.ds(rows + start, tokens), :columns
            ].astype(out.dtype)
            if extra:
                out[j, :, 2 * columns :] = product[own, columns:].astype(out.dtype)


def multiply(left, weight, first, columns, product):
    depth, _, wide = weight.shape
    flat = weight.reshape(2 * depth, wide)
    tile = column_tile(columns)
    for start in range(0, columns, tile):
        product[:, start : start + tile] = dot(
            left, flat[:, first + start : first + start + tile]
        )


def placed_parts(value):
    lane = lax.broadcasted_iota(jnp.int32, (value.shape[0], LANES), 1)
    pieces = three_parts(value)
    return sum(jnp.where(lane == place, piece, 0.0) for place, piece in enumerate(pieces))


def feed_first_kernel(pre_count, row_count, columns, gain, *rest):
    blocks, weight = rest[:pre_count], rest[pre_count]
    keep, sent, spread, stacked, product = rest[pre_count + 1 :]
    amount, depth = blocks[0].shape
    rows = pre_count * amount
    pre_at = lax.axis_index("pre")
    for s, ref in enumerate(blocks):
        start = pl.multiple_of(source_of(pre_at, s, pre_count) * amount, amount)
        stacked[pl.ds(start, amount), :] = ref[...].astype(f32)
    value = stacked[...]
    squares = jnp.sum(value * value, axis=1, keepdims=True)
    normed = (value * gain[...].astype(f32).reshape(1, depth)).astype(bf16)
    source = lax.broadcasted_iota(jnp.int32, (HD, 2 * HD), 0)
    target = lax.broadcasted_iota(jnp.int32, (HD, 2 * HD), 1)
    for b in range(depth // HD):
        piece = normed[:, b * HD : (b + 1) * HD]
        for half in range(2):
            selector = (target == 2 * source + half).astype(bf16)
            spread[half * rows : (half + 1) * rows, 2 * b * HD : 2 * (b + 1) * HD] = dot(
                piece, selector
            ).astype(bf16)
    multiply(spread[...], weight, 0, columns, product)
    product[0:rows, columns:] = placed_parts(squares)
    hand_out(row_count, product, columns, True, keep, sent)


def feed_second_kernel(row_count, first, columns, spread, weight, keep, sent, product):
    multiply(spread[...], weight, first, columns, product)
    hand_out(row_count, product, columns, False, keep, sent)


def pair_kernel(extra, keep, received, *outs):
    for j, out in enumerate(outs):
        value = keep[j] + received[j].astype(f32)
        if extra:
            edge = value.shape[1] - LANES
            out[:, :edge] = value[:, :edge].astype(out.dtype)
            total = jnp.sum(value[:, edge:], axis=1, keepdims=True)
            out[:, edge:] = placed_parts(total).astype(out.dtype)
        else:
            out[...] = value.astype(out.dtype)


def scale_kernel(ids, table, out):
    tokens = out.shape[0]
    adapters = table.shape[0]
    row_of = lax.broadcasted_iota(jnp.int32, (tokens, adapters), 0) // STEPS
    column = lax.broadcasted_iota(jnp.int32, (tokens, adapters), 1)
    chosen = pick(row_of, [ids[r] for r in range(tokens // STEPS)])
    out[...] = dot((chosen == column).astype(bf16), table[...])


def activate_kernel(parts, first, scales, *rest):
    front, back, out = rest[:parts], rest[parts : 2 * parts], rest[2 * parts]
    wide = scales.shape[1]
    squares = sum(ref[:, 2 * first :].astype(f32) for ref in front)
    squares = jnp.sum(squares, axis=1, keepdims=True)
    inverse = lax.rsqrt(squares / D + 1e-05)
    for blocks, start, columns in ((front, 0, first), (back, first, wide - first)):
        gate = sum(ref[:, :columns].astype(f32) for ref in blocks) * inverse
        up = sum(ref[:, columns : 2 * columns].astype(f32) for ref in blocks) * inverse
        value = gate / (1.0 + jnp.exp(-gate)) * up * scales[:, start : start + columns]
        rows, steps, _ = out.shape
        out[:, :, start : start + columns] = value.astype(bf16).reshape(rows, steps, columns)


def shifted(parts, axis):
    count = lax.axis_size(axis)
    return [parts[0]] + [
        lax.ppermute(parts[s], axis, [(i, target_of(i, s, count)) for i in range(count)])
        for s in range(1, count)
    ]


def shape_of(dims, dtype=bf16):
    return jax.ShapeDtypeStruct(dims, dtype)


def params(mib):
    return pltpu.CompilerParams(vmem_limit_bytes=mib << 20)


def cost(micros):
    return pl.CostEstimate(flops=micros * 10**9, bytes_accessed=0, transcendentals=0)


def per_device(
    queries,
    prefix_keys,
    prefix_values,
    suffix_keys,
    suffix_values,
    new_keys,
    new_values,
    hidden,
    adapter_ids,
    suffix_lengths,
    kv_scales,
    ffn_scales,
    out_weight,
    norm_gain,
    gate_up,
):
    rows = queries.shape[0]
    tokens = rows * STEPS
    kv_width = prefix_keys.shape[1]
    pre_count = lax.axis_size("pre")
    row_count = lax.axis_size("row")
    block = HEADS * HD // pre_count
    amount = hidden.shape[0] * STEPS
    out_cols = out_weight.shape[1]
    depth, _, wide = gate_up.shape

    ffn_rows = pl.pallas_call(
        scale_kernel,
        in_specs=[SMEM, VMEM],
        out_specs=VMEM,
        out_shape=shape_of((tokens, wide), f32),
        compiler_params=params(4),
    )(adapter_ids, ffn_scales)

    partials = pl.pallas_call(
        functools.partial(attend_kernel, pre_count),
        in_specs=[HBM] * 10,
        out_specs=[VMEM] * pre_count,
        out_shape=[shape_of((tokens, block + LANES))] * pre_count,
        scratch_shapes=[
            pltpu.VMEM((rows, 2, kv_width), bf16),
            pltpu.VMEM((pre_count, tokens, block + LANES), bf16),
            pltpu.SemaphoreType.DMA((rows,)),
        ]
        + [
            pltpu.VMEM(source.shape, source.dtype)
            for source in (
                queries,
                prefix_keys,
                suffix_keys,
                new_keys,
                new_values,
                suffix_values,
                prefix_values,
            )
        ]
        + [
            pltpu.SMEM((rows,), jnp.int32),
            pltpu.SMEM((rows,), jnp.int32),
            pltpu.SemaphoreType.DMA((2,)),
            pltpu.SemaphoreType.DMA((7,)),
        ],
        compiler_params=params(60),
        cost_estimate=cost(20),
    )(
        adapter_ids,
        suffix_lengths,
        queries,
        prefix_keys,
        prefix_values,
        suffix_keys,
        suffix_values,
        new_keys,
        new_values,
        kv_scales,
    )
    mixed = pl.pallas_call(
        functools.partial(merge_kernel, pre_count),
        in_specs=[VMEM] * pre_count,
        out_specs=VMEM,
        out_shape=shape_of((tokens, block)),
        compiler_params=params(4),
        cost_estimate=cost(40),
    )(*shifted(partials, "pre"))
    gathered = shifted([mixed] * row_count, "row")
    products = pl.pallas_call(
        functools.partial(project_kernel, row_count, pre_count),
        in_specs=[VMEM] * (row_count + 1),
        out_specs=[VMEM] * pre_count,
        out_shape=[
            shape_of((amount, out_cols), bf16 if s else f32) for s in range(pre_count)
        ],
        scratch_shapes=[
            pltpu.VMEM((row_count * tokens, block), f32),
            pltpu.VMEM((row_count * tokens, out_cols), f32),
        ],
        compiler_params=params(8),
        cost_estimate=cost(40),
    )(*gathered, out_weight)
    residual, sent = pl.pallas_call(
        functools.partial(residual_kernel, pre_count),
        in_specs=[VMEM] * (pre_count + 1),
        out_specs=[VMEM] * 2,
        out_shape=[shape_of(hidden.shape), shape_of((amount, out_cols))],
        compiler_params=params(4),
        cost_estimate=cost(40),
    )(hidden, *shifted(products, "pre"))
    stacked = shifted([sent] * pre_count, "pre")
    total_rows = pre_count * amount
    half = row_count // 2
    first, second = split_columns(wide)
    sizes = (2 * first + LANES, 2 * second)
    *front, spread = pl.pallas_call(
        functools.partial(feed_first_kernel, pre_count, row_count, first),
        in_specs=[VMEM] * (pre_count + 2),
        out_specs=[VMEM] * 3,
        out_shape=[
            shape_of((half, tokens, sizes[0]), f32),
            shape_of((half, tokens, sizes[0])),
            shape_of((2 * total_rows, 2 * depth)),
        ],
        scratch_shapes=[
            pltpu.VMEM((total_rows, depth), f32),
            pltpu.VMEM((2 * total_rows, first + LANES), f32),
        ],
        compiler_params=params(8),
        cost_estimate=cost(16),
    )(norm_gain, *stacked, gate_up)
    back = pl.pallas_call(
        functools.partial(feed_second_kernel, row_count, first, second),
        in_specs=[VMEM] * 2,
        out_specs=[VMEM] * 2,
        out_shape=[
            shape_of((half, tokens, sizes[1]), f32),
            shape_of((half, tokens, sizes[1])),
        ],
        scratch_shapes=[pltpu.VMEM((2 * total_rows, second), f32)],
        compiler_params=pltpu.CompilerParams(
            vmem_limit_bytes=(8 << 20) + 2 * depth * (total_rows + 1)
        ),
        cost_estimate=cost(16),
    )(spread, gate_up)
    finals = []
    for extra, size, (keep, sent) in ((True, sizes[0], front), (False, sizes[1], back)):
        received = lax.ppermute(sent, "row", [(i, i ^ 1) for i in range(row_count)])
        sums = pl.pallas_call(
            functools.partial(pair_kernel, extra),
            in_specs=[VMEM] * 2,
            out_specs=[VMEM] * half,
            out_shape=[shape_of((tokens, size), bf16 if j else f32) for j in range(half)],
            compiler_params=params(4),
        )(keep, received)
        finals.append(sums[0])
        finals += [
            lax.ppermute(sums[j], "row", [(i, i ^ (2 * j)) for i in range(row_count)])
            for j in range(1, half)
        ]
    activation = pl.pallas_call(
        functools.partial(activate_kernel, half, first),
        in_specs=[VMEM] * (2 * half + 1),
        out_specs=VMEM,
        out_shape=shape_of((rows, STEPS, wide)),
        compiler_params=params(4),
    )(ffn_rows, *finals)
    return (residual, activation)


def solution(mesh):
    placed = (
        P(("grp", "row"), None, None),
        P(("grp", "pre"), None),
        P(("grp", "pre"), None),
        P(("grp", "row"), "pre", None),
        P(("grp", "row"), "pre", None),
        P(("grp", "row"), None, None),
        P(("grp", "row"), None, None),
        P(("grp", "pre"), None, "row"),
        P(("grp", "row")),
        P(("grp", "row")),
        P(),
        P(None, "pre"),
        P("pre", "row"),
        P("row"),
        P("row", None, "pre"),
    )
    return jax.shard_map(
        per_device,
        mesh=mesh,
        in_specs=placed,
        out_specs=(P(("grp", "pre"), None, "row"), P(("grp", "row"), None, "pre")),
        check_vma=False,
    )
```

```python
import functools

import jax
import jax.numpy as jnp
from jax import lax
from jax.experimental import pallas as pl
from jax.experimental.pallas import tpu as pltpu
from jax.sharding import PartitionSpec as P

D = 8192
HEADS = 64
KV_HEADS = 8
HD = 128
STEPS = 2
LANES = 128

masked_score = -1e30
f32 = jnp.float32
bf16 = jnp.bfloat16
VMEM = pl.BlockSpec(memory_space=pltpu.VMEM)
SMEM = pl.BlockSpec(memory_space=pltpu.SMEM)


def target_of(index, step, count):
    if count & (count - 1) == 0:
        return index ^ step
    return (index + step) % count


def source_of(index, step, count):
    if count & (count - 1) == 0:
        return index ^ step
    return lax.rem(index + count - step, count)


def dot(left, right):
    return jnp.dot(left, right, preferred_element_type=f32)


def dot_t(left, right):
    return lax.dot_general(left, right, (((1,), (1,)), ((), ())), preferred_element_type=f32)


def pick(index, scalars):
    value = jnp.full(index.shape, scalars[0], jnp.int32)
    for at in range(1, len(scalars)):
        value = jnp.where(index == at, scalars[at], value)
    return value


def three_parts(value):
    high = value.astype(bf16).astype(f32)
    rest = value - high
    middle = rest.astype(bf16).astype(f32)
    return high, middle, rest - middle


def mask_kernel(tokens, suffix_local, lengths, out):
    rows = tokens // STEPS
    suffix_all = rows * suffix_local
    me = lax.axis_index("pre")
    row_at = lax.broadcasted_iota(jnp.int32, out.shape, 0)
    column = lax.broadcasted_iota(jnp.int32, out.shape, 1)
    token = lax.rem(row_at, tokens)
    row_of = token // STEPS
    step = lax.rem(token, STEPS)
    limit = pick(row_of, [lengths[r] for r in range(rows)])
    in_suffix = (
        (column < suffix_all)
        & (column // suffix_local == row_of)
        & (me * suffix_local + lax.rem(column, suffix_local) < limit)
    )
    fresh = column - suffix_all
    in_new = (
        (fresh >= 0)
        & (fresh < tokens)
        & (fresh // STEPS == row_of)
        & (lax.rem(fresh + LANES * STEPS, STEPS) <= step)
        & (me == 0)
    )
    out[...] = (in_suffix | in_new).astype(jnp.int32)


def attend_kernel(
    pre_count,
    ids,
    mask,
    queries,
    prefix_keys,
    prefix_values,
    suffix_keys,
    suffix_values,
    new_keys,
    new_values,
    kv_scales,
    *rest,
):
    outs, (scales, stage) = rest[:pre_count], rest[pre_count:]
    rows = queries.shape[0]
    tokens = rows * STEPS
    suffix_local = suffix_keys.shape[1]
    width = suffix_keys.shape[2]
    suffix_all = rows * suffix_local
    group = HEADS // KV_HEADS
    block = HEADS * HD // pre_count
    block_heads = block // HD
    me = lax.axis_index("pre")
    allowed = mask[...] != 0
    for r in range(rows):
        scales[2 * r : 2 * r + 2, :] = kv_scales[ids[r]].astype(f32)

    query = queries[...].reshape(tokens, HEADS * HD).astype(f32)
    fill = jnp.zeros((LANES - suffix_all - tokens, width), f32)
    scale = scales[...]
    odd = lax.rem(lax.broadcasted_iota(jnp.int32, scale.shape, 0), 2) == 1
    key_scale = jnp.where(odd, pltpu.roll(scale, 1, 0), scale)
    value_scale = jnp.where(odd, scale, pltpu.roll(scale, tokens - 1, 0))
    fresh_key = new_keys[...].reshape(tokens, width).astype(f32) * key_scale
    fresh_value = new_values[...].reshape(tokens, width).astype(f32) * value_scale
    own_keys = jnp.concatenate(
        [
            suffix_keys[...].reshape(suffix_all, width),
            jnp.concatenate([fresh_key, fill], axis=0).astype(bf16),
        ],
        axis=0,
    )
    own_values = jnp.concatenate(
        [
            suffix_values[...].reshape(suffix_all, width),
            jnp.concatenate([fresh_value, fill], axis=0).astype(bf16),
        ],
        axis=0,
    )
    lane = lax.broadcasted_iota(jnp.int32, (tokens, LANES), 1)
    peaks = [jnp.zeros((tokens, LANES), f32) for _ in range(pre_count)]
    sums = [jnp.zeros((tokens, LANES), f32) for _ in range(pre_count)]
    for k in range(KV_HEADS):
        span = slice(k * HD, (k + 1) * HD)
        heads = [query[:, h * HD : (h + 1) * HD] for h in range(k * group, (k + 1) * group)]
        plain = jnp.concatenate(heads, axis=0).astype(bf16)
        scaled = jnp.concatenate([head * key_scale[:, span] for head in heads], axis=0).astype(bf16)
        prefix_scores = dot_t(scaled, prefix_keys[:, span]) * (HD**-0.5)
        own_scores = jnp.where(allowed, dot_t(plain, own_keys[:, span]) * (HD**-0.5), masked_score)
        peak = jnp.max(jnp.maximum(prefix_scores, own_scores), axis=1, keepdims=True)
        prefix_weight = jnp.exp(prefix_scores - peak).astype(bf16)
        own_weight = jnp.where(allowed, jnp.exp(own_scores - peak), 0.0).astype(bf16)
        total = jnp.sum(prefix_weight.astype(f32) + own_weight.astype(f32), axis=1, keepdims=True)
        from_prefix = dot(prefix_weight, prefix_values[:, span])
        from_own = dot(own_weight, own_values[:, span])
        for g in range(group):
            h = k * group + g
            at, j = h // block_heads, h % block_heads
            part = slice(g * tokens, (g + 1) * tokens)
            value = from_prefix[part] * value_scale[:, span] + from_own[part]
            stage[at, :, j * HD : (j + 1) * HD] = value.astype(bf16)
            peaks[at] = jnp.where(lane == j, peak[part], peaks[at])
            sums[at] = jnp.where(lane == j, total[part], sums[at])
    for at in range(pre_count):
        packed = jnp.zeros((tokens, LANES), f32)
        for place, piece in enumerate(three_parts(peaks[at]) + three_parts(sums[at])):
            packed = packed + (pltpu.roll(piece, place * block_heads, 1) if place else piece)
        stage[at, :, block:] = packed.astype(bf16)
    for s in range(pre_count):
        outs[s][...] = stage[target_of(me, s, pre_count)]


def merge_kernel(parts, *rest):
    blocks, out = rest[:parts], rest[parts]
    block = out.shape[1]
    block_heads = block // HD
    peaks, sums = [], []
    for ref in blocks:
        packed = ref[:, block:].astype(f32)
        pieces = [
            pltpu.roll(packed, LANES - place * block_heads, 1) if place else packed
            for place in range(6)
        ]
        peaks.append(pieces[0] + pieces[1] + pieces[2])
        sums.append(pieces[3] + pieces[4] + pieces[5])
    lane = lax.broadcasted_iota(jnp.int32, peaks[0].shape, 1)
    real = lane < block_heads
    highest = functools.reduce(jnp.maximum, peaks)
    factors = [jnp.where(real, jnp.exp(jnp.where(real, peak - highest, 0.0)), 0.0) for peak in peaks]
    total = sum(factor * amount for factor, amount in zip(factors, sums))
    total = jnp.where(real, total, 1.0)
    factors = [factor / total for factor in factors]
    for j in range(block_heads):
        span = slice(j * HD, (j + 1) * HD)
        value = sum(
            ref[:, span].astype(f32) * factor[:, j : j + 1] for ref, factor in zip(blocks, factors)
        )
        out[:, span] = value.astype(bf16)


def project_kernel(row_count, pre_count, *rest):
    blocks, weight = rest[:row_count], rest[row_count]
    outs = rest[row_count + 1 : row_count + 1 + pre_count]
    stacked, product = rest[row_count + 1 + pre_count :]
    tokens = blocks[0].shape[0]
    amount = outs[0].shape[0]
    pre_at, row_at = lax.axis_index("pre"), lax.axis_index("row")
    for s, ref in enumerate(blocks):
        start = pl.multiple_of(source_of(row_at, s, row_count) * tokens, tokens)
        stacked[pl.ds(start, tokens), :] = ref[...].astype(f32)
    product[...] = dot(stacked[...].astype(bf16), weight[...])
    for s, out in enumerate(outs):
        start = pl.multiple_of(target_of(pre_at, s, pre_count) * amount, amount)
        out[...] = product[pl.ds(start, amount), :].astype(out.dtype)


def residual_kernel(parts, hidden, *rest):
    blocks, (out, sent) = rest[:parts], rest[parts:]
    amount, width = sent.shape
    value = sum(ref[...].astype(f32) for ref in blocks)
    value = hidden[...].reshape(amount, width).astype(f32) + value
    sent[...] = value.astype(bf16)
    out[...] = value.astype(bf16).reshape(out.shape)


def column_tile(columns):
    return next(size for size in (512, 256, 128) if columns % size == 0)


def split_columns(wide):
    unit = 512 if wide >= 1024 else LANES
    first = -(-(wide // 2) // unit) * unit
    return first, wide - first


def hand_out(row_count, product, columns, extra, keep, sent):
    rows = product.shape[0] // 2
    tokens = keep.shape[1]
    row_at = lax.axis_index("row")
    for j in range(row_count // 2):
        for at, out in ((row_at ^ (2 * j), keep), (row_at ^ (2 * j + 1), sent)):
            start = pl.multiple_of(at * tokens, tokens)
            own = pl.ds(start, tokens)
            out[j, :, :columns] = product[own, :columns].astype(out.dtype)
            out[j, :, columns : 2 * columns] = product[
                pl.ds(rows + start, tokens), :columns
            ].astype(out.dtype)
            if extra:
                out[j, :, 2 * columns :] = product[own, columns:].astype(out.dtype)


def multiply(left, weight, first, columns, product):
    depth, _, wide = weight.shape
    flat = weight.reshape(2 * depth, wide)
    tile = column_tile(columns)
    for start in range(0, columns, tile):
        product[:, start : start + tile] = dot(
            left, flat[:, first + start : first + start + tile]
        )


def placed_parts(value):
    lane = lax.broadcasted_iota(jnp.int32, (value.shape[0], LANES), 1)
    pieces = three_parts(value)
    return sum(jnp.where(lane == place, piece, 0.0) for place, piece in enumerate(pieces))


def feed_first_kernel(pre_count, row_count, columns, gain, *rest):
    blocks, weight = rest[:pre_count], rest[pre_count]
    keep, sent, spread, stacked, product = rest[pre_count + 1 :]
    amount, depth = blocks[0].shape
    rows = pre_count * amount
    pre_at = lax.axis_index("pre")
    for s, ref in enumerate(blocks):
        start = pl.multiple_of(source_of(pre_at, s, pre_count) * amount, amount)
        stacked[pl.ds(start, amount), :] = ref[...].astype(f32)
    value = stacked[...]
    squares = jnp.sum(value * value, axis=1, keepdims=True)
    normed = (value * gain[...].astype(f32).reshape(1, depth)).astype(bf16)
    source = lax.broadcasted_iota(jnp.int32, (HD, 2 * HD), 0)
    target = lax.broadcasted_iota(jnp.int32, (HD, 2 * HD), 1)
    for b in range(depth // HD):
        piece = normed[:, b * HD : (b + 1) * HD]
        for half in range(2):
            selector = (target == 2 * source + half).astype(bf16)
            spread[half * rows : (half + 1) * rows, 2 * b * HD : 2 * (b + 1) * HD] = dot(
                piece, selector
            ).astype(bf16)
    multiply(spread[...], weight, 0, columns, product)
    product[0:rows, columns:] = placed_parts(squares)
    hand_out(row_count, product, columns, True, keep, sent)


def feed_second_kernel(row_count, first, columns, spread, weight, keep, sent, product):
    multiply(spread[...], weight, first, columns, product)
    hand_out(row_count, product, columns, False, keep, sent)


def pair_kernel(extra, keep, received, *outs):
    for j, out in enumerate(outs):
        value = keep[j] + received[j].astype(f32)
        if extra:
            edge = value.shape[1] - LANES
            out[:, :edge] = value[:, :edge].astype(out.dtype)
            total = jnp.sum(value[:, edge:], axis=1, keepdims=True)
            out[:, edge:] = placed_parts(total).astype(out.dtype)
        else:
            out[...] = value.astype(out.dtype)


def scale_kernel(ids, table, out):
    tokens = out.shape[0]
    adapters = table.shape[0]
    row_of = lax.broadcasted_iota(jnp.int32, (tokens, adapters), 0) // STEPS
    column = lax.broadcasted_iota(jnp.int32, (tokens, adapters), 1)
    chosen = pick(row_of, [ids[r] for r in range(tokens // STEPS)])
    out[...] = dot((chosen == column).astype(bf16), table[...])


def activate_kernel(parts, first, scales, *rest):
    front, back, out = rest[:parts], rest[parts : 2 * parts], rest[2 * parts]
    wide = scales.shape[1]
    squares = sum(ref[:, 2 * first :].astype(f32) for ref in front)
    squares = jnp.sum(squares, axis=1, keepdims=True)
    inverse = lax.rsqrt(squares / D + 1e-05)
    for blocks, start, columns in ((front, 0, first), (back, first, wide - first)):
        gate = sum(ref[:, :columns].astype(f32) for ref in blocks) * inverse
        up = sum(ref[:, columns : 2 * columns].astype(f32) for ref in blocks) * inverse
        value = gate / (1.0 + jnp.exp(-gate)) * up * scales[:, start : start + columns]
        rows, steps, _ = out.shape
        out[:, :, start : start + columns] = value.astype(bf16).reshape(rows, steps, columns)


def shifted(parts, axis):
    count = lax.axis_size(axis)
    return [parts[0]] + [
        lax.ppermute(parts[s], axis, [(i, target_of(i, s, count)) for i in range(count)])
        for s in range(1, count)
    ]


def shape_of(dims, dtype=bf16):
    return jax.ShapeDtypeStruct(dims, dtype)


def params(mib):
    return pltpu.CompilerParams(vmem_limit_bytes=mib << 20)


def cost(micros):
    return pl.CostEstimate(flops=micros * 10**9, bytes_accessed=0, transcendentals=0)


def per_device(
    queries,
    prefix_keys,
    prefix_values,
    suffix_keys,
    suffix_values,
    new_keys,
    new_values,
    hidden,
    adapter_ids,
    suffix_lengths,
    kv_scales,
    ffn_scales,
    out_weight,
    norm_gain,
    gate_up,
):
    rows = queries.shape[0]
    tokens = rows * STEPS
    kv_width = prefix_keys.shape[1]
    pre_count = lax.axis_size("pre")
    row_count = lax.axis_size("row")
    block = HEADS * HD // pre_count
    amount = hidden.shape[0] * STEPS
    out_cols = out_weight.shape[1]
    depth, _, wide = gate_up.shape

    ffn_rows = pl.pallas_call(
        scale_kernel,
        in_specs=[SMEM, VMEM],
        out_specs=VMEM,
        out_shape=shape_of((tokens, wide), f32),
        compiler_params=params(4),
    )(adapter_ids, ffn_scales)

    suffix_local = suffix_keys.shape[1]
    mask = pl.pallas_call(
        functools.partial(mask_kernel, tokens, suffix_local),
        in_specs=[SMEM],
        out_specs=VMEM,
        out_shape=shape_of((HEADS // KV_HEADS * tokens, LANES), jnp.int32),
        compiler_params=params(1),
        cost_estimate=cost(20),
    )(suffix_lengths)
    partials = pl.pallas_call(
        functools.partial(attend_kernel, pre_count),
        in_specs=[SMEM] + [VMEM] * 9,
        out_specs=[VMEM] * pre_count,
        out_shape=[shape_of((tokens, block + LANES))] * pre_count,
        scratch_shapes=[
            pltpu.VMEM((tokens, kv_width), f32),
            pltpu.VMEM((pre_count, tokens, block + LANES), bf16),
        ],
        compiler_params=params(8),
        cost_estimate=cost(20),
    )(
        adapter_ids,
        mask,
        queries,
        prefix_keys,
        prefix_values,
        suffix_keys,
        suffix_values,
        new_keys,
        new_values,
        kv_scales,
    )
    mixed = pl.pallas_call(
        functools.partial(merge_kernel, pre_count),
        in_specs=[VMEM] * pre_count,
        out_specs=VMEM,
        out_shape=shape_of((tokens, block)),
        compiler_params=params(4),
        cost_estimate=cost(40),
    )(*shifted(partials, "pre"))
    gathered = shifted([mixed] * row_count, "row")
    products = pl.pallas_call(
        functools.partial(project_kernel, row_count, pre_count),
        in_specs=[VMEM] * (row_count + 1),
        out_specs=[VMEM] * pre_count,
        out_shape=[
            shape_of((amount, out_cols), bf16 if s else f32) for s in range(pre_count)
        ],
        scratch_shapes=[
            pltpu.VMEM((row_count * tokens, block), f32),
            pltpu.VMEM((row_count * tokens, out_cols), f32),
        ],
        compiler_params=params(8),
        cost_estimate=cost(40),
    )(*gathered, out_weight)
    residual, sent = pl.pallas_call(
        functools.partial(residual_kernel, pre_count),
        in_specs=[VMEM] * (pre_count + 1),
        out_specs=[VMEM] * 2,
        out_shape=[shape_of(hidden.shape), shape_of((amount, out_cols))],
        compiler_params=params(4),
        cost_estimate=cost(40),
    )(hidden, *shifted(products, "pre"))
    stacked = shifted([sent] * pre_count, "pre")
    total_rows = pre_count * amount
    half = row_count // 2
    first, second = split_columns(wide)
    sizes = (2 * first + LANES, 2 * second)
    *front, spread = pl.pallas_call(
        functools.partial(feed_first_kernel, pre_count, row_count, first),
        in_specs=[VMEM] * (pre_count + 2),
        out_specs=[VMEM] * 3,
        out_shape=[
            shape_of((half, tokens, sizes[0]), f32),
            shape_of((half, tokens, sizes[0])),
            shape_of((2 * total_rows, 2 * depth)),
        ],
        scratch_shapes=[
            pltpu.VMEM((total_rows, depth), f32),
            pltpu.VMEM((2 * total_rows, first + LANES), f32),
        ],
        compiler_params=params(8),
        cost_estimate=cost(16),
    )(norm_gain, *stacked, gate_up)
    back = pl.pallas_call(
        functools.partial(feed_second_kernel, row_count, first, second),
        in_specs=[VMEM] * 2,
        out_specs=[VMEM] * 2,
        out_shape=[
            shape_of((half, tokens, sizes[1]), f32),
            shape_of((half, tokens, sizes[1])),
        ],
        scratch_shapes=[pltpu.VMEM((2 * total_rows, second), f32)],
        compiler_params=pltpu.CompilerParams(
            vmem_limit_bytes=(8 << 20) + 2 * depth * (total_rows + 1)
        ),
        cost_estimate=cost(16),
    )(spread, gate_up)
    finals = []
    for extra, size, (keep, sent) in ((True, sizes[0], front), (False, sizes[1], back)):
        received = lax.ppermute(sent, "row", [(i, i ^ 1) for i in range(row_count)])
        sums = pl.pallas_call(
            functools.partial(pair_kernel, extra),
            in_specs=[VMEM] * 2,
            out_specs=[VMEM] * half,
            out_shape=[shape_of((tokens, size), bf16 if j else f32) for j in range(half)],
            compiler_params=params(4),
        )(keep, received)
        finals.append(sums[0])
        finals += [
            lax.ppermute(sums[j], "row", [(i, i ^ (2 * j)) for i in range(row_count)])
            for j in range(1, half)
        ]
    activation = pl.pallas_call(
        functools.partial(activate_kernel, half, first),
        in_specs=[VMEM] * (2 * half + 1),
        out_specs=VMEM,
        out_shape=shape_of((rows, STEPS, wide)),
        compiler_params=params(4),
    )(ffn_rows, *finals)
    return (residual, activation)


def solution(mesh):
    placed = (
        P(("grp", "row"), None, None),
        P(("grp", "pre"), None),
        P(("grp", "pre"), None),
        P(("grp", "row"), "pre", None),
        P(("grp", "row"), "pre", None),
        P(("grp", "row"), None, None),
        P(("grp", "row"), None, None),
        P(("grp", "pre"), None, "row"),
        P(("grp", "row")),
        P(("grp", "row")),
        P(),
        P(None, "pre"),
        P("pre", "row"),
        P("row"),
        P("row", None, "pre"),
    )
    return jax.shard_map(
        per_device,
        mesh=mesh,
        in_specs=placed,
        out_specs=(P(("grp", "pre"), None, "row"), P(("grp", "row"), None, "pre")),
        check_vma=False,
    )
```

```python
import functools

import jax
import jax.numpy as jnp
from jax import lax
from jax.experimental import pallas as pl
from jax.experimental.pallas import tpu as pltpu
from jax.sharding import PartitionSpec as P

D = 8192
HEADS = 64
KV_HEADS = 8
HD = 128
STEPS = 2
LANES = 128

masked_score = -1e30
f32 = jnp.float32
bf16 = jnp.bfloat16
VMEM = pl.BlockSpec(memory_space=pltpu.VMEM)
SMEM = pl.BlockSpec(memory_space=pltpu.SMEM)


def target_of(index, step, count):
    if count & (count - 1) == 0:
        return index ^ step
    return (index + step) % count


def source_of(index, step, count):
    if count & (count - 1) == 0:
        return index ^ step
    return lax.rem(index + count - step, count)


def dot(left, right):
    return jnp.dot(left, right, preferred_element_type=f32)


def dot_t(left, right):
    return lax.dot_general(left, right, (((1,), (1,)), ((), ())), preferred_element_type=f32)


def pick(index, scalars):
    value = jnp.full(index.shape, scalars[0], jnp.int32)
    for at in range(1, len(scalars)):
        value = jnp.where(index == at, scalars[at], value)
    return value


def three_parts(value):
    high = value.astype(bf16).astype(f32)
    rest = value - high
    middle = rest.astype(bf16).astype(f32)
    return high, middle, rest - middle


def mask_kernel(tokens, suffix_local, lengths, out):
    rows = tokens // STEPS
    suffix_all = rows * suffix_local
    me = lax.axis_index("pre")
    row_at = lax.broadcasted_iota(jnp.int32, out.shape, 0)
    column = lax.broadcasted_iota(jnp.int32, out.shape, 1)
    token = lax.rem(row_at, tokens)
    row_of = token // STEPS
    step = lax.rem(token, STEPS)
    limit = pick(row_of, [lengths[r] for r in range(rows)])
    in_suffix = (
        (column < suffix_all)
        & (column // suffix_local == row_of)
        & (me * suffix_local + lax.rem(column, suffix_local) < limit)
    )
    fresh = column - suffix_all
    in_new = (
        (fresh >= 0)
        & (fresh < tokens)
        & (fresh // STEPS == row_of)
        & (lax.rem(fresh + LANES * STEPS, STEPS) <= step)
        & (me == 0)
    )
    out[...] = (in_suffix | in_new).astype(jnp.int32)


def attend_kernel(
    pre_count,
    ids,
    mask,
    queries,
    prefix_keys,
    prefix_values,
    suffix_keys,
    suffix_values,
    new_keys,
    new_values,
    kv_scales,
    *rest,
):
    outs, (scales, stage) = rest[:pre_count], rest[pre_count:]
    rows = queries.shape[0]
    tokens = rows * STEPS
    suffix_local = suffix_keys.shape[1]
    width = suffix_keys.shape[2]
    suffix_all = rows * suffix_local
    group = HEADS // KV_HEADS
    block = HEADS * HD // pre_count
    block_heads = block // HD
    me = lax.axis_index("pre")
    allowed = mask[...] != 0
    for r in range(rows):
        scales[2 * r : 2 * r + 2, :] = kv_scales[ids[r]].astype(f32)

    query = queries[...].reshape(tokens, HEADS * HD).astype(f32)
    fill = jnp.zeros((LANES - suffix_all - tokens, width), f32)
    scale = scales[...]
    odd = lax.rem(lax.broadcasted_iota(jnp.int32, scale.shape, 0), 2) == 1
    key_scale = jnp.where(odd, pltpu.roll(scale, 1, 0), scale)
    value_scale = jnp.where(odd, scale, pltpu.roll(scale, tokens - 1, 0))
    fresh_key = new_keys[...].reshape(tokens, width).astype(f32) * key_scale
    fresh_value = new_values[...].reshape(tokens, width).astype(f32) * value_scale
    own_keys = jnp.concatenate(
        [
            suffix_keys[...].reshape(suffix_all, width),
            jnp.concatenate([fresh_key, fill], axis=0).astype(bf16),
        ],
        axis=0,
    )
    own_values = jnp.concatenate(
        [
            suffix_values[...].reshape(suffix_all, width),
            jnp.concatenate([fresh_value, fill], axis=0).astype(bf16),
        ],
        axis=0,
    )
    lane = lax.broadcasted_iota(jnp.int32, (tokens, LANES), 1)
    peaks = [jnp.zeros((tokens, LANES), f32) for _ in range(pre_count)]
    sums = [jnp.zeros((tokens, LANES), f32) for _ in range(pre_count)]
    for k in range(KV_HEADS):
        span = slice(k * HD, (k + 1) * HD)
        heads = [query[:, h * HD : (h + 1) * HD] for h in range(k * group, (k + 1) * group)]
        plain = jnp.concatenate(heads, axis=0).astype(bf16)
        scaled = jnp.concatenate([head * key_scale[:, span] for head in heads], axis=0).astype(bf16)
        prefix_scores = dot_t(scaled, prefix_keys[:, span]) * (HD**-0.5)
        own_scores = jnp.where(allowed, dot_t(plain, own_keys[:, span]) * (HD**-0.5), masked_score)
        peak = jnp.max(jnp.maximum(prefix_scores, own_scores), axis=1, keepdims=True)
        prefix_weight = jnp.exp(prefix_scores - peak).astype(bf16)
        own_weight = jnp.where(allowed, jnp.exp(own_scores - peak), 0.0).astype(bf16)
        total = jnp.sum(prefix_weight.astype(f32) + own_weight.astype(f32), axis=1, keepdims=True)
        from_prefix = dot(prefix_weight, prefix_values[:, span])
        from_own = dot(own_weight, own_values[:, span])
        for g in range(group):
            h = k * group + g
            at, j = h // block_heads, h % block_heads
            part = slice(g * tokens, (g + 1) * tokens)
            value = from_prefix[part] * value_scale[:, span] + from_own[part]
            stage[at, :, j * HD : (j + 1) * HD] = value.astype(bf16)
            peaks[at] = jnp.where(lane == j, peak[part], peaks[at])
            sums[at] = jnp.where(lane == j, total[part], sums[at])
    for at in range(pre_count):
        packed = jnp.zeros((tokens, LANES), f32)
        for place, piece in enumerate(three_parts(peaks[at]) + three_parts(sums[at])):
            packed = packed + (pltpu.roll(piece, place * block_heads, 1) if place else piece)
        stage[at, :, block:] = packed.astype(bf16)
    for s in range(pre_count):
        outs[s][...] = stage[target_of(me, s, pre_count)]


def merge_kernel(parts, *rest):
    blocks, out = rest[:parts], rest[parts]
    block = out.shape[1]
    block_heads = block // HD
    peaks, sums = [], []
    for ref in blocks:
        packed = ref[:, block:].astype(f32)
        pieces = [
            pltpu.roll(packed, LANES - place * block_heads, 1) if place else packed
            for place in range(6)
        ]
        peaks.append(pieces[0] + pieces[1] + pieces[2])
        sums.append(pieces[3] + pieces[4] + pieces[5])
    lane = lax.broadcasted_iota(jnp.int32, peaks[0].shape, 1)
    real = lane < block_heads
    highest = functools.reduce(jnp.maximum, peaks)
    factors = [jnp.where(real, jnp.exp(jnp.where(real, peak - highest, 0.0)), 0.0) for peak in peaks]
    total = sum(factor * amount for factor, amount in zip(factors, sums))
    total = jnp.where(real, total, 1.0)
    factors = [factor / total for factor in factors]
    for j in range(block_heads):
        span = slice(j * HD, (j + 1) * HD)
        value = sum(
            ref[:, span].astype(f32) * factor[:, j : j + 1] for ref, factor in zip(blocks, factors)
        )
        out[:, span] = value.astype(bf16)


def project_kernel(row_count, pre_count, *rest):
    blocks, weight = rest[:row_count], rest[row_count]
    outs = rest[row_count + 1 : row_count + 1 + pre_count]
    stacked, product = rest[row_count + 1 + pre_count :]
    tokens = blocks[0].shape[0]
    amount = outs[0].shape[0]
    pre_at, row_at = lax.axis_index("pre"), lax.axis_index("row")
    for s, ref in enumerate(blocks):
        start = pl.multiple_of(source_of(row_at, s, row_count) * tokens, tokens)
        stacked[pl.ds(start, tokens), :] = ref[...].astype(f32)
    product[...] = dot(stacked[...].astype(bf16), weight[...])
    for s, out in enumerate(outs):
        start = pl.multiple_of(target_of(pre_at, s, pre_count) * amount, amount)
        out[...] = product[pl.ds(start, amount), :].astype(out.dtype)


def residual_kernel(parts, hidden, *rest):
    blocks, (out, sent) = rest[:parts], rest[parts:]
    amount, width = sent.shape
    value = sum(ref[...].astype(f32) for ref in blocks)
    value = hidden[...].reshape(amount, width).astype(f32) + value
    sent[...] = value.astype(bf16)
    out[...] = value.astype(bf16).reshape(out.shape)


def column_tile(columns):
    return next(size for size in (512, 256, 128) if columns % size == 0)


def split_columns(wide):
    unit = 512 if wide >= 1024 else LANES
    first = -(-(wide // 2) // unit) * unit
    return first, wide - first


def hand_out(row_count, product, columns, extra, keep, sent):
    rows = product.shape[0] // 2
    tokens = keep.shape[1]
    row_at = lax.axis_index("row")
    for j in range(row_count // 2):
        for at, out in ((row_at ^ (2 * j), keep), (row_at ^ (2 * j + 1), sent)):
            start = pl.multiple_of(at * tokens, tokens)
            own = pl.ds(start, tokens)
            out[j, :, :columns] = product[own, :columns].astype(out.dtype)
            out[j, :, columns : 2 * columns] = product[
                pl.ds(rows + start, tokens), :columns
            ].astype(out.dtype)
            if extra:
                out[j, :, 2 * columns :] = product[own, columns:].astype(out.dtype)


def multiply(left, weight, first, columns, product):
    depth, _, wide = weight.shape
    flat = weight.reshape(2 * depth, wide)
    tile = column_tile(columns)
    for start in range(0, columns, tile):
        product[:, start : start + tile] = dot(
            left, flat[:, first + start : first + start + tile]
        )


def placed_parts(value):
    lane = lax.broadcasted_iota(jnp.int32, (value.shape[0], LANES), 1)
    pieces = three_parts(value)
    return sum(jnp.where(lane == place, piece, 0.0) for place, piece in enumerate(pieces))


def feed_first_kernel(pre_count, row_count, columns, gain, *rest):
    blocks, weight = rest[:pre_count], rest[pre_count]
    keep, sent, spread, stacked, product = rest[pre_count + 1 :]
    amount, depth = blocks[0].shape
    rows = pre_count * amount
    pre_at = lax.axis_index("pre")
    for s, ref in enumerate(blocks):
        start = pl.multiple_of(source_of(pre_at, s, pre_count) * amount, amount)
        stacked[pl.ds(start, amount), :] = ref[...].astype(f32)
    value = stacked[...]
    squares = jnp.sum(value * value, axis=1, keepdims=True)
    normed = (value * gain[...].astype(f32).reshape(1, depth)).astype(bf16)
    source = lax.broadcasted_iota(jnp.int32, (HD, 2 * HD), 0)
    target = lax.broadcasted_iota(jnp.int32, (HD, 2 * HD), 1)
    for b in range(depth // HD):
        piece = normed[:, b * HD : (b + 1) * HD]
        for half in range(2):
            selector = (target == 2 * source + half).astype(bf16)
            spread[half * rows : (half + 1) * rows, 2 * b * HD : 2 * (b + 1) * HD] = dot(
                piece, selector
            ).astype(bf16)
    multiply(spread[...], weight, 0, columns, product)
    product[0:rows, columns:] = placed_parts(squares)
    hand_out(row_count, product, columns, True, keep, sent)


def feed_second_kernel(row_count, first, columns, spread, weight, keep, sent, product):
    multiply(spread[...], weight, first, columns, product)
    hand_out(row_count, product, columns, False, keep, sent)


def pair_kernel(extra, keep, received, *outs):
    for j, out in enumerate(outs):
        value = keep[j] + received[j].astype(f32)
        if extra:
            edge = value.shape[1] - LANES
            out[:, :edge] = value[:, :edge].astype(out.dtype)
            total = jnp.sum(value[:, edge:], axis=1, keepdims=True)
            out[:, edge:] = placed_parts(total).astype(out.dtype)
        else:
            out[...] = value.astype(out.dtype)


def scale_kernel(ids, table, out):
    tokens = out.shape[0]
    adapters = table.shape[0]
    row_of = lax.broadcasted_iota(jnp.int32, (tokens, adapters), 0) // STEPS
    column = lax.broadcasted_iota(jnp.int32, (tokens, adapters), 1)
    chosen = pick(row_of, [ids[r] for r in range(tokens // STEPS)])
    out[...] = dot((chosen == column).astype(bf16), table[...])


def activate_kernel(parts, first, scales, *rest):
    front, back, out = rest[:parts], rest[parts : 2 * parts], rest[2 * parts]
    wide = scales.shape[1]
    squares = sum(ref[:, 2 * first :].astype(f32) for ref in front)
    squares = jnp.sum(squares, axis=1, keepdims=True)
    inverse = lax.rsqrt(squares / D + 1e-05)
    for blocks, start, columns in ((front, 0, first), (back, first, wide - first)):
        gate = sum(ref[:, :columns].astype(f32) for ref in blocks) * inverse
        up = sum(ref[:, columns : 2 * columns].astype(f32) for ref in blocks) * inverse
        value = gate / (1.0 + jnp.exp(-gate)) * up * scales[:, start : start + columns]
        rows, steps, _ = out.shape
        out[:, :, start : start + columns] = value.astype(bf16).reshape(rows, steps, columns)


def shifted(parts, axis):
    count = lax.axis_size(axis)
    return [parts[0]] + [
        lax.ppermute(parts[s], axis, [(i, target_of(i, s, count)) for i in range(count)])
        for s in range(1, count)
    ]


def gathered_pairs(value, axis):
    count = lax.axis_size(axis)
    if count & (count - 1) or count < 2:
        return shifted([value] * count, axis)
    near = [(i, i ^ 1) for i in range(count)]
    parts = []
    for s in range(0, count, 2):
        far = lax.ppermute(value, axis, [(i, i ^ s) for i in range(count)]) if s else value
        parts += [far, lax.ppermute(far, axis, near)]
    return parts


def shape_of(dims, dtype=bf16):
    return jax.ShapeDtypeStruct(dims, dtype)


def params(mib):
    return pltpu.CompilerParams(vmem_limit_bytes=mib << 20)


def cost(micros):
    return pl.CostEstimate(flops=micros * 10**9, bytes_accessed=0, transcendentals=0)


def per_device(
    queries,
    prefix_keys,
    prefix_values,
    suffix_keys,
    suffix_values,
    new_keys,
    new_values,
    hidden,
    adapter_ids,
    suffix_lengths,
    kv_scales,
    ffn_scales,
    out_weight,
    norm_gain,
    gate_up,
):
    rows = queries.shape[0]
    tokens = rows * STEPS
    kv_width = prefix_keys.shape[1]
    pre_count = lax.axis_size("pre")
    row_count = lax.axis_size("row")
    block = HEADS * HD // pre_count
    amount = hidden.shape[0] * STEPS
    out_cols = out_weight.shape[1]
    depth, _, wide = gate_up.shape

    ffn_rows = pl.pallas_call(
        scale_kernel,
        in_specs=[SMEM, VMEM],
        out_specs=VMEM,
        out_shape=shape_of((tokens, wide), f32),
        compiler_params=params(4),
    )(adapter_ids, ffn_scales)

    suffix_local = suffix_keys.shape[1]
    mask = pl.pallas_call(
        functools.partial(mask_kernel, tokens, suffix_local),
        in_specs=[SMEM],
        out_specs=VMEM,
        out_shape=shape_of((HEADS // KV_HEADS * tokens, LANES), jnp.int32),
        compiler_params=params(1),
        cost_estimate=cost(20),
    )(suffix_lengths)
    partials = pl.pallas_call(
        functools.partial(attend_kernel, pre_count),
        in_specs=[SMEM] + [VMEM] * 9,
        out_specs=[VMEM] * pre_count,
        out_shape=[shape_of((tokens, block + LANES))] * pre_count,
        scratch_shapes=[
            pltpu.VMEM((tokens, kv_width), f32),
            pltpu.VMEM((pre_count, tokens, block + LANES), bf16),
        ],
        compiler_params=params(8),
        cost_estimate=cost(20),
    )(
        adapter_ids,
        mask,
        queries,
        prefix_keys,
        prefix_values,
        suffix_keys,
        suffix_values,
        new_keys,
        new_values,
        kv_scales,
    )
    mixed = pl.pallas_call(
        functools.partial(merge_kernel, pre_count),
        in_specs=[VMEM] * pre_count,
        out_specs=VMEM,
        out_shape=shape_of((tokens, block)),
        compiler_params=params(4),
        cost_estimate=cost(40),
    )(*shifted(partials, "pre"))
    gathered = gathered_pairs(mixed, "row")
    products = pl.pallas_call(
        functools.partial(project_kernel, row_count, pre_count),
        in_specs=[VMEM] * (row_count + 1),
        out_specs=[VMEM] * pre_count,
        out_shape=[
            shape_of((amount, out_cols), bf16 if s else f32) for s in range(pre_count)
        ],
        scratch_shapes=[
            pltpu.VMEM((row_count * tokens, block), f32),
            pltpu.VMEM((row_count * tokens, out_cols), f32),
        ],
        compiler_params=params(8),
        cost_estimate=cost(40),
    )(*gathered, out_weight)
    residual, sent = pl.pallas_call(
        functools.partial(residual_kernel, pre_count),
        in_specs=[VMEM] * (pre_count + 1),
        out_specs=[VMEM] * 2,
        out_shape=[shape_of(hidden.shape), shape_of((amount, out_cols))],
        compiler_params=params(4),
        cost_estimate=cost(40),
    )(hidden, *shifted(products, "pre"))
    stacked = gathered_pairs(sent, "pre")
    total_rows = pre_count * amount
    half = row_count // 2
    first, second = split_columns(wide)
    sizes = (2 * first + LANES, 2 * second)
    *front, spread = pl.pallas_call(
        functools.partial(feed_first_kernel, pre_count, row_count, first),
        in_specs=[VMEM] * (pre_count + 2),
        out_specs=[VMEM] * 3,
        out_shape=[
            shape_of((half, tokens, sizes[0]), f32),
            shape_of((half, tokens, sizes[0])),
            shape_of((2 * total_rows, 2 * depth)),
        ],
        scratch_shapes=[
            pltpu.VMEM((total_rows, depth), f32),
            pltpu.VMEM((2 * total_rows, first + LANES), f32),
        ],
        compiler_params=params(8),
        cost_estimate=cost(16),
    )(norm_gain, *stacked, gate_up)
    back = pl.pallas_call(
        functools.partial(feed_second_kernel, row_count, first, second),
        in_specs=[VMEM] * 2,
        out_specs=[VMEM] * 2,
        out_shape=[
            shape_of((half, tokens, sizes[1]), f32),
            shape_of((half, tokens, sizes[1])),
        ],
        scratch_shapes=[pltpu.VMEM((2 * total_rows, second), f32)],
        compiler_params=pltpu.CompilerParams(
            vmem_limit_bytes=(8 << 20) + 2 * depth * (total_rows + 1)
        ),
        cost_estimate=cost(16),
    )(spread, gate_up)
    finals = []
    for extra, size, (keep, sent) in ((True, sizes[0], front), (False, sizes[1], back)):
        received = lax.ppermute(sent, "row", [(i, i ^ 1) for i in range(row_count)])
        sums = pl.pallas_call(
            functools.partial(pair_kernel, extra),
            in_specs=[VMEM] * 2,
            out_specs=[VMEM] * half,
            out_shape=[shape_of((tokens, size), bf16 if j else f32) for j in range(half)],
            compiler_params=params(4),
        )(keep, received)
        finals.append(sums[0])
        finals += [
            lax.ppermute(sums[j], "row", [(i, i ^ (2 * j)) for i in range(row_count)])
            for j in range(1, half)
        ]
    activation = pl.pallas_call(
        functools.partial(activate_kernel, half, first),
        in_specs=[VMEM] * (2 * half + 1),
        out_specs=VMEM,
        out_shape=shape_of((rows, STEPS, wide)),
        compiler_params=params(4),
    )(ffn_rows, *finals)
    return (residual, activation)


def solution(mesh):
    placed = (
        P(("grp", "row"), None, None),
        P(("grp", "pre"), None),
        P(("grp", "pre"), None),
        P(("grp", "row"), "pre", None),
        P(("grp", "row"), "pre", None),
        P(("grp", "row"), None, None),
        P(("grp", "row"), None, None),
        P(("grp", "pre"), None, "row"),
        P(("grp", "row")),
        P(("grp", "row")),
        P(),
        P(None, "pre"),
        P("pre", "row"),
        P("row"),
        P("row", None, "pre"),
    )
    return jax.shard_map(
        per_device,
        mesh=mesh,
        in_specs=placed,
        out_specs=(P(("grp", "pre"), None, "row"), P(("grp", "row"), None, "pre")),
        check_vma=False,
    )
```

```python
import functools

import jax
import jax.numpy as jnp
from jax import lax
from jax.experimental import pallas as pl
from jax.experimental.pallas import tpu as pltpu
from jax.sharding import PartitionSpec as P

D = 8192
HEADS = 64
KV_HEADS = 8
HD = 128
STEPS = 2
LANES = 128

masked_score = -1e30
f32 = jnp.float32
bf16 = jnp.bfloat16
VMEM = pl.BlockSpec(memory_space=pltpu.VMEM)
SMEM = pl.BlockSpec(memory_space=pltpu.SMEM)


def target_of(index, step, count):
    if count & (count - 1) == 0:
        return index ^ step
    return (index + step) % count


def source_of(index, step, count):
    if count & (count - 1) == 0:
        return index ^ step
    return lax.rem(index + count - step, count)


def dot(left, right):
    return jnp.dot(left, right, preferred_element_type=f32)


def dot_t(left, right):
    return lax.dot_general(left, right, (((1,), (1,)), ((), ())), preferred_element_type=f32)


def pick(index, scalars):
    value = jnp.full(index.shape, scalars[0], jnp.int32)
    for at in range(1, len(scalars)):
        value = jnp.where(index == at, scalars[at], value)
    return value


def three_parts(value):
    high = value.astype(bf16).astype(f32)
    rest = value - high
    middle = rest.astype(bf16).astype(f32)
    return high, middle, rest - middle


def mask_kernel(tokens, suffix_local, lengths, out):
    rows = tokens // STEPS
    suffix_all = rows * suffix_local
    me = lax.axis_index("pre")
    token = lax.broadcasted_iota(jnp.int32, out.shape, 0)
    column = lax.broadcasted_iota(jnp.int32, out.shape, 1)
    row_of = token // STEPS
    step = token - row_of * STEPS
    limit = pick(row_of, [lengths[r] for r in range(rows)])
    at = column - row_of * suffix_local
    in_suffix = (at >= 0) & (at < suffix_local) & (me * suffix_local + at < limit)
    fresh = column - suffix_all - row_of * STEPS
    in_new = (fresh >= 0) & (fresh <= step) & (me == 0)
    out[...] = (in_suffix | in_new).astype(jnp.int32)


def attend_kernel(
    pre_count,
    ids,
    mask,
    queries,
    prefix_keys,
    prefix_values,
    suffix_keys,
    suffix_values,
    new_keys,
    new_values,
    kv_scales,
    *rest,
):
    outs, (scales, stage) = rest[:pre_count], rest[pre_count:]
    rows = queries.shape[0]
    tokens = rows * STEPS
    suffix_local = suffix_keys.shape[1]
    width = suffix_keys.shape[2]
    suffix_all = rows * suffix_local
    group = HEADS // KV_HEADS
    block = HEADS * HD // pre_count
    block_heads = block // HD
    me = lax.axis_index("pre")
    allowed = jnp.concatenate([mask[...]] * group, axis=0) != 0
    for r in range(rows):
        scales[2 * r : 2 * r + 2, :] = kv_scales[ids[r]].astype(f32)

    query = queries[...].reshape(tokens, HEADS * HD).astype(f32)
    fill = jnp.zeros((LANES - suffix_all - tokens, width), f32)
    scale = scales[...]
    odd = lax.rem(lax.broadcasted_iota(jnp.int32, scale.shape, 0), 2) == 1
    key_scale = jnp.where(odd, pltpu.roll(scale, 1, 0), scale)
    value_scale = jnp.where(odd, scale, pltpu.roll(scale, tokens - 1, 0))
    fresh_key = new_keys[...].reshape(tokens, width).astype(f32) * key_scale
    fresh_value = new_values[...].reshape(tokens, width).astype(f32) * value_scale
    own_keys = jnp.concatenate(
        [
            suffix_keys[...].reshape(suffix_all, width),
            jnp.concatenate([fresh_key, fill], axis=0).astype(bf16),
        ],
        axis=0,
    )
    own_values = jnp.concatenate(
        [
            suffix_values[...].reshape(suffix_all, width),
            jnp.concatenate([fresh_value, fill], axis=0).astype(bf16),
        ],
        axis=0,
    )
    lane = lax.broadcasted_iota(jnp.int32, (tokens, LANES), 1)
    peaks = [jnp.zeros((tokens, LANES), f32) for _ in range(pre_count)]
    sums = [jnp.zeros((tokens, LANES), f32) for _ in range(pre_count)]
    for k in range(KV_HEADS):
        span = slice(k * HD, (k + 1) * HD)
        heads = [query[:, h * HD : (h + 1) * HD] for h in range(k * group, (k + 1) * group)]
        plain = jnp.concatenate(heads, axis=0).astype(bf16)
        scaled = jnp.concatenate([head * key_scale[:, span] for head in heads], axis=0).astype(bf16)
        prefix_scores = dot_t(scaled, prefix_keys[:, span]) * (HD**-0.5)
        own_scores = jnp.where(allowed, dot_t(plain, own_keys[:, span]) * (HD**-0.5), masked_score)
        peak = jnp.max(jnp.maximum(prefix_scores, own_scores), axis=1, keepdims=True)
        prefix_weight = jnp.exp(prefix_scores - peak).astype(bf16)
        own_weight = jnp.where(allowed, jnp.exp(own_scores - peak), 0.0).astype(bf16)
        total = jnp.sum(prefix_weight.astype(f32) + own_weight.astype(f32), axis=1, keepdims=True)
        from_prefix = dot(prefix_weight, prefix_values[:, span])
        from_own = dot(own_weight, own_values[:, span])
        for g in range(group):
            h = k * group + g
            at, j = h // block_heads, h % block_heads
            part = slice(g * tokens, (g + 1) * tokens)
            value = from_prefix[part] * value_scale[:, span] + from_own[part]
            stage[at, :, j * HD : (j + 1) * HD] = value.astype(bf16)
            peaks[at] = jnp.where(lane == j, peak[part], peaks[at])
            sums[at] = jnp.where(lane == j, total[part], sums[at])
    for at in range(pre_count):
        packed = jnp.zeros((tokens, LANES), f32)
        for place, piece in enumerate(three_parts(peaks[at]) + three_parts(sums[at])):
            packed = packed + (pltpu.roll(piece, place * block_heads, 1) if place else piece)
        stage[at, :, block:] = packed.astype(bf16)
    for s in range(pre_count):
        outs[s][...] = stage[target_of(me, s, pre_count)]


def merge_kernel(parts, *rest):
    blocks, out = rest[:parts], rest[parts]
    block = out.shape[1]
    block_heads = block // HD
    peaks, sums = [], []
    for ref in blocks:
        packed = ref[:, block:].astype(f32)
        pieces = [
            pltpu.roll(packed, LANES - place * block_heads, 1) if place else packed
            for place in range(6)
        ]
        peaks.append(pieces[0] + pieces[1] + pieces[2])
        sums.append(pieces[3] + pieces[4] + pieces[5])
    lane = lax.broadcasted_iota(jnp.int32, peaks[0].shape, 1)
    real = lane < block_heads
    highest = functools.reduce(jnp.maximum, peaks)
    factors = [jnp.where(real, jnp.exp(jnp.where(real, peak - highest, 0.0)), 0.0) for peak in peaks]
    total = sum(factor * amount for factor, amount in zip(factors, sums))
    total = jnp.where(real, total, 1.0)
    factors = [factor / total for factor in factors]
    for j in range(block_heads):
        span = slice(j * HD, (j + 1) * HD)
        value = sum(
            ref[:, span].astype(f32) * factor[:, j : j + 1] for ref, factor in zip(blocks, factors)
        )
        out[:, span] = value.astype(bf16)


def project_kernel(row_count, pre_count, *rest):
    blocks, weight = rest[:row_count], rest[row_count]
    outs = rest[row_count + 1 : row_count + 1 + pre_count]
    stacked, product = rest[row_count + 1 + pre_count :]
    tokens = blocks[0].shape[0]
    amount = outs[0].shape[0]
    pre_at, row_at = lax.axis_index("pre"), lax.axis_index("row")
    for s, ref in enumerate(blocks):
        start = pl.multiple_of(source_of(row_at, s, row_count) * tokens, tokens)
        stacked[pl.ds(start, tokens), :] = ref[...].astype(f32)
    product[...] = dot(stacked[...].astype(bf16), weight[...])
    for s, out in enumerate(outs):
        start = pl.multiple_of(target_of(pre_at, s, pre_count) * amount, amount)
        out[...] = product[pl.ds(start, amount), :].astype(out.dtype)


def residual_kernel(parts, hidden, *rest):
    blocks, (out, sent) = rest[:parts], rest[parts:]
    amount, width = sent.shape
    value = sum(ref[...].astype(f32) for ref in blocks)
    value = hidden.reshape(amount, width)[...].astype(f32) + value
    sent[...] = value.astype(bf16)
    out.reshape(amount, width)[...] = value.astype(bf16)


def column_tile(columns):
    return next(size for size in (512, 256, 128) if columns % size == 0)


def split_columns(wide):
    unit = 512 if wide >= 1024 else LANES
    first = -(-(wide // 2) // unit) * unit
    return first, wide - first


def hand_out(row_count, product, columns, extra, keep, sent):
    rows = product.shape[0] // 2
    tokens = keep.shape[1]
    row_at = lax.axis_index("row")
    for j in range(row_count // 2):
        for at, out in ((row_at ^ (2 * j), keep), (row_at ^ (2 * j + 1), sent)):
            start = pl.multiple_of(at * tokens, tokens)
            own = pl.ds(start, tokens)
            out[j, :, :columns] = product[own, :columns].astype(out.dtype)
            out[j, :, columns : 2 * columns] = product[
                pl.ds(rows + start, tokens), :columns
            ].astype(out.dtype)
            if extra:
                out[j, :, 2 * columns :] = product[own, columns:].astype(out.dtype)


def multiply(left, weight, first, columns, product):
    depth, _, wide = weight.shape
    flat = weight.reshape(2 * depth, wide)
    tile = column_tile(columns)
    for start in range(0, columns, tile):
        product[:, start : start + tile] = dot(
            left, flat[:, first + start : first + start + tile]
        )


def placed_parts(value):
    lane = lax.broadcasted_iota(jnp.int32, (value.shape[0], LANES), 1)
    pieces = three_parts(value)
    return sum(jnp.where(lane == place, piece, 0.0) for place, piece in enumerate(pieces))


def feed_first_kernel(pre_count, row_count, columns, gain, *rest):
    blocks, weight = rest[:pre_count], rest[pre_count]
    keep, sent, spread, stacked, product = rest[pre_count + 1 :]
    amount, depth = blocks[0].shape
    rows = pre_count * amount
    pre_at = lax.axis_index("pre")
    for s, ref in enumerate(blocks):
        start = pl.multiple_of(source_of(pre_at, s, pre_count) * amount, amount)
        stacked[pl.ds(start, amount), :] = ref[...].astype(f32)
    value = stacked[...]
    squares = jnp.sum(value * value, axis=1, keepdims=True)
    normed = (value * gain[...].astype(f32).reshape(1, depth)).astype(bf16)
    source = lax.broadcasted_iota(jnp.int32, (HD, 2 * HD), 0)
    target = lax.broadcasted_iota(jnp.int32, (HD, 2 * HD), 1)
    pieces = jnp.concatenate(
        [normed[:, b * HD : (b + 1) * HD] for b in range(depth // HD)], axis=0
    )
    for half in range(2):
        selector = (target == 2 * source + half).astype(bf16)
        wider = dot(pieces, selector).astype(bf16)
        for b in range(depth // HD):
            spread[half * rows : (half + 1) * rows, 2 * b * HD : 2 * (b + 1) * HD] = wider[
                b * rows : (b + 1) * rows
            ]
    multiply(spread[...], weight, 0, columns, product)
    product[0:rows, columns:] = placed_parts(squares)
    hand_out(row_count, product, columns, True, keep, sent)


def feed_second_kernel(row_count, first, columns, spread, weight, keep, sent, product):
    multiply(spread[...], weight, first, columns, product)
    hand_out(row_count, product, columns, False, keep, sent)


def pair_kernel(extra, keep, received, *outs):
    for j, out in enumerate(outs):
        value = keep[j] + received[j].astype(f32)
        if extra:
            edge = value.shape[1] - LANES
            out[:, :edge] = value[:, :edge].astype(out.dtype)
            total = jnp.sum(value[:, edge:], axis=1, keepdims=True)
            out[:, edge:] = placed_parts(total).astype(out.dtype)
        else:
            out[...] = value.astype(out.dtype)


def scale_kernel(ids, table, out):
    tokens = out.shape[0]
    adapters = table.shape[0]
    row_of = lax.broadcasted_iota(jnp.int32, (tokens, adapters), 0) // STEPS
    column = lax.broadcasted_iota(jnp.int32, (tokens, adapters), 1)
    chosen = pick(row_of, [ids[r] for r in range(tokens // STEPS)])
    out[...] = dot((chosen == column).astype(bf16), table[...])


def activate_kernel(parts, first, scales, *rest):
    front, back, out = rest[:parts], rest[parts : 2 * parts], rest[2 * parts]
    tokens, wide = scales.shape
    flat = out.reshape(tokens, wide)
    squares = sum(ref[:, 2 * first :].astype(f32) for ref in front)
    squares = jnp.sum(squares, axis=1, keepdims=True)
    inverse = lax.rsqrt(squares / D + 1e-05)
    for blocks, start, columns in ((front, 0, first), (back, first, wide - first)):
        gate = sum(ref[:, :columns].astype(f32) for ref in blocks) * inverse
        up = sum(ref[:, columns : 2 * columns].astype(f32) for ref in blocks) * inverse
        value = gate / (1.0 + jnp.exp(-gate)) * up * scales[:, start : start + columns]
        flat[:, start : start + columns] = value.astype(bf16)


def shifted(parts, axis):
    count = lax.axis_size(axis)
    return [parts[0]] + [
        lax.ppermute(parts[s], axis, [(i, target_of(i, s, count)) for i in range(count)])
        for s in range(1, count)
    ]


def shape_of(dims, dtype=bf16):
    return jax.ShapeDtypeStruct(dims, dtype)


def params(mib):
    return pltpu.CompilerParams(vmem_limit_bytes=mib << 20)


def cost(micros):
    return pl.CostEstimate(flops=micros * 10**9, bytes_accessed=0, transcendentals=0)


def per_device(
    queries,
    prefix_keys,
    prefix_values,
    suffix_keys,
    suffix_values,
    new_keys,
    new_values,
    hidden,
    adapter_ids,
    suffix_lengths,
    kv_scales,
    ffn_scales,
    out_weight,
    norm_gain,
    gate_up,
):
    rows = queries.shape[0]
    tokens = rows * STEPS
    kv_width = prefix_keys.shape[1]
    pre_count = lax.axis_size("pre")
    row_count = lax.axis_size("row")
    block = HEADS * HD // pre_count
    amount = hidden.shape[0] * STEPS
    out_cols = out_weight.shape[1]
    depth, _, wide = gate_up.shape

    ffn_rows = pl.pallas_call(
        scale_kernel,
        in_specs=[SMEM, VMEM],
        out_specs=VMEM,
        out_shape=shape_of((tokens, wide), f32),
        compiler_params=params(4),
    )(adapter_ids, ffn_scales)

    suffix_local = suffix_keys.shape[1]
    mask = pl.pallas_call(
        functools.partial(mask_kernel, tokens, suffix_local),
        in_specs=[SMEM],
        out_specs=VMEM,
        out_shape=shape_of((tokens, LANES), jnp.int32),
        compiler_params=params(1),
        cost_estimate=cost(20),
    )(suffix_lengths)
    partials = pl.pallas_call(
        functools.partial(attend_kernel, pre_count),
        in_specs=[SMEM] + [VMEM] * 9,
        out_specs=[VMEM] * pre_count,
        out_shape=[shape_of((tokens, block + LANES))] * pre_count,
        scratch_shapes=[
            pltpu.VMEM((tokens, kv_width), f32),
            pltpu.VMEM((pre_count, tokens, block + LANES), bf16),
        ],
        compiler_params=params(8),
        cost_estimate=cost(20),
    )(
        adapter_ids,
        mask,
        queries,
        prefix_keys,
        prefix_values,
        suffix_keys,
        suffix_values,
        new_keys,
        new_values,
        kv_scales,
    )
    mixed = pl.pallas_call(
        functools.partial(merge_kernel, pre_count),
        in_specs=[VMEM] * pre_count,
        out_specs=VMEM,
        out_shape=shape_of((tokens, block)),
        compiler_params=params(4),
        cost_estimate=cost(40),
    )(*shifted(partials, "pre"))
    gathered = shifted([mixed] * row_count, "row")
    products = pl.pallas_call(
        functools.partial(project_kernel, row_count, pre_count),
        in_specs=[VMEM] * (row_count + 1),
        out_specs=[VMEM] * pre_count,
        out_shape=[
            shape_of((amount, out_cols), bf16 if s else f32) for s in range(pre_count)
        ],
        scratch_shapes=[
            pltpu.VMEM((row_count * tokens, block), f32),
            pltpu.VMEM((row_count * tokens, out_cols), f32),
        ],
        compiler_params=params(8),
        cost_estimate=cost(40),
    )(*gathered, out_weight)
    residual, sent = pl.pallas_call(
        functools.partial(residual_kernel, pre_count),
        in_specs=[VMEM] * (pre_count + 1),
        out_specs=[VMEM] * 2,
        out_shape=[shape_of(hidden.shape), shape_of((amount, out_cols))],
        compiler_params=params(4),
        cost_estimate=cost(40),
    )(hidden, *shifted(products, "pre"))
    stacked = shifted([sent] * pre_count, "pre")
    total_rows = pre_count * amount
    half = row_count // 2
    first, second = split_columns(wide)
    sizes = (2 * first + LANES, 2 * second)
    *front, spread = pl.pallas_call(
        functools.partial(feed_first_kernel, pre_count, row_count, first),
        in_specs=[VMEM] * (pre_count + 2),
        out_specs=[VMEM] * 3,
        out_shape=[
            shape_of((half, tokens, sizes[0]), f32),
            shape_of((half, tokens, sizes[0])),
            shape_of((2 * total_rows, 2 * depth)),
        ],
        scratch_shapes=[
            pltpu.VMEM((total_rows, depth), f32),
            pltpu.VMEM((2 * total_rows, first + LANES), f32),
        ],
        compiler_params=params(8),
        cost_estimate=cost(16),
    )(norm_gain, *stacked, gate_up)
    back = pl.pallas_call(
        functools.partial(feed_second_kernel, row_count, first, second),
        in_specs=[VMEM] * 2,
        out_specs=[VMEM] * 2,
        out_shape=[
            shape_of((half, tokens, sizes[1]), f32),
            shape_of((half, tokens, sizes[1])),
        ],
        scratch_shapes=[pltpu.VMEM((2 * total_rows, second), f32)],
        compiler_params=pltpu.CompilerParams(
            vmem_limit_bytes=(8 << 20) + 2 * depth * (total_rows + 1)
        ),
        cost_estimate=cost(16),
    )(spread, gate_up)
    finals = []
    for extra, size, (keep, sent) in ((True, sizes[0], front), (False, sizes[1], back)):
        received = lax.ppermute(sent, "row", [(i, i ^ 1) for i in range(row_count)])
        sums = pl.pallas_call(
            functools.partial(pair_kernel, extra),
            in_specs=[VMEM] * 2,
            out_specs=[VMEM] * half,
            out_shape=[shape_of((tokens, size), bf16 if j else f32) for j in range(half)],
            compiler_params=params(4),
        )(keep, received)
        finals.append(sums[0])
        finals += [
            lax.ppermute(sums[j], "row", [(i, i ^ (2 * j)) for i in range(row_count)])
            for j in range(1, half)
        ]
    activation = pl.pallas_call(
        functools.partial(activate_kernel, half, first),
        in_specs=[VMEM] * (2 * half + 1),
        out_specs=VMEM,
        out_shape=shape_of((rows, STEPS, wide)),
        compiler_params=params(4),
    )(ffn_rows, *finals)
    return (residual, activation)


def solution(mesh):
    placed = (
        P(("grp", "row"), None, None),
        P(("grp", "pre"), None),
        P(("grp", "pre"), None),
        P(("grp", "row"), "pre", None),
        P(("grp", "row"), "pre", None),
        P(("grp", "row"), None, None),
        P(("grp", "row"), None, None),
        P(("grp", "pre"), None, "row"),
        P(("grp", "row")),
        P(("grp", "row")),
        P(),
        P(None, "pre"),
        P("pre", "row"),
        P("row"),
        P("row", None, "pre"),
    )
    return jax.shard_map(
        per_device,
        mesh=mesh,
        in_specs=placed,
        out_specs=(P(("grp", "pre"), None, "row"), P(("grp", "row"), None, "pre")),
        check_vma=False,
    )
```

```python
import functools

import jax
import jax.numpy as jnp
from jax import lax
from jax.experimental import pallas as pl
from jax.experimental.pallas import tpu as pltpu
from jax.sharding import PartitionSpec as P

D = 8192
HEADS = 64
KV_HEADS = 8
HD = 128
STEPS = 2
LANES = 128

masked_score = -1e30
f32 = jnp.float32
bf16 = jnp.bfloat16
VMEM = pl.BlockSpec(memory_space=pltpu.VMEM)
SMEM = pl.BlockSpec(memory_space=pltpu.SMEM)


def target_of(index, step, count):
    if count & (count - 1) == 0:
        return index ^ step
    return (index + step) % count


def source_of(index, step, count):
    if count & (count - 1) == 0:
        return index ^ step
    return lax.rem(index + count - step, count)


def dot(left, right):
    return jnp.dot(left, right, preferred_element_type=f32)


def dot_t(left, right):
    return lax.dot_general(left, right, (((1,), (1,)), ((), ())), preferred_element_type=f32)


def pick(index, scalars):
    value = jnp.full(index.shape, scalars[0], jnp.int32)
    for at in range(1, len(scalars)):
        value = jnp.where(index == at, scalars[at], value)
    return value


def three_parts(value):
    high = value.astype(bf16).astype(f32)
    rest = value - high
    middle = rest.astype(bf16).astype(f32)
    return high, middle, rest - middle


def mask_kernel(tokens, suffix_local, lengths, out):
    rows = tokens // STEPS
    suffix_all = rows * suffix_local
    me = lax.axis_index("pre")
    token = lax.broadcasted_iota(jnp.int32, out.shape, 0)
    column = lax.broadcasted_iota(jnp.int32, out.shape, 1)
    row_of = token // STEPS
    step = token - row_of * STEPS
    limit = pick(row_of, [lengths[r] for r in range(rows)])
    at = column - row_of * suffix_local
    in_suffix = (at >= 0) & (at < suffix_local) & (me * suffix_local + at < limit)
    fresh = column - suffix_all - row_of * STEPS
    in_new = (fresh >= 0) & (fresh <= step) & (me == 0)
    out[...] = (in_suffix | in_new).astype(jnp.int32)


def attend_kernel(
    pre_count,
    ids,
    mask,
    queries,
    prefix_keys,
    prefix_values,
    suffix_keys,
    suffix_values,
    new_keys,
    new_values,
    kv_scales,
    *rest,
):
    outs, (scales, stage) = rest[:pre_count], rest[pre_count:]
    rows = queries.shape[0]
    tokens = rows * STEPS
    suffix_local = suffix_keys.shape[1]
    width = suffix_keys.shape[2]
    suffix_all = rows * suffix_local
    group = HEADS // KV_HEADS
    block = HEADS * HD // pre_count
    block_heads = block // HD
    me = lax.axis_index("pre")
    allowed = jnp.concatenate([mask[...]] * group, axis=0) != 0
    for r in range(rows):
        scales[2 * r : 2 * r + 2, :] = kv_scales[ids[r]].astype(f32)

    query = queries[...].reshape(tokens, HEADS * HD).astype(f32)
    fill = jnp.zeros((LANES - suffix_all - tokens, width), f32)
    scale = scales[...]
    odd = lax.rem(lax.broadcasted_iota(jnp.int32, scale.shape, 0), 2) == 1
    key_scale = jnp.where(odd, pltpu.roll(scale, 1, 0), scale)
    value_scale = jnp.where(odd, scale, pltpu.roll(scale, tokens - 1, 0))
    fresh_key = new_keys[...].reshape(tokens, width).astype(f32) * key_scale
    fresh_value = new_values[...].reshape(tokens, width).astype(f32) * value_scale
    own_keys = jnp.concatenate(
        [
            suffix_keys[...].reshape(suffix_all, width),
            jnp.concatenate([fresh_key, fill], axis=0).astype(bf16),
        ],
        axis=0,
    )
    own_values = jnp.concatenate(
        [
            suffix_values[...].reshape(suffix_all, width),
            jnp.concatenate([fresh_value, fill], axis=0).astype(bf16),
        ],
        axis=0,
    )
    lane = lax.broadcasted_iota(jnp.int32, (tokens, LANES), 1)
    peaks = [jnp.zeros((tokens, LANES), f32) for _ in range(pre_count)]
    sums = [jnp.zeros((tokens, LANES), f32) for _ in range(pre_count)]
    for k in range(KV_HEADS):
        span = slice(k * HD, (k + 1) * HD)
        heads = [query[:, h * HD : (h + 1) * HD] for h in range(k * group, (k + 1) * group)]
        plain = jnp.concatenate(heads, axis=0).astype(bf16)
        scaled = jnp.concatenate([head * key_scale[:, span] for head in heads], axis=0).astype(bf16)
        prefix_scores = dot_t(scaled, prefix_keys[:, span]) * (HD**-0.5)
        own_scores = jnp.where(allowed, dot_t(plain, own_keys[:, span]) * (HD**-0.5), masked_score)
        peak = jnp.max(jnp.maximum(prefix_scores, own_scores), axis=1, keepdims=True)
        prefix_weight = jnp.exp(prefix_scores - peak).astype(bf16)
        own_weight = jnp.where(allowed, jnp.exp(own_scores - peak), 0.0).astype(bf16)
        total = jnp.sum(prefix_weight.astype(f32) + own_weight.astype(f32), axis=1, keepdims=True)
        from_prefix = dot(prefix_weight, prefix_values[:, span])
        from_own = dot(own_weight, own_values[:, span])
        for g in range(group):
            h = k * group + g
            at, j = h // block_heads, h % block_heads
            part = slice(g * tokens, (g + 1) * tokens)
            value = from_prefix[part] * value_scale[:, span] + from_own[part]
            stage[at, :, j * HD : (j + 1) * HD] = value.astype(bf16)
            peaks[at] = jnp.where(lane == j, peak[part], peaks[at])
            sums[at] = jnp.where(lane == j, total[part], sums[at])
    for at in range(pre_count):
        packed = jnp.zeros((tokens, LANES), f32)
        for place, piece in enumerate(three_parts(peaks[at]) + three_parts(sums[at])):
            packed = packed + (pltpu.roll(piece, place * block_heads, 1) if place else piece)
        stage[at, :, block:] = packed.astype(bf16)
    for s in range(pre_count):
        outs[s][...] = stage[target_of(me, s, pre_count)]


def merge_kernel(parts, *rest):
    blocks, out = rest[:parts], rest[parts]
    block = out.shape[1]
    block_heads = block // HD
    peaks, sums = [], []
    for ref in blocks:
        packed = ref[:, block:].astype(f32)
        pieces = [
            pltpu.roll(packed, LANES - place * block_heads, 1) if place else packed
            for place in range(6)
        ]
        peaks.append(pieces[0] + pieces[1] + pieces[2])
        sums.append(pieces[3] + pieces[4] + pieces[5])
    lane = lax.broadcasted_iota(jnp.int32, peaks[0].shape, 1)
    real = lane < block_heads
    highest = functools.reduce(jnp.maximum, peaks)
    factors = [jnp.where(real, jnp.exp(jnp.where(real, peak - highest, 0.0)), 0.0) for peak in peaks]
    total = sum(factor * amount for factor, amount in zip(factors, sums))
    total = jnp.where(real, total, 1.0)
    factors = [factor / total for factor in factors]
    for j in range(block_heads):
        span = slice(j * HD, (j + 1) * HD)
        value = sum(
            ref[:, span].astype(f32) * factor[:, j : j + 1] for ref, factor in zip(blocks, factors)
        )
        out[:, span] = value.astype(bf16)


def project_kernel(pre_count, stacked, weight, *rest):
    outs, product = rest[:pre_count], rest[pre_count]
    amount = outs[0].shape[0]
    pre_at = lax.axis_index("pre")
    product[...] = dot(stacked[...], weight[...])
    for s, out in enumerate(outs):
        start = pl.multiple_of(target_of(pre_at, s, pre_count) * amount, amount)
        out[...] = product[pl.ds(start, amount), :].astype(out.dtype)


def residual_kernel(parts, hidden, *rest):
    blocks, (out, sent) = rest[:parts], rest[parts:]
    amount, width = sent.shape
    value = sum(ref[...].astype(f32) for ref in blocks)
    value = hidden.reshape(amount, width)[...].astype(f32) + value
    sent[...] = value.astype(bf16)
    out.reshape(amount, width)[...] = value.astype(bf16)


def column_tile(columns):
    return next(size for size in (512, 256, 128) if columns % size == 0)


def split_columns(wide):
    unit = 512 if wide >= 1024 else LANES
    first = -(-(wide // 2) // unit) * unit
    return first, wide - first


def hand_out(row_count, product, columns, extra, keep, sent):
    rows = product.shape[0] // 2
    tokens = keep.shape[1]
    row_at = lax.axis_index("row")
    for j in range(row_count // 2):
        for at, out in ((row_at ^ (2 * j), keep), (row_at ^ (2 * j + 1), sent)):
            start = pl.multiple_of(at * tokens, tokens)
            own = pl.ds(start, tokens)
            out[j, :, :columns] = product[own, :columns].astype(out.dtype)
            out[j, :, columns : 2 * columns] = product[
                pl.ds(rows + start, tokens), :columns
            ].astype(out.dtype)
            if extra:
                out[j, :, 2 * columns :] = product[own, columns:].astype(out.dtype)


def multiply(left, weight, first, columns, product):
    depth, _, wide = weight.shape
    flat = weight.reshape(2 * depth, wide)
    tile = column_tile(columns)
    for start in range(0, columns, tile):
        product[:, start : start + tile] = dot(
            left, flat[:, first + start : first + start + tile]
        )


def placed_parts(value):
    lane = lax.broadcasted_iota(jnp.int32, (value.shape[0], LANES), 1)
    pieces = three_parts(value)
    return sum(jnp.where(lane == place, piece, 0.0) for place, piece in enumerate(pieces))


def feed_first_kernel(pre_count, row_count, columns, gain, *rest):
    blocks, weight = rest[:pre_count], rest[pre_count]
    keep, sent, spread, stacked, product = rest[pre_count + 1 :]
    amount, depth = blocks[0].shape
    rows = pre_count * amount
    pre_at = lax.axis_index("pre")
    for s, ref in enumerate(blocks):
        start = pl.multiple_of(source_of(pre_at, s, pre_count) * amount, amount)
        stacked[pl.ds(start, amount), :] = ref[...].astype(f32)
    value = stacked[...]
    squares = jnp.sum(value * value, axis=1, keepdims=True)
    normed = (value * gain[...].astype(f32).reshape(1, depth)).astype(bf16)
    source = lax.broadcasted_iota(jnp.int32, (HD, 2 * HD), 0)
    target = lax.broadcasted_iota(jnp.int32, (HD, 2 * HD), 1)
    pieces = jnp.concatenate(
        [normed[:, b * HD : (b + 1) * HD] for b in range(depth // HD)], axis=0
    )
    for half in range(2):
        selector = (target == 2 * source + half).astype(bf16)
        wider = dot(pieces, selector).astype(bf16)
        for b in range(depth // HD):
            spread[half * rows : (half + 1) * rows, 2 * b * HD : 2 * (b + 1) * HD] = wider[
                b * rows : (b + 1) * rows
            ]
    multiply(spread[...], weight, 0, columns, product)
    product[0:rows, columns:] = placed_parts(squares)
    hand_out(row_count, product, columns, True, keep, sent)


def feed_second_kernel(row_count, first, columns, spread, weight, keep, sent, product):
    multiply(spread[...], weight, first, columns, product)
    hand_out(row_count, product, columns, False, keep, sent)


def pair_kernel(extra, keep, received, *outs):
    for j, out in enumerate(outs):
        value = keep[j] + received[j].astype(f32)
        if extra:
            edge = value.shape[1] - LANES
            out[:, :edge] = value[:, :edge].astype(out.dtype)
            total = jnp.sum(value[:, edge:], axis=1, keepdims=True)
            out[:, edge:] = placed_parts(total).astype(out.dtype)
        else:
            out[...] = value.astype(out.dtype)


def scale_kernel(ids, table, out):
    tokens = out.shape[0]
    adapters = table.shape[0]
    row_of = lax.broadcasted_iota(jnp.int32, (tokens, adapters), 0) // STEPS
    column = lax.broadcasted_iota(jnp.int32, (tokens, adapters), 1)
    chosen = pick(row_of, [ids[r] for r in range(tokens // STEPS)])
    out[...] = dot((chosen == column).astype(bf16), table[...])


def activate_kernel(parts, first, scales, *rest):
    front, back, out = rest[:parts], rest[parts : 2 * parts], rest[2 * parts]
    tokens, wide = scales.shape
    flat = out.reshape(tokens, wide)
    squares = sum(ref[:, 2 * first :].astype(f32) for ref in front)
    squares = jnp.sum(squares, axis=1, keepdims=True)
    inverse = lax.rsqrt(squares / D + 1e-05)
    for blocks, start, columns in ((front, 0, first), (back, first, wide - first)):
        gate = sum(ref[:, :columns].astype(f32) for ref in blocks) * inverse
        up = sum(ref[:, columns : 2 * columns].astype(f32) for ref in blocks) * inverse
        value = gate / (1.0 + jnp.exp(-gate)) * up * scales[:, start : start + columns]
        flat[:, start : start + columns] = value.astype(bf16)


def shifted(parts, axis):
    count = lax.axis_size(axis)
    return [parts[0]] + [
        lax.ppermute(parts[s], axis, [(i, target_of(i, s, count)) for i in range(count)])
        for s in range(1, count)
    ]


def shape_of(dims, dtype=bf16):
    return jax.ShapeDtypeStruct(dims, dtype)


def params(mib):
    return pltpu.CompilerParams(vmem_limit_bytes=mib << 20)


def cost(micros):
    return pl.CostEstimate(flops=micros * 10**9, bytes_accessed=0, transcendentals=0)


def per_device(
    queries,
    prefix_keys,
    prefix_values,
    suffix_keys,
    suffix_values,
    new_keys,
    new_values,
    hidden,
    adapter_ids,
    suffix_lengths,
    kv_scales,
    ffn_scales,
    out_weight,
    norm_gain,
    gate_up,
):
    rows = queries.shape[0]
    tokens = rows * STEPS
    kv_width = prefix_keys.shape[1]
    pre_count = lax.axis_size("pre")
    row_count = lax.axis_size("row")
    block = HEADS * HD // pre_count
    amount = hidden.shape[0] * STEPS
    out_cols = out_weight.shape[1]
    depth, _, wide = gate_up.shape

    ffn_rows = pl.pallas_call(
        scale_kernel,
        in_specs=[SMEM, VMEM],
        out_specs=VMEM,
        out_shape=shape_of((tokens, wide), f32),
        compiler_params=params(4),
    )(adapter_ids, ffn_scales)

    suffix_local = suffix_keys.shape[1]
    mask = pl.pallas_call(
        functools.partial(mask_kernel, tokens, suffix_local),
        in_specs=[SMEM],
        out_specs=VMEM,
        out_shape=shape_of((tokens, LANES), jnp.int32),
        compiler_params=params(1),
        cost_estimate=cost(20),
    )(suffix_lengths)
    partials = pl.pallas_call(
        functools.partial(attend_kernel, pre_count),
        in_specs=[SMEM] + [VMEM] * 9,
        out_specs=[VMEM] * pre_count,
        out_shape=[shape_of((tokens, block + LANES))] * pre_count,
        scratch_shapes=[
            pltpu.VMEM((tokens, kv_width), f32),
            pltpu.VMEM((pre_count, tokens, block + LANES), bf16),
        ],
        compiler_params=params(8),
        cost_estimate=cost(20),
    )(
        adapter_ids,
        mask,
        queries,
        prefix_keys,
        prefix_values,
        suffix_keys,
        suffix_values,
        new_keys,
        new_values,
        kv_scales,
    )
    mixed = pl.pallas_call(
        functools.partial(merge_kernel, pre_count),
        in_specs=[VMEM] * pre_count,
        out_specs=VMEM,
        out_shape=shape_of((tokens, block)),
        compiler_params=params(4),
        cost_estimate=cost(40),
    )(*shifted(partials, "pre"))
    gathered = lax.all_gather(mixed, "row", axis=0, tiled=True)
    products = pl.pallas_call(
        functools.partial(project_kernel, pre_count),
        in_specs=[VMEM] * 2,
        out_specs=[VMEM] * pre_count,
        out_shape=[
            shape_of((amount, out_cols), bf16 if s else f32) for s in range(pre_count)
        ],
        scratch_shapes=[
            pltpu.VMEM((row_count * tokens, out_cols), f32),
        ],
        compiler_params=params(8),
        cost_estimate=cost(40),
    )(gathered, out_weight)
    residual, sent = pl.pallas_call(
        functools.partial(residual_kernel, pre_count),
        in_specs=[VMEM] * (pre_count + 1),
        out_specs=[VMEM] * 2,
        out_shape=[shape_of(hidden.shape), shape_of((amount, out_cols))],
        compiler_params=params(4),
        cost_estimate=cost(40),
    )(hidden, *shifted(products, "pre"))
    stacked = shifted([sent] * pre_count, "pre")
    total_rows = pre_count * amount
    half = row_count // 2
    first, second = split_columns(wide)
    sizes = (2 * first + LANES, 2 * second)
    *front, spread = pl.pallas_call(
        functools.partial(feed_first_kernel, pre_count, row_count, first),
        in_specs=[VMEM] * (pre_count + 2),
        out_specs=[VMEM] * 3,
        out_shape=[
            shape_of((half, tokens, sizes[0]), f32),
            shape_of((half, tokens, sizes[0])),
            shape_of((2 * total_rows, 2 * depth)),
        ],
        scratch_shapes=[
            pltpu.VMEM((total_rows, depth), f32),
            pltpu.VMEM((2 * total_rows, first + LANES), f32),
        ],
        compiler_params=params(8),
        cost_estimate=cost(16),
    )(norm_gain, *stacked, gate_up)
    back = pl.pallas_call(
        functools.partial(feed_second_kernel, row_count, first, second),
        in_specs=[VMEM] * 2,
        out_specs=[VMEM] * 2,
        out_shape=[
            shape_of((half, tokens, sizes[1]), f32),
            shape_of((half, tokens, sizes[1])),
        ],
        scratch_shapes=[pltpu.VMEM((2 * total_rows, second), f32)],
        compiler_params=pltpu.CompilerParams(
            vmem_limit_bytes=(8 << 20) + 2 * depth * (total_rows + 1)
        ),
        cost_estimate=cost(16),
    )(spread, gate_up)
    finals = []
    for extra, size, (keep, sent) in ((True, sizes[0], front), (False, sizes[1], back)):
        received = lax.ppermute(sent, "row", [(i, i ^ 1) for i in range(row_count)])
        sums = pl.pallas_call(
            functools.partial(pair_kernel, extra),
            in_specs=[VMEM] * 2,
            out_specs=[VMEM] * half,
            out_shape=[shape_of((tokens, size), bf16 if j else f32) for j in range(half)],
            compiler_params=params(4),
        )(keep, received)
        finals.append(sums[0])
        finals += [
            lax.ppermute(sums[j], "row", [(i, i ^ (2 * j)) for i in range(row_count)])
            for j in range(1, half)
        ]
    activation = pl.pallas_call(
        functools.partial(activate_kernel, half, first),
        in_specs=[VMEM] * (2 * half + 1),
        out_specs=VMEM,
        out_shape=shape_of((rows, STEPS, wide)),
        compiler_params=params(4),
    )(ffn_rows, *finals)
    return (residual, activation)


def solution(mesh):
    placed = (
        P(("grp", "row"), None, None),
        P(("grp", "pre"), None),
        P(("grp", "pre"), None),
        P(("grp", "row"), "pre", None),
        P(("grp", "row"), "pre", None),
        P(("grp", "row"), None, None),
        P(("grp", "row"), None, None),
        P(("grp", "pre"), None, "row"),
        P(("grp", "row")),
        P(("grp", "row")),
        P(),
        P(None, "pre"),
        P("pre", "row"),
        P("row"),
        P("row", None, "pre"),
    )
    return jax.shard_map(
        per_device,
        mesh=mesh,
        in_specs=placed,
        out_specs=(P(("grp", "pre"), None, "row"), P(("grp", "row"), None, "pre")),
        check_vma=False,
    )
```

```python
import functools

import jax
import jax.numpy as jnp
from jax import lax
from jax.experimental import pallas as pl
from jax.experimental.pallas import tpu as pltpu
from jax.sharding import PartitionSpec as P

D = 8192
HEADS = 64
KV_HEADS = 8
HD = 128
STEPS = 2
LANES = 128

masked_score = -1e30
f32 = jnp.float32
bf16 = jnp.bfloat16
VMEM = pl.BlockSpec(memory_space=pltpu.VMEM)
SMEM = pl.BlockSpec(memory_space=pltpu.SMEM)


def target_of(index, step, count):
    if count & (count - 1) == 0:
        return index ^ step
    return (index + step) % count


def source_of(index, step, count):
    if count & (count - 1) == 0:
        return index ^ step
    return lax.rem(index + count - step, count)


def dot(left, right):
    return jnp.dot(left, right, preferred_element_type=f32)


def dot_t(left, right):
    return lax.dot_general(left, right, (((1,), (1,)), ((), ())), preferred_element_type=f32)


def pick(index, scalars):
    value = jnp.full(index.shape, scalars[0], jnp.int32)
    for at in range(1, len(scalars)):
        value = jnp.where(index == at, scalars[at], value)
    return value


def three_parts(value):
    high = value.astype(bf16).astype(f32)
    rest = value - high
    middle = rest.astype(bf16).astype(f32)
    return high, middle, rest - middle


def mask_kernel(tokens, suffix_local, lengths, out):
    rows = tokens // STEPS
    suffix_all = rows * suffix_local
    me = lax.axis_index("pre")
    token = lax.broadcasted_iota(jnp.int32, out.shape, 0)
    column = lax.broadcasted_iota(jnp.int32, out.shape, 1)
    row_of = token // STEPS
    step = token - row_of * STEPS
    limit = pick(row_of, [lengths[r] for r in range(rows)])
    at = column - row_of * suffix_local
    in_suffix = (at >= 0) & (at < suffix_local) & (me * suffix_local + at < limit)
    fresh = column - suffix_all - row_of * STEPS
    in_new = (fresh >= 0) & (fresh <= step) & (me == 0)
    out[...] = (in_suffix | in_new).astype(jnp.int32)


def attend_kernel(
    pre_count,
    ids,
    mask,
    queries,
    prefix_keys,
    prefix_values,
    suffix_keys,
    suffix_values,
    new_keys,
    new_values,
    kv_scales,
    *rest,
):
    outs, (scales, stage) = rest[:pre_count], rest[pre_count:]
    rows = queries.shape[0]
    tokens = rows * STEPS
    suffix_local = suffix_keys.shape[1]
    width = suffix_keys.shape[2]
    suffix_all = rows * suffix_local
    group = HEADS // KV_HEADS
    block = HEADS * HD // pre_count
    block_heads = block // HD
    me = lax.axis_index("pre")
    allowed = jnp.concatenate([mask[...]] * group, axis=0) != 0
    for r in range(rows):
        scales[2 * r : 2 * r + 2, :] = kv_scales[ids[r]].astype(f32)

    query = queries[...].reshape(tokens, HEADS * HD).astype(f32)
    fill = jnp.zeros((LANES - suffix_all - tokens, width), f32)
    scale = scales[...]
    odd = lax.rem(lax.broadcasted_iota(jnp.int32, scale.shape, 0), 2) == 1
    key_scale = jnp.where(odd, pltpu.roll(scale, 1, 0), scale)
    value_scale = jnp.where(odd, scale, pltpu.roll(scale, tokens - 1, 0))
    fresh_key = new_keys[...].reshape(tokens, width).astype(f32) * key_scale
    fresh_value = new_values[...].reshape(tokens, width).astype(f32) * value_scale
    own_keys = jnp.concatenate(
        [
            suffix_keys[...].reshape(suffix_all, width),
            jnp.concatenate([fresh_key, fill], axis=0).astype(bf16),
        ],
        axis=0,
    )
    own_values = jnp.concatenate(
        [
            suffix_values[...].reshape(suffix_all, width),
            jnp.concatenate([fresh_value, fill], axis=0).astype(bf16),
        ],
        axis=0,
    )
    lane = lax.broadcasted_iota(jnp.int32, (tokens, LANES), 1)
    peaks = [jnp.zeros((tokens, LANES), f32) for _ in range(pre_count)]
    sums = [jnp.zeros((tokens, LANES), f32) for _ in range(pre_count)]
    for k in range(KV_HEADS):
        span = slice(k * HD, (k + 1) * HD)
        heads = [query[:, h * HD : (h + 1) * HD] for h in range(k * group, (k + 1) * group)]
        plain = jnp.concatenate(heads, axis=0).astype(bf16)
        scaled = jnp.concatenate([head * key_scale[:, span] for head in heads], axis=0).astype(bf16)
        prefix_scores = dot_t(scaled, prefix_keys[:, span]) * (HD**-0.5)
        own_scores = jnp.where(allowed, dot_t(plain, own_keys[:, span]) * (HD**-0.5), masked_score)
        peak = jnp.max(jnp.maximum(prefix_scores, own_scores), axis=1, keepdims=True)
        prefix_weight = jnp.exp(prefix_scores - peak).astype(bf16)
        own_weight = jnp.where(allowed, jnp.exp(own_scores - peak), 0.0).astype(bf16)
        total = jnp.sum(prefix_weight.astype(f32) + own_weight.astype(f32), axis=1, keepdims=True)
        from_prefix = dot(prefix_weight, prefix_values[:, span])
        from_own = dot(own_weight, own_values[:, span])
        for g in range(group):
            h = k * group + g
            at, j = h // block_heads, h % block_heads
            part = slice(g * tokens, (g + 1) * tokens)
            value = from_prefix[part] * value_scale[:, span] + from_own[part]
            stage[at, :, j * HD : (j + 1) * HD] = value.astype(bf16)
            peaks[at] = jnp.where(lane == j, peak[part], peaks[at])
            sums[at] = jnp.where(lane == j, total[part], sums[at])
    for at in range(pre_count):
        packed = jnp.zeros((tokens, LANES), f32)
        for place, piece in enumerate(three_parts(peaks[at]) + three_parts(sums[at])):
            packed = packed + (pltpu.roll(piece, place * block_heads, 1) if place else piece)
        stage[at, :, block:] = packed.astype(bf16)
    for s in range(pre_count):
        outs[s][...] = stage[lax.rem(me + s, pre_count)]


def merge_kernel(parts, *rest):
    blocks, out = rest[:parts], rest[parts]
    block = out.shape[1]
    block_heads = block // HD
    peaks, sums = [], []
    for ref in blocks:
        packed = ref[:, block:].astype(f32)
        pieces = [
            pltpu.roll(packed, LANES - place * block_heads, 1) if place else packed
            for place in range(6)
        ]
        peaks.append(pieces[0] + pieces[1] + pieces[2])
        sums.append(pieces[3] + pieces[4] + pieces[5])
    lane = lax.broadcasted_iota(jnp.int32, peaks[0].shape, 1)
    real = lane < block_heads
    highest = functools.reduce(jnp.maximum, peaks)
    factors = [jnp.where(real, jnp.exp(jnp.where(real, peak - highest, 0.0)), 0.0) for peak in peaks]
    total = sum(factor * amount for factor, amount in zip(factors, sums))
    total = jnp.where(real, total, 1.0)
    factors = [factor / total for factor in factors]
    for j in range(block_heads):
        span = slice(j * HD, (j + 1) * HD)
        value = sum(
            ref[:, span].astype(f32) * factor[:, j : j + 1] for ref, factor in zip(blocks, factors)
        )
        out[:, span] = value.astype(bf16)


def project_kernel(row_count, pre_count, *rest):
    blocks, weight = rest[:row_count], rest[row_count]
    outs = rest[row_count + 1 : row_count + 1 + pre_count]
    stacked, product = rest[row_count + 1 + pre_count :]
    tokens = blocks[0].shape[0]
    amount = outs[0].shape[0]
    pre_at, row_at = lax.axis_index("pre"), lax.axis_index("row")
    for s, ref in enumerate(blocks):
        start = pl.multiple_of(source_of(row_at, s, row_count) * tokens, tokens)
        stacked[pl.ds(start, tokens), :] = ref[...].astype(f32)
    product[...] = dot(stacked[...].astype(bf16), weight[...])
    for s, out in enumerate(outs):
        start = pl.multiple_of(target_of(pre_at, s, pre_count) * amount, amount)
        out[...] = product[pl.ds(start, amount), :].astype(out.dtype)


def residual_kernel(parts, hidden, *rest):
    blocks, (out, sent) = rest[:parts], rest[parts:]
    amount, width = sent.shape
    value = sum(ref[...].astype(f32) for ref in blocks)
    value = hidden.reshape(amount, width)[...].astype(f32) + value
    sent[...] = value.astype(bf16)
    out.reshape(amount, width)[...] = value.astype(bf16)


def column_tile(columns):
    return next(size for size in (512, 256, 128) if columns % size == 0)


def split_columns(wide):
    unit = 512 if wide >= 1024 else LANES
    first = -(-(wide // 2) // unit) * unit
    return first, wide - first


def hand_out(row_count, product, columns, extra, keep, sent):
    rows = product.shape[0] // 2
    tokens = keep.shape[1]
    row_at = lax.axis_index("row")
    for j in range(row_count // 2):
        for at, out in ((row_at ^ (2 * j), keep), (row_at ^ (2 * j + 1), sent)):
            start = pl.multiple_of(at * tokens, tokens)
            own = pl.ds(start, tokens)
            out[j, :, :columns] = product[own, :columns].astype(out.dtype)
            out[j, :, columns : 2 * columns] = product[
                pl.ds(rows + start, tokens), :columns
            ].astype(out.dtype)
            if extra:
                out[j, :, 2 * columns :] = product[own, columns:].astype(out.dtype)


def multiply(left, weight, first, columns, product):
    depth, _, wide = weight.shape
    flat = weight.reshape(2 * depth, wide)
    tile = column_tile(columns)
    for start in range(0, columns, tile):
        product[:, start : start + tile] = dot(
            left, flat[:, first + start : first + start + tile]
        )


def placed_parts(value):
    lane = lax.broadcasted_iota(jnp.int32, (value.shape[0], LANES), 1)
    pieces = three_parts(value)
    return sum(jnp.where(lane == place, piece, 0.0) for place, piece in enumerate(pieces))


def feed_first_kernel(pre_count, row_count, columns, gain, *rest):
    blocks, weight = rest[:pre_count], rest[pre_count]
    keep, sent, spread, stacked, product = rest[pre_count + 1 :]
    amount, depth = blocks[0].shape
    rows = pre_count * amount
    pre_at = lax.axis_index("pre")
    for s, ref in enumerate(blocks):
        start = pl.multiple_of(source_of(pre_at, s, pre_count) * amount, amount)
        stacked[pl.ds(start, amount), :] = ref[...].astype(f32)
    value = stacked[...]
    squares = jnp.sum(value * value, axis=1, keepdims=True)
    normed = (value * gain[...].astype(f32).reshape(1, depth)).astype(bf16)
    source = lax.broadcasted_iota(jnp.int32, (HD, 2 * HD), 0)
    target = lax.broadcasted_iota(jnp.int32, (HD, 2 * HD), 1)
    pieces = jnp.concatenate(
        [normed[:, b * HD : (b + 1) * HD] for b in range(depth // HD)], axis=0
    )
    for half in range(2):
        selector = (target == 2 * source + half).astype(bf16)
        wider = dot(pieces, selector).astype(bf16)
        for b in range(depth // HD):
            spread[half * rows : (half + 1) * rows, 2 * b * HD : 2 * (b + 1) * HD] = wider[
                b * rows : (b + 1) * rows
            ]
    multiply(spread[...], weight, 0, columns, product)
    product[0:rows, columns:] = placed_parts(squares)
    hand_out(row_count, product, columns, True, keep, sent)


def feed_second_kernel(row_count, first, columns, spread, weight, keep, sent, product):
    multiply(spread[...], weight, first, columns, product)
    hand_out(row_count, product, columns, False, keep, sent)


def pair_kernel(extra, keep, received, *outs):
    for j, out in enumerate(outs):
        value = keep[j] + received[j].astype(f32)
        if extra:
            edge = value.shape[1] - LANES
            out[:, :edge] = value[:, :edge].astype(out.dtype)
            total = jnp.sum(value[:, edge:], axis=1, keepdims=True)
            out[:, edge:] = placed_parts(total).astype(out.dtype)
        else:
            out[...] = value.astype(out.dtype)


def scale_kernel(ids, table, out):
    tokens = out.shape[0]
    adapters = table.shape[0]
    row_of = lax.broadcasted_iota(jnp.int32, (tokens, adapters), 0) // STEPS
    column = lax.broadcasted_iota(jnp.int32, (tokens, adapters), 1)
    chosen = pick(row_of, [ids[r] for r in range(tokens // STEPS)])
    out[...] = dot((chosen == column).astype(bf16), table[...])


def activate_kernel(parts, first, scales, *rest):
    front, back, out = rest[:parts], rest[parts : 2 * parts], rest[2 * parts]
    tokens, wide = scales.shape
    flat = out.reshape(tokens, wide)
    squares = sum(ref[:, 2 * first :].astype(f32) for ref in front)
    squares = jnp.sum(squares, axis=1, keepdims=True)
    inverse = lax.rsqrt(squares / D + 1e-05)
    for blocks, start, columns in ((front, 0, first), (back, first, wide - first)):
        gate = sum(ref[:, :columns].astype(f32) for ref in blocks) * inverse
        up = sum(ref[:, columns : 2 * columns].astype(f32) for ref in blocks) * inverse
        value = gate / (1.0 + jnp.exp(-gate)) * up * scales[:, start : start + columns]
        flat[:, start : start + columns] = value.astype(bf16)


def shifted(parts, axis):
    count = lax.axis_size(axis)
    return [parts[0]] + [
        lax.ppermute(parts[s], axis, [(i, target_of(i, s, count)) for i in range(count)])
        for s in range(1, count)
    ]


def shape_of(dims, dtype=bf16):
    return jax.ShapeDtypeStruct(dims, dtype)


def params(mib):
    return pltpu.CompilerParams(vmem_limit_bytes=mib << 20)


def cost(micros):
    return pl.CostEstimate(flops=micros * 10**9, bytes_accessed=0, transcendentals=0)


def per_device(
    queries,
    prefix_keys,
    prefix_values,
    suffix_keys,
    suffix_values,
    new_keys,
    new_values,
    hidden,
    adapter_ids,
    suffix_lengths,
    kv_scales,
    ffn_scales,
    out_weight,
    norm_gain,
    gate_up,
):
    rows = queries.shape[0]
    tokens = rows * STEPS
    kv_width = prefix_keys.shape[1]
    pre_count = lax.axis_size("pre")
    row_count = lax.axis_size("row")
    block = HEADS * HD // pre_count
    amount = hidden.shape[0] * STEPS
    out_cols = out_weight.shape[1]
    depth, _, wide = gate_up.shape

    ffn_rows = pl.pallas_call(
        scale_kernel,
        in_specs=[SMEM, VMEM],
        out_specs=VMEM,
        out_shape=shape_of((tokens, wide), f32),
        compiler_params=params(4),
    )(adapter_ids, ffn_scales)

    suffix_local = suffix_keys.shape[1]
    mask = pl.pallas_call(
        functools.partial(mask_kernel, tokens, suffix_local),
        in_specs=[SMEM],
        out_specs=VMEM,
        out_shape=shape_of((tokens, LANES), jnp.int32),
        compiler_params=params(1),
        cost_estimate=cost(20),
    )(suffix_lengths)
    partials = pl.pallas_call(
        functools.partial(attend_kernel, pre_count),
        in_specs=[SMEM] + [VMEM] * 9,
        out_specs=[VMEM] * pre_count,
        out_shape=[shape_of((tokens, block + LANES))] * pre_count,
        scratch_shapes=[
            pltpu.VMEM((tokens, kv_width), f32),
            pltpu.VMEM((pre_count, tokens, block + LANES), bf16),
        ],
        compiler_params=params(8),
        cost_estimate=cost(20),
    )(
        adapter_ids,
        mask,
        queries,
        prefix_keys,
        prefix_values,
        suffix_keys,
        suffix_values,
        new_keys,
        new_values,
        kv_scales,
    )
    ring = [partials[0]] + [
        lax.ppermute(partials[s], "pre", [(i, (i + s) % pre_count) for i in range(pre_count)])
        for s in range(1, pre_count)
    ]
    mixed = pl.pallas_call(
        functools.partial(merge_kernel, pre_count),
        in_specs=[VMEM] * pre_count,
        out_specs=VMEM,
        out_shape=shape_of((tokens, block)),
        compiler_params=params(4),
        cost_estimate=cost(40),
    )(*ring)
    gathered = shifted([mixed] * row_count, "row")
    products = pl.pallas_call(
        functools.partial(project_kernel, row_count, pre_count),
        in_specs=[VMEM] * (row_count + 1),
        out_specs=[VMEM] * pre_count,
        out_shape=[
            shape_of((amount, out_cols), bf16 if s else f32) for s in range(pre_count)
        ],
        scratch_shapes=[
            pltpu.VMEM((row_count * tokens, block), f32),
            pltpu.VMEM((row_count * tokens, out_cols), f32),
        ],
        compiler_params=params(8),
        cost_estimate=cost(40),
    )(*gathered, out_weight)
    residual, sent = pl.pallas_call(
        functools.partial(residual_kernel, pre_count),
        in_specs=[VMEM] * (pre_count + 1),
        out_specs=[VMEM] * 2,
        out_shape=[shape_of(hidden.shape), shape_of((amount, out_cols))],
        compiler_params=params(4),
        cost_estimate=cost(40),
    )(hidden, *shifted(products, "pre"))
    stacked = shifted([sent] * pre_count, "pre")
    total_rows = pre_count * amount
    half = row_count // 2
    first, second = split_columns(wide)
    sizes = (2 * first + LANES, 2 * second)
    *front, spread = pl.pallas_call(
        functools.partial(feed_first_kernel, pre_count, row_count, first),
        in_specs=[VMEM] * (pre_count + 2),
        out_specs=[VMEM] * 3,
        out_shape=[
            shape_of((half, tokens, sizes[0]), f32),
            shape_of((half, tokens, sizes[0])),
            shape_of((2 * total_rows, 2 * depth)),
        ],
        scratch_shapes=[
            pltpu.VMEM((total_rows, depth), f32),
            pltpu.VMEM((2 * total_rows, first + LANES), f32),
        ],
        compiler_params=params(8),
        cost_estimate=cost(16),
    )(norm_gain, *stacked, gate_up)
    back = pl.pallas_call(
        functools.partial(feed_second_kernel, row_count, first, second),
        in_specs=[VMEM] * 2,
        out_specs=[VMEM] * 2,
        out_shape=[
            shape_of((half, tokens, sizes[1]), f32),
            shape_of((half, tokens, sizes[1])),
        ],
        scratch_shapes=[pltpu.VMEM((2 * total_rows, second), f32)],
        compiler_params=pltpu.CompilerParams(
            vmem_limit_bytes=(8 << 20) + 2 * depth * (total_rows + 1)
        ),
        cost_estimate=cost(16),
    )(spread, gate_up)
    finals = []
    for extra, size, (keep, sent) in ((True, sizes[0], front), (False, sizes[1], back)):
        received = lax.ppermute(sent, "row", [(i, i ^ 1) for i in range(row_count)])
        sums = pl.pallas_call(
            functools.partial(pair_kernel, extra),
            in_specs=[VMEM] * 2,
            out_specs=[VMEM] * half,
            out_shape=[shape_of((tokens, size), bf16 if j else f32) for j in range(half)],
            compiler_params=params(4),
        )(keep, received)
        finals.append(sums[0])
        finals += [
            lax.ppermute(sums[j], "row", [(i, i ^ (2 * j)) for i in range(row_count)])
            for j in range(1, half)
        ]
    activation = pl.pallas_call(
        functools.partial(activate_kernel, half, first),
        in_specs=[VMEM] * (2 * half + 1),
        out_specs=VMEM,
        out_shape=shape_of((rows, STEPS, wide)),
        compiler_params=params(4),
    )(ffn_rows, *finals)
    return (residual, activation)


def solution(mesh):
    placed = (
        P(("grp", "row"), None, None),
        P(("grp", "pre"), None),
        P(("grp", "pre"), None),
        P(("grp", "row"), "pre", None),
        P(("grp", "row"), "pre", None),
        P(("grp", "row"), None, None),
        P(("grp", "row"), None, None),
        P(("grp", "pre"), None, "row"),
        P(("grp", "row")),
        P(("grp", "row")),
        P(),
        P(None, "pre"),
        P("pre", "row"),
        P("row"),
        P("row", None, "pre"),
    )
    return jax.shard_map(
        per_device,
        mesh=mesh,
        in_specs=placed,
        out_specs=(P(("grp", "pre"), None, "row"), P(("grp", "row"), None, "pre")),
        check_vma=False,
    )
```

```python
import functools

import jax
import jax.numpy as jnp
from jax import lax
from jax.experimental import pallas as pl
from jax.experimental.pallas import tpu as pltpu
from jax.sharding import PartitionSpec as P

D = 8192
HEADS = 64
KV_HEADS = 8
HD = 128
STEPS = 2
LANES = 128

masked_score = -1e30
f32 = jnp.float32
bf16 = jnp.bfloat16
VMEM = pl.BlockSpec(memory_space=pltpu.VMEM)
SMEM = pl.BlockSpec(memory_space=pltpu.SMEM)


def target_of(index, step, count):
    if count & (count - 1) == 0:
        return index ^ step
    return (index + step) % count


def source_of(index, step, count):
    if count & (count - 1) == 0:
        return index ^ step
    return lax.rem(index + count - step, count)


def dot(left, right):
    return jnp.dot(left, right, preferred_element_type=f32)


def dot_t(left, right):
    return lax.dot_general(left, right, (((1,), (1,)), ((), ())), preferred_element_type=f32)


def pick(index, scalars):
    value = jnp.full(index.shape, scalars[0], jnp.int32)
    for at in range(1, len(scalars)):
        value = jnp.where(index == at, scalars[at], value)
    return value


def three_parts(value):
    high = value.astype(bf16).astype(f32)
    rest = value - high
    middle = rest.astype(bf16).astype(f32)
    return high, middle, rest - middle


def mask_kernel(tokens, suffix_local, lengths, out):
    rows = tokens // STEPS
    suffix_all = rows * suffix_local
    me = lax.axis_index("pre")
    token = lax.broadcasted_iota(jnp.int32, out.shape, 0)
    column = lax.broadcasted_iota(jnp.int32, out.shape, 1)
    row_of = token // STEPS
    step = token - row_of * STEPS
    limit = pick(row_of, [lengths[r] for r in range(rows)])
    at = column - row_of * suffix_local
    in_suffix = (at >= 0) & (at < suffix_local) & (me * suffix_local + at < limit)
    fresh = column - suffix_all - row_of * STEPS
    in_new = (fresh >= 0) & (fresh <= step) & (me == 0)
    out[...] = (in_suffix | in_new).astype(jnp.int32)


def attend_kernel(
    pre_count,
    ids,
    mask,
    queries,
    prefix_keys,
    prefix_values,
    suffix_keys,
    suffix_values,
    new_keys,
    new_values,
    kv_scales,
    *rest,
):
    outs, (scales, stage) = rest[:pre_count], rest[pre_count:]
    rows = queries.shape[0]
    tokens = rows * STEPS
    suffix_local = suffix_keys.shape[1]
    width = suffix_keys.shape[2]
    suffix_all = rows * suffix_local
    group = HEADS // KV_HEADS
    block = HEADS * HD // pre_count
    block_heads = block // HD
    me = lax.axis_index("pre")
    allowed = jnp.concatenate([mask[...]] * group, axis=0) != 0
    for r in range(rows):
        scales[2 * r : 2 * r + 2, :] = kv_scales[ids[r]].astype(f32)

    query = queries[...].reshape(tokens, HEADS * HD).astype(f32)
    fill = jnp.zeros((LANES - suffix_all - tokens, width), f32)
    scale = scales[...]
    odd = lax.rem(lax.broadcasted_iota(jnp.int32, scale.shape, 0), 2) == 1
    key_scale = jnp.where(odd, pltpu.roll(scale, 1, 0), scale)
    value_scale = jnp.where(odd, scale, pltpu.roll(scale, tokens - 1, 0))
    fresh_key = new_keys[...].reshape(tokens, width).astype(f32) * key_scale
    fresh_value = new_values[...].reshape(tokens, width).astype(f32) * value_scale
    own_keys = jnp.concatenate(
        [
            suffix_keys[...].reshape(suffix_all, width),
            jnp.concatenate([fresh_key, fill], axis=0).astype(bf16),
        ],
        axis=0,
    )
    own_values = jnp.concatenate(
        [
            suffix_values[...].reshape(suffix_all, width),
            jnp.concatenate([fresh_value, fill], axis=0).astype(bf16),
        ],
        axis=0,
    )
    lane = lax.broadcasted_iota(jnp.int32, (tokens, LANES), 1)
    peaks = [jnp.zeros((tokens, LANES), f32) for _ in range(pre_count)]
    sums = [jnp.zeros((tokens, LANES), f32) for _ in range(pre_count)]
    for k in range(KV_HEADS):
        span = slice(k * HD, (k + 1) * HD)
        heads = [query[:, h * HD : (h + 1) * HD] for h in range(k * group, (k + 1) * group)]
        plain = jnp.concatenate(heads, axis=0).astype(bf16)
        scaled = jnp.concatenate([head * key_scale[:, span] for head in heads], axis=0).astype(bf16)
        prefix_scores = dot_t(scaled, prefix_keys[:, span]) * (HD**-0.5)
        own_scores = jnp.where(allowed, dot_t(plain, own_keys[:, span]) * (HD**-0.5), masked_score)
        peak = jnp.max(jnp.maximum(prefix_scores, own_scores), axis=1, keepdims=True)
        prefix_weight = jnp.exp(prefix_scores - peak).astype(bf16)
        own_weight = jnp.where(allowed, jnp.exp(own_scores - peak), 0.0).astype(bf16)
        total = jnp.sum(prefix_weight.astype(f32) + own_weight.astype(f32), axis=1, keepdims=True)
        from_prefix = dot(prefix_weight, prefix_values[:, span])
        from_own = dot(own_weight, own_values[:, span])
        for g in range(group):
            h = k * group + g
            at, j = h // block_heads, h % block_heads
            part = slice(g * tokens, (g + 1) * tokens)
            value = from_prefix[part] * value_scale[:, span] + from_own[part]
            stage[at, :, j * HD : (j + 1) * HD] = value.astype(bf16)
            peaks[at] = jnp.where(lane == j, peak[part], peaks[at])
            sums[at] = jnp.where(lane == j, total[part], sums[at])
    for at in range(pre_count):
        packed = jnp.zeros((tokens, LANES), f32)
        for place, piece in enumerate(three_parts(peaks[at]) + three_parts(sums[at])):
            packed = packed + (pltpu.roll(piece, place * block_heads, 1) if place else piece)
        stage[at, :, block:] = packed.astype(bf16)
    for s in range(pre_count):
        outs[s][...] = stage[lax.rem(me + s, pre_count)]


def merge_kernel(parts, *rest):
    blocks, out = rest[:parts], rest[parts]
    block = out.shape[1]
    block_heads = block // HD
    peaks, sums = [], []
    for ref in blocks:
        packed = ref[:, block:].astype(f32)
        pieces = [
            pltpu.roll(packed, LANES - place * block_heads, 1) if place else packed
            for place in range(6)
        ]
        peaks.append(pieces[0] + pieces[1] + pieces[2])
        sums.append(pieces[3] + pieces[4] + pieces[5])
    lane = lax.broadcasted_iota(jnp.int32, peaks[0].shape, 1)
    real = lane < block_heads
    highest = functools.reduce(jnp.maximum, peaks)
    factors = [jnp.where(real, jnp.exp(jnp.where(real, peak - highest, 0.0)), 0.0) for peak in peaks]
    total = sum(factor * amount for factor, amount in zip(factors, sums))
    total = jnp.where(real, total, 1.0)
    factors = [factor / total for factor in factors]
    for j in range(block_heads):
        span = slice(j * HD, (j + 1) * HD)
        value = sum(
            ref[:, span].astype(f32) * factor[:, j : j + 1] for ref, factor in zip(blocks, factors)
        )
        out[:, span] = value.astype(bf16)


def project_kernel(row_count, pre_count, *rest):
    blocks, weight = rest[:row_count], rest[row_count]
    outs = rest[row_count + 1 : row_count + 1 + pre_count]
    stacked, product = rest[row_count + 1 + pre_count :]
    tokens = blocks[0].shape[0]
    amount = outs[0].shape[0]
    pre_at, row_at = lax.axis_index("pre"), lax.axis_index("row")
    for s, ref in enumerate(blocks):
        start = pl.multiple_of(lax.rem(row_at + row_count - s, row_count) * tokens, tokens)
        stacked[pl.ds(start, tokens), :] = ref[...].astype(f32)
    product[...] = dot(stacked[...].astype(bf16), weight[...])
    for s, out in enumerate(outs):
        start = pl.multiple_of(target_of(pre_at, s, pre_count) * amount, amount)
        out[...] = product[pl.ds(start, amount), :].astype(out.dtype)


def residual_kernel(parts, hidden, *rest):
    blocks, (out, sent) = rest[:parts], rest[parts:]
    amount, width = sent.shape
    value = sum(ref[...].astype(f32) for ref in blocks)
    value = hidden.reshape(amount, width)[...].astype(f32) + value
    sent[...] = value.astype(bf16)
    out.reshape(amount, width)[...] = value.astype(bf16)


def column_tile(columns):
    return next(size for size in (512, 256, 128) if columns % size == 0)


def split_columns(wide):
    unit = 512 if wide >= 1024 else LANES
    first = -(-(wide // 2) // unit) * unit
    return first, wide - first


def hand_out(row_count, product, columns, extra, keep, sent):
    rows = product.shape[0] // 2
    tokens = keep.shape[1]
    row_at = lax.axis_index("row")
    for j in range(row_count // 2):
        for at, out in ((row_at ^ (2 * j), keep), (row_at ^ (2 * j + 1), sent)):
            start = pl.multiple_of(at * tokens, tokens)
            own = pl.ds(start, tokens)
            out[j, :, :columns] = product[own, :columns].astype(out.dtype)
            out[j, :, columns : 2 * columns] = product[
                pl.ds(rows + start, tokens), :columns
            ].astype(out.dtype)
            if extra:
                out[j, :, 2 * columns :] = product[own, columns:].astype(out.dtype)


def multiply(left, weight, first, columns, product):
    depth, _, wide = weight.shape
    flat = weight.reshape(2 * depth, wide)
    tile = column_tile(columns)
    for start in range(0, columns, tile):
        product[:, start : start + tile] = dot(
            left, flat[:, first + start : first + start + tile]
        )


def placed_parts(value):
    lane = lax.broadcasted_iota(jnp.int32, (value.shape[0], LANES), 1)
    pieces = three_parts(value)
    return sum(jnp.where(lane == place, piece, 0.0) for place, piece in enumerate(pieces))


def feed_first_kernel(pre_count, row_count, columns, gain, *rest):
    blocks, weight = rest[:pre_count], rest[pre_count]
    keep, sent, spread, stacked, product = rest[pre_count + 1 :]
    amount, depth = blocks[0].shape
    rows = pre_count * amount
    pre_at = lax.axis_index("pre")
    for s, ref in enumerate(blocks):
        start = pl.multiple_of(source_of(pre_at, s, pre_count) * amount, amount)
        stacked[pl.ds(start, amount), :] = ref[...].astype(f32)
    value = stacked[...]
    squares = jnp.sum(value * value, axis=1, keepdims=True)
    normed = (value * gain[...].astype(f32).reshape(1, depth)).astype(bf16)
    source = lax.broadcasted_iota(jnp.int32, (HD, 2 * HD), 0)
    target = lax.broadcasted_iota(jnp.int32, (HD, 2 * HD), 1)
    pieces = jnp.concatenate(
        [normed[:, b * HD : (b + 1) * HD] for b in range(depth // HD)], axis=0
    )
    for half in range(2):
        selector = (target == 2 * source + half).astype(bf16)
        wider = dot(pieces, selector).astype(bf16)
        for b in range(depth // HD):
            spread[half * rows : (half + 1) * rows, 2 * b * HD : 2 * (b + 1) * HD] = wider[
                b * rows : (b + 1) * rows
            ]
    multiply(spread[...], weight, 0, columns, product)
    product[0:rows, columns:] = placed_parts(squares)
    hand_out(row_count, product, columns, True, keep, sent)


def feed_second_kernel(row_count, first, columns, spread, weight, keep, sent, product):
    multiply(spread[...], weight, first, columns, product)
    hand_out(row_count, product, columns, False, keep, sent)


def pair_kernel(extra, keep, received, *outs):
    for j, out in enumerate(outs):
        value = keep[j] + received[j].astype(f32)
        if extra:
            edge = value.shape[1] - LANES
            out[:, :edge] = value[:, :edge].astype(out.dtype)
            total = jnp.sum(value[:, edge:], axis=1, keepdims=True)
            out[:, edge:] = placed_parts(total).astype(out.dtype)
        else:
            out[...] = value.astype(out.dtype)


def scale_kernel(ids, table, out):
    tokens = out.shape[0]
    adapters = table.shape[0]
    row_of = lax.broadcasted_iota(jnp.int32, (tokens, adapters), 0) // STEPS
    column = lax.broadcasted_iota(jnp.int32, (tokens, adapters), 1)
    chosen = pick(row_of, [ids[r] for r in range(tokens // STEPS)])
    out[...] = dot((chosen == column).astype(bf16), table[...])


def activate_kernel(parts, first, scales, *rest):
    front, back, out = rest[:parts], rest[parts : 2 * parts], rest[2 * parts]
    tokens, wide = scales.shape
    flat = out.reshape(tokens, wide)
    squares = sum(ref[:, 2 * first :].astype(f32) for ref in front)
    squares = jnp.sum(squares, axis=1, keepdims=True)
    inverse = lax.rsqrt(squares / D + 1e-05)
    for blocks, start, columns in ((front, 0, first), (back, first, wide - first)):
        gate = sum(ref[:, :columns].astype(f32) for ref in blocks) * inverse
        up = sum(ref[:, columns : 2 * columns].astype(f32) for ref in blocks) * inverse
        value = gate / (1.0 + jnp.exp(-gate)) * up * scales[:, start : start + columns]
        flat[:, start : start + columns] = value.astype(bf16)


def shifted(parts, axis):
    count = lax.axis_size(axis)
    return [parts[0]] + [
        lax.ppermute(parts[s], axis, [(i, target_of(i, s, count)) for i in range(count)])
        for s in range(1, count)
    ]


def shape_of(dims, dtype=bf16):
    return jax.ShapeDtypeStruct(dims, dtype)


def params(mib):
    return pltpu.CompilerParams(vmem_limit_bytes=mib << 20)


def cost(micros):
    return pl.CostEstimate(flops=micros * 10**9, bytes_accessed=0, transcendentals=0)


def per_device(
    queries,
    prefix_keys,
    prefix_values,
    suffix_keys,
    suffix_values,
    new_keys,
    new_values,
    hidden,
    adapter_ids,
    suffix_lengths,
    kv_scales,
    ffn_scales,
    out_weight,
    norm_gain,
    gate_up,
):
    rows = queries.shape[0]
    tokens = rows * STEPS
    kv_width = prefix_keys.shape[1]
    pre_count = lax.axis_size("pre")
    row_count = lax.axis_size("row")
    block = HEADS * HD // pre_count
    amount = hidden.shape[0] * STEPS
    out_cols = out_weight.shape[1]
    depth, _, wide = gate_up.shape

    ffn_rows = pl.pallas_call(
        scale_kernel,
        in_specs=[SMEM, VMEM],
        out_specs=VMEM,
        out_shape=shape_of((tokens, wide), f32),
        compiler_params=params(4),
    )(adapter_ids, ffn_scales)

    suffix_local = suffix_keys.shape[1]
    mask = pl.pallas_call(
        functools.partial(mask_kernel, tokens, suffix_local),
        in_specs=[SMEM],
        out_specs=VMEM,
        out_shape=shape_of((tokens, LANES), jnp.int32),
        compiler_params=params(1),
        cost_estimate=cost(20),
    )(suffix_lengths)
    partials = pl.pallas_call(
        functools.partial(attend_kernel, pre_count),
        in_specs=[SMEM] + [VMEM] * 9,
        out_specs=[VMEM] * pre_count,
        out_shape=[shape_of((tokens, block + LANES))] * pre_count,
        scratch_shapes=[
            pltpu.VMEM((tokens, kv_width), f32),
            pltpu.VMEM((pre_count, tokens, block + LANES), bf16),
        ],
        compiler_params=params(8),
        cost_estimate=cost(20),
    )(
        adapter_ids,
        mask,
        queries,
        prefix_keys,
        prefix_values,
        suffix_keys,
        suffix_values,
        new_keys,
        new_values,
        kv_scales,
    )
    ring = [partials[0]] + [
        lax.ppermute(partials[s], "pre", [(i, (i + s) % pre_count) for i in range(pre_count)])
        for s in range(1, pre_count)
    ]
    mixed = pl.pallas_call(
        functools.partial(merge_kernel, pre_count),
        in_specs=[VMEM] * pre_count,
        out_specs=VMEM,
        out_shape=shape_of((tokens, block)),
        compiler_params=params(4),
        cost_estimate=cost(40),
    )(*ring)
    gathered = [mixed] + [
        lax.ppermute(mixed, "row", [(i, (i + s) % row_count) for i in range(row_count)])
        for s in range(1, row_count)
    ]
    products = pl.pallas_call(
        functools.partial(project_kernel, row_count, pre_count),
        in_specs=[VMEM] * (row_count + 1),
        out_specs=[VMEM] * pre_count,
        out_shape=[
            shape_of((amount, out_cols), bf16 if s else f32) for s in range(pre_count)
        ],
        scratch_shapes=[
            pltpu.VMEM((row_count * tokens, block), f32),
            pltpu.VMEM((row_count * tokens, out_cols), f32),
        ],
        compiler_params=params(8),
        cost_estimate=cost(40),
    )(*gathered, out_weight)
    residual, sent = pl.pallas_call(
        functools.partial(residual_kernel, pre_count),
        in_specs=[VMEM] * (pre_count + 1),
        out_specs=[VMEM] * 2,
        out_shape=[shape_of(hidden.shape), shape_of((amount, out_cols))],
        compiler_params=params(4),
        cost_estimate=cost(40),
    )(hidden, *shifted(products, "pre"))
    stacked = shifted([sent] * pre_count, "pre")
    total_rows = pre_count * amount
    half = row_count // 2
    first, second = split_columns(wide)
    sizes = (2 * first + LANES, 2 * second)
    *front, spread = pl.pallas_call(
        functools.partial(feed_first_kernel, pre_count, row_count, first),
        in_specs=[VMEM] * (pre_count + 2),
        out_specs=[VMEM] * 3,
        out_shape=[
            shape_of((half, tokens, sizes[0]), f32),
            shape_of((half, tokens, sizes[0])),
            shape_of((2 * total_rows, 2 * depth)),
        ],
        scratch_shapes=[
            pltpu.VMEM((total_rows, depth), f32),
            pltpu.VMEM((2 * total_rows, first + LANES), f32),
        ],
        compiler_params=params(8),
        cost_estimate=cost(16),
    )(norm_gain, *stacked, gate_up)
    back = pl.pallas_call(
        functools.partial(feed_second_kernel, row_count, first, second),
        in_specs=[VMEM] * 2,
        out_specs=[VMEM] * 2,
        out_shape=[
            shape_of((half, tokens, sizes[1]), f32),
            shape_of((half, tokens, sizes[1])),
        ],
        scratch_shapes=[pltpu.VMEM((2 * total_rows, second), f32)],
        compiler_params=pltpu.CompilerParams(
            vmem_limit_bytes=(8 << 20) + 2 * depth * (total_rows + 1)
        ),
        cost_estimate=cost(16),
    )(spread, gate_up)
    finals = []
    for extra, size, (keep, sent) in ((True, sizes[0], front), (False, sizes[1], back)):
        received = lax.ppermute(sent, "row", [(i, i ^ 1) for i in range(row_count)])
        sums = pl.pallas_call(
            functools.partial(pair_kernel, extra),
            in_specs=[VMEM] * 2,
            out_specs=[VMEM] * half,
            out_shape=[shape_of((tokens, size), bf16 if j else f32) for j in range(half)],
            compiler_params=params(4),
        )(keep, received)
        finals.append(sums[0])
        finals += [
            lax.ppermute(sums[j], "row", [(i, i ^ (2 * j)) for i in range(row_count)])
            for j in range(1, half)
        ]
    activation = pl.pallas_call(
        functools.partial(activate_kernel, half, first),
        in_specs=[VMEM] * (2 * half + 1),
        out_specs=VMEM,
        out_shape=shape_of((rows, STEPS, wide)),
        compiler_params=params(4),
    )(ffn_rows, *finals)
    return (residual, activation)


def solution(mesh):
    placed = (
        P(("grp", "row"), None, None),
        P(("grp", "pre"), None),
        P(("grp", "pre"), None),
        P(("grp", "row"), "pre", None),
        P(("grp", "row"), "pre", None),
        P(("grp", "row"), None, None),
        P(("grp", "row"), None, None),
        P(("grp", "pre"), None, "row"),
        P(("grp", "row")),
        P(("grp", "row")),
        P(),
        P(None, "pre"),
        P("pre", "row"),
        P("row"),
        P("row", None, "pre"),
    )
    return jax.shard_map(
        per_device,
        mesh=mesh,
        in_specs=placed,
        out_specs=(P(("grp", "pre"), None, "row"), P(("grp", "row"), None, "pre")),
        check_vma=False,
    )
```
